32 devices in a mesh: leaf: 8 (over z, core), front: 4 (over y, x).
Axes of the slice: x: 2, y: 2, z: 4, core: 2. Of those that a mesh axis runs over, the one named last changes fastest.
Arguments:
- parent_border_inverse: float32 [8, 1536, 1536], P('leaf', 'front')
- parent_border_rows: float32 [8, 1536, 768], P('leaf', 'front'), may hold values from -0.09 to 0.09
- parent_diagonal_inverse: float32 [8, 768, 768], P('leaf', 'front')
- child_border_rows: float32 [16, 1024, 512], P('leaf', 'front'), may hold values from -0.13 to 0.13
- child_factor_inverse: float32 [16, 512, 512], P('leaf', 'front')
- child_index: int32 [16, 1024], replicated, may hold values from 0 to 2303, as said below
- child_parent: int32 [16], replicated, may hold values from 0 to 7, as said below
Outputs:
- parent_variance: float32 [8, 768], P('leaf')
- child_variance: float32 [16, 512], P('leaf')
The draws below stay inside these ranges and needn't reach their ends.
Inputs may be any that keep to these rules, and one draw needn't show every extreme that they name: `child_index`: each row holds 1024 distinct positions in increasing order, the first 0 and the last 2303. `child_parent`: child c's parent is c // 2 or c // 2 with its lowest bit flipped, and every parent has exactly two children.
All inputs are finite; a program needn't handle non-finite values.
Results may differ from the reference program's by a relative error of at most 0.0003.
Values sent between devices are 32-bit elements; how exact they have to be, the bound alone decides.
No kernel may reach another device: no remote copies, remote signals or barrier semaphores. Data moves between devices by JAX's collectives and lax.ppermute only.
A program may use at most 64 MiB of HBM per device.

```python
import math
import jax
import jax.numpy as jnp
from jax import lax

ELIMINATED_SIZE = 768
BORDER_SIZE = 1536
CHILD_ELIMINATED = 512
CHILD_BORDER = 1024
PARENT_FRONTS = 8
CHILD_FRONTS = 16


def inverse_lower(key, count, size, spread):
    first, second = jax.random.split(key)
    noise = jax.random.normal(first, (count, size, size), jnp.float32) * spread
    rowpos = jnp.arange(size)[:, None]
    colpos = jnp.arange(size)[None, :]
    strict = (rowpos > colpos).astype(jnp.float32)
    eye_mask = (rowpos == colpos).astype(jnp.float32)
    diagonal = jnp.exp(jax.random.uniform(second, (count, size), jnp.float32, math.log(0.5), math.log(1.5)))
    return noise * strict[None] + eye_mask[None] * diagonal[:, :, None]


def draw_parent_border_inverse(key, part):
    first, second = jax.random.split(key, 2)
    noise = jax.random.normal(first, (PARENT_FRONTS, BORDER_SIZE, BORDER_SIZE), jnp.float32)
    symmetric = (noise + jnp.transpose(noise, (0, 2, 1))) * (0.6 / math.sqrt(BORDER_SIZE))
    diagonal = jnp.exp(jax.random.uniform(second, (PARENT_FRONTS, BORDER_SIZE), jnp.float32, math.log(2.5), math.log(7.0)))
    eye_mask = (jnp.arange(BORDER_SIZE)[:, None] == jnp.arange(BORDER_SIZE)[None, :]).astype(jnp.float32)
    result = symmetric + eye_mask[None] * diagonal[:, :, None]
    return result


def draw_parent_diagonal_inverse(key, part):
    return inverse_lower(key, PARENT_FRONTS, ELIMINATED_SIZE, 0.02)


def draw_child_factor_inverse(key, part):
    return inverse_lower(key, CHILD_FRONTS, CHILD_ELIMINATED, 0.025)


def draw_child_index(key, part):
    random_keys = jax.random.split(jax.random.fold_in(key, 11), CHILD_FRONTS)
    front_orders = jax.vmap(lambda single_front: jax.random.permutation(single_front, ELIMINATED_SIZE + BORDER_SIZE - 2))(random_keys)
    middle = front_orders[:, :CHILD_BORDER - 2].astype(jnp.int32) + 1
    first_col = jnp.zeros((CHILD_FRONTS, 1), jnp.int32)
    final_column = jnp.full((CHILD_FRONTS, 1), ELIMINATED_SIZE + BORDER_SIZE - 1, jnp.int32)
    return jnp.sort(jnp.concatenate([first_col, middle, final_column], axis=1), axis=1).astype(jnp.int32)


def draw_child_parent(key, part):
    groups = CHILD_FRONTS // 4
    random_keys = jax.random.split(jax.random.fold_in(key, 23), groups)
    perms = jax.vmap(lambda single_front: jax.random.permutation(single_front, 4))(random_keys).astype(jnp.int32)
    group = jnp.arange(groups, dtype=jnp.int32)[:, None]
    targets = (4 * group + perms).reshape(-1)
    values = (2 * group + jnp.array([0, 0, 1, 1], jnp.int32)[None, :]).reshape(-1)
    return jnp.zeros((CHILD_FRONTS,), jnp.int32).at[targets].set(values).astype(jnp.int32)


def block_levels(stream_key, shape, cuts, least, top_value):
    def one(axis_at, shards_of):
        steps = jax.random.uniform(jax.random.fold_in(jax.random.fold_in(stream_key, 6), axis_at), (shards_of,), jnp.float32, least / len(cuts), top_value / len(cuts))
        return jnp.repeat(jnp.exp(steps), shape[axis_at] // shards_of).reshape((-1,) + (1,) * (len(shape) - axis_at - 1))

    loudness = one(*cuts[0])
    for cut in cuts[1:]:
        loudness = loudness * one(*cut)
    return loudness


def normal_values(stream_key, extent, scale, most, cuts=(), kind=jnp.bfloat16):
    values = jax.random.normal(stream_key, extent, jnp.float32) * scale
    if len(cuts) > 0:
        values = block_levels(stream_key, extent, cuts, -0.22, 0.18) * values
    return jnp.clip(values, min=-most, max=most).astype(kind)


def setup_inputs(seed: int = 0) -> dict:
    keys = jax.random.split(jax.random.key(seed), 8)
    parent_border_inverse = draw_parent_border_inverse(jax.random.fold_in(keys[7], 71), 0)
    parent_border_rows = normal_values(keys[1], (PARENT_FRONTS, BORDER_SIZE, ELIMINATED_SIZE), 0.015, 0.09, ((0, 8), (1, 4)), jnp.float32)
    parent_diagonal_inverse = draw_parent_diagonal_inverse(jax.random.fold_in(keys[7], 71), 0)
    child_border_rows = normal_values(keys[3], (CHILD_FRONTS, CHILD_BORDER, CHILD_ELIMINATED), 0.022, 0.13, ((0, 8), (1, 4)), jnp.float32)
    child_factor_inverse = draw_child_factor_inverse(jax.random.fold_in(keys[7], 71), 0)
    child_index = draw_child_index(jax.random.fold_in(keys[7], 71), 0)
    child_parent = draw_child_parent(jax.random.fold_in(keys[7], 71), 0)
    return {"parent_border_inverse": parent_border_inverse, "parent_border_rows": parent_border_rows, "parent_diagonal_inverse": parent_diagonal_inverse, "child_border_rows": child_border_rows, "child_factor_inverse": child_factor_inverse, "child_index": child_index, "child_parent": child_parent}


def matrix_product(left, right):
    return jnp.dot(left, right, precision=lax.Precision.HIGHEST, preferred_element_type=jnp.float32)


def children_of(child_parent, owner):
    partner = jnp.bitwise_xor(owner, 1)
    pool_ids = jnp.stack([2 * owner, 2 * owner + 1, 2 * partner, 2 * partner + 1]).astype(jnp.int32)
    member = (jnp.take(child_parent, pool_ids) == owner).astype(jnp.int32)
    first = jnp.argmax(member).astype(jnp.int32)
    second = (3 - jnp.argmax(member[::-1])).astype(jnp.int32)
    slots = jnp.stack([first, second]).astype(jnp.int32)
    return slots, jnp.take(pool_ids, slots).astype(jnp.int32)


def paired_fronts(border_inverse, border_factor, eliminated_inverse, child_factors, child_inverses, index_list):
    weight_rows = matrix_product(border_factor, eliminated_inverse)
    border_product = matrix_product(border_inverse, weight_rows)
    parent_marginal = jnp.sum(eliminated_inverse * eliminated_inverse, axis=0) + jnp.sum(weight_rows * border_product, axis=0)
    quadratic_terms = []
    for child_front in range(2):
        child_weight = matrix_product(child_factors[child_front], child_inverses[child_front])
        placed_rows = jnp.zeros((ELIMINATED_SIZE + BORDER_SIZE, CHILD_ELIMINATED), jnp.float32).at[index_list[child_front]].set(child_weight)
        upper_block = placed_rows[:ELIMINATED_SIZE]
        lower_block = placed_rows[ELIMINATED_SIZE:]
        reduced = lower_block - matrix_product(weight_rows, upper_block)
        kid_image = matrix_product(border_inverse, reduced)
        lifted_rows = matrix_product(eliminated_inverse, upper_block)
        quadratic_terms.append(jnp.sum(lifted_rows * lifted_rows, axis=0) + jnp.sum(reduced * kid_image, axis=0))
    return parent_marginal, jnp.stack(quadratic_terms)


def reference(parent_border_inverse, parent_border_rows, parent_diagonal_inverse, child_border_rows, child_factor_inverse, child_index, child_parent):
    counter = jnp.arange(PARENT_FRONTS, dtype=jnp.int32)

    def one_parent(position):
        slots, child_fronts = children_of(child_parent, position)
        parent_marginal, quadratic_terms = paired_fronts(parent_border_inverse[position], parent_border_rows[position],
                                       parent_diagonal_inverse[position], child_border_rows[child_fronts],
                                       child_factor_inverse[child_fronts], child_index[child_fronts])
        return parent_marginal, quadratic_terms, child_fronts

    parent_marginal, quadratic_terms, child_fronts = lax.map(one_parent, counter)
    own_term = jnp.sum(child_factor_inverse * child_factor_inverse, axis=1)
    placed_quadratics = jnp.zeros((CHILD_FRONTS, CHILD_ELIMINATED), jnp.float32).at[child_fronts.reshape(-1)].set(quadratic_terms.reshape(-1, CHILD_ELIMINATED))
    return parent_marginal, own_term + placed_quadratics
```

```python
import functools

import jax
import jax.numpy as jnp
from jax import lax
from jax.experimental import pallas as pl
from jax.experimental.pallas import tpu as pltpu
from jax.sharding import PartitionSpec as P

VMEM = pl.BlockSpec(memory_space=pltpu.VMEM)
SMEM = pl.BlockSpec(memory_space=pltpu.SMEM)
LIMIT = 56 * 1024 * 1024
COLS = 256


def shape_of(shape, dtype=jnp.float32):
    return jax.ShapeDtypeStruct(shape, dtype)


def over_core(value):
    pairs = [(leaf, leaf ^ 1) for leaf in range(lax.axis_size("leaf"))]
    return lax.ppermute(value, "leaf", pairs)


def over_front(value, mask):
    pairs = [(front, front ^ mask) for front in range(lax.axis_size("front"))]
    return lax.ppermute(value, "front", pairs)


def cross(value):
    fronts = lax.axis_size("front")
    pairs = []
    for leaf in range(lax.axis_size("leaf")):
        for front in range(fronts):
            flip = (leaf ^ front) & 1
            pairs.append((leaf * fronts + front, (leaf ^ flip) * fronts + (front ^ flip)))
    return lax.ppermute(value, ("leaf", "front"), pairs)


def after(value, *others):
    return lax.optimization_barrier((value, *others))[0]


def kids_of(parent_ref, owner):
    partner = owner ^ 1
    pool = [2 * owner, 2 * owner + 1, 2 * partner, 2 * partner + 1]
    member = [parent_ref[kid] == owner for kid in pool]
    first = jnp.where(member[0], 0, jnp.where(member[1], 1, 2))
    second = jnp.where(member[3], 3, jnp.where(member[2], 2, 1))
    ids = [2 * jnp.where(slot < 2, owner, partner) + (slot & 1) for slot in (first, second)]
    return (first, second), ids


def place_of():
    front, leaf = lax.axis_index("front"), lax.axis_index("leaf")
    owner = (leaf & -2) | (front & 1)
    block = (front & -2) | (leaf & 1)
    return owner, block


def halves(value):
    high = value.astype(jnp.bfloat16)
    return high, (value - high.astype(jnp.float32)).astype(jnp.bfloat16)


def dot(left, right):
    return jnp.dot(left, right, preferred_element_type=jnp.float32)


def product(left, right):
    (left_high, left_low), (right_high, right_low) = left, right
    return dot(left_high, right_high) + (dot(left_high, right_low) + dot(left_low, right_high))


def column_sum(value):
    return jnp.sum(value, axis=0, keepdims=True)


def select_kernel(parent_ref, *refs):
    slots, _ = kids_of(parent_ref, lax.axis_index("leaf"))
    half = len(refs) // 3
    for own, other, out in zip(refs[:half], refs[half : 2 * half], refs[2 * half :]):
        for place, slot in enumerate(slots):
            for source in range(4):

                @pl.when(slot == source)
                def _(own=own, other=other, out=out, place=place, source=source):
                    out[place] = (own if source < 2 else other)[source % 2]


def kid_kernel(pieces, *refs):
    parent_ref, index_ref, border, factor = refs[:4]
    diagonal = refs[4 : 4 + pieces]
    kid_inverse = refs[4 + pieces : 4 + 2 * pieces]
    kid_rows = refs[4 + 2 * pieces : 4 + 3 * pieces]
    reduced, border_lower, weights, lift_high, lift_low, diag_high, diag_low, parent_sum, kid_sum = refs[
        4 + 3 * pieces : 13 + 3 * pieces
    ]
    placed, kid_weight, inv_high, inv_low, border_high, border_low = refs[13 + 3 * pieces :]
    owner, block = place_of()
    _, ids = kids_of(parent_ref, owner)
    size = diag_high.shape[0]
    own_rows, own_border = diagonal[0].shape[0], factor.shape[0]
    kid_size = kid_inverse[0].shape[2]
    kid_block, inv_block = kid_rows[0].shape[1], kid_inverse[0].shape[1]
    columns = kid_size // COLS

    parent_sum[...] = column_sum(diagonal[0][...] * diagonal[0][...])
    for mask in range(pieces):
        start = pl.multiple_of((block ^ mask) * own_rows, 16)
        high, low = halves(diagonal[mask][...])
        diag_high[pl.ds(start, own_rows), :] = high
        diag_low[pl.ds(start, own_rows), :] = low
    high, low = halves(border[...])
    border_high[...] = high
    border_low[...] = low

    for kid in range(2):
        kid_sum[kid : kid + 1] = column_sum(kid_inverse[0][kid] * kid_inverse[0][kid])
        for mask in range(pieces):
            start = pl.multiple_of((block ^ mask) * inv_block, 16)
            high, low = halves(kid_inverse[mask][kid])
            inv_high[pl.ds(start, inv_block), :] = high
            inv_low[pl.ds(start, inv_block), :] = low

        def clear(step, carry, kid=kid):
            placed[kid, pl.ds(pl.multiple_of(step * 256, 256), 256), :] = jnp.zeros((256, kid_size), jnp.float32)
            return carry

        lax.fori_loop(0, placed.shape[1] // 256, clear, 0)
        for mask in range(pieces):
            kid_weight[...] = product(halves(kid_rows[mask][kid]), (inv_high[...], inv_low[...]))
            start = (block ^ mask) * kid_block

            def put(row, carry, kid=kid, start=start):
                target = index_ref[ids[kid], start + row]
                placed[kid, pl.ds(target, 1), :] = kid_weight[pl.ds(row, 1), :]
                return carry

            lax.fori_loop(0, kid_block, put, 0, unroll=8)

    factor_halves = halves(factor[...])
    lower_start = pl.multiple_of(size + block * own_border, 8)
    own_start = pl.multiple_of(block * own_rows, 8)
    for kid in range(2):
        for column in range(columns):
            span = slice(column * COLS, (column + 1) * COLS)
            upper = halves(placed[kid, :size, span])
            lifted = product((diag_high[...], diag_low[...]), upper)
            lifted_halves = halves(lifted)
            lift_high[kid, :, span], lift_low[kid, :, span] = lifted_halves
            weights_part = product(factor_halves, lifted_halves)
            reduced[kid, :, span] = placed[kid, pl.ds(lower_start, own_border), span] - weights_part
            lower = halves(placed[kid, size:, span])
            border_lower[kid, :, span] = product((border_high[...], border_low[...]), lower)
    for kid in range(2):
        own = lift_high[kid, pl.ds(pl.multiple_of(own_start, 16), own_rows), :].astype(jnp.float32) + lift_low[
            kid, pl.ds(pl.multiple_of(own_start, 16), own_rows), :
        ].astype(jnp.float32)
        kid_sum[kid : kid + 1] += column_sum(own * own)
    for column in range(size // COLS):
        span = slice(column * COLS, (column + 1) * COLS)
        weights[:, span] = product(factor_halves, (diag_high[:, span], diag_low[:, span]))


def image_kernel(pieces, *refs):
    factor = refs[:pieces]
    border, reduced, border_lower, weights, lift_high, lift_low, diag_high, diag_low, parent_sum, kid_sum, out = refs[
        pieces : pieces + 11
    ]
    factor_high, factor_low, fold_high, fold_low = refs[pieces + 11 :]
    _, block = place_of()
    own_border, size = factor[0].shape
    kid_size = reduced.shape[2]
    for mask in range(pieces):
        start = pl.multiple_of((block ^ mask) * own_border, 16)
        high, low = halves(factor[mask][...])
        factor_high[pl.ds(start, own_border), :] = high
        factor_low[pl.ds(start, own_border), :] = low
    border_halves = halves(border[...])
    for column in range(size // COLS):
        span = slice(column * COLS, (column + 1) * COLS)
        fold_high[:, span], fold_low[:, span] = halves(
            product(border_halves, (factor_high[:, span], factor_low[:, span]))
        )
    fold = fold_high[...], fold_low[...]
    for column in range(size // COLS):
        span = slice(column * COLS, (column + 1) * COLS)
        image = product(fold, (diag_high[:, span], diag_low[:, span]))
        out[:, span] = parent_sum[:, span] + column_sum(weights[:, span] * image)
    for kid in range(2):
        for column in range(kid_size // COLS):
            span = slice(column * COLS, (column + 1) * COLS)
            image = border_lower[kid, :, span] - product(fold, (lift_high[kid, :, span], lift_low[kid, :, span]))
            target = size + kid * kid_size + column * COLS
            out[:, target : target + COLS] = kid_sum[kid : kid + 1, span] + column_sum(reduced[kid, :, span] * image)


def finish_kernel(parent_ref, own, other, parent_out, kid_out):
    front, leaf = lax.axis_index("front"), lax.axis_index("leaf")
    size, kid_size = parent_out.shape[1], kid_out.shape[1]
    mine = (front & 1) == (leaf & 1)
    parent_out[...] = jnp.where(mine, own[:, :size], other[:, :size])
    owner, _ = place_of()
    for parent, sums in ((owner, own), (owner ^ 1, other)):
        _, ids = kids_of(parent_ref, parent)
        for place in range(2):
            for kid in range(2):

                @pl.when(ids[place] == 2 * leaf + kid)
                def _(sums=sums, place=place, kid=kid):
                    start = size + place * kid_size
                    kid_out[kid : kid + 1] = sums[:, start : start + kid_size]


def call(kernel, out_shape, in_specs, scratch=(), flops=0, moved=0):
    specs = jax.tree.map(lambda _: VMEM, out_shape)
    return pl.pallas_call(
        kernel,
        out_shape=out_shape,
        in_specs=in_specs,
        out_specs=specs,
        scratch_shapes=scratch,
        compiler_params=pltpu.CompilerParams(vmem_limit_bytes=LIMIT),
        cost_estimate=pl.CostEstimate(flops=flops, bytes_accessed=moved, transcendentals=0),
    )


def shards(border, factor, diagonal, kid_rows, kid_inverse, child_index, child_parent):
    border, factor, diagonal = border[0], factor[0], diagonal[0]
    pieces = lax.axis_size("front")
    masks = [mask for mask in range(pieces) if mask % 2 == 0]
    size, kid_size, border_size = diagonal.shape[1], kid_rows.shape[2], border.shape[1]
    own_border = border.shape[0]
    kid_border = kid_rows.shape[1] * pieces

    def spread(value):
        parts = {0: value}
        bit = 2
        while bit < pieces:
            for mask in [mask for mask in masks if mask < bit]:
                parts[mask | bit] = over_front(parts[mask], bit)
            bit *= 2
        for mask in masks:
            parts[mask | 1] = over_core(parts[mask])
        return [parts[mask] for mask in range(pieces)]

    kid_bytes = kid_rows.size * 4 + kid_inverse.size * 4
    own_inverse, own_kids = call(
        select_kernel,
        (shape_of(kid_inverse.shape), shape_of(kid_rows.shape)),
        [SMEM] + [VMEM] * 4,
        moved=3 * kid_bytes,
    )(child_parent, kid_inverse, kid_rows, over_core(kid_inverse), over_core(kid_rows))

    own_diagonal = cross(diagonal)
    own_inverse = cross(own_inverse)
    own_kids = cross(own_kids)
    own_border_rows = cross(after(border, own_inverse))
    own_factor = cross(after(factor, own_kids))
    diagonal_parts = spread(own_diagonal)
    inverse_parts = spread(own_inverse)
    kid_parts = spread(own_kids)
    factor_parts = spread(own_factor)

    kid_flops = 6 * kid_size * (kid_border * kid_size + size * size + own_border * (size + border_size)) * 2
    half = jnp.bfloat16
    state = call(
        functools.partial(kid_kernel, pieces),
        (
            shape_of((2, own_border, kid_size)),
            shape_of((2, own_border, kid_size)),
            shape_of((own_border, size)),
            shape_of((2, size, kid_size), half),
            shape_of((2, size, kid_size), half),
            shape_of((size, size), half),
            shape_of((size, size), half),
            shape_of((1, size)),
            shape_of((2, kid_size)),
        ),
        [SMEM, SMEM] + [VMEM] * (2 + 3 * pieces),
        [
            pltpu.VMEM((2, size + border_size, kid_size), jnp.float32),
            pltpu.VMEM(kid_rows.shape[1:], jnp.float32),
            pltpu.VMEM((kid_size, kid_size), half),
            pltpu.VMEM((kid_size, kid_size), half),
            pltpu.VMEM(border.shape, half),
            pltpu.VMEM(border.shape, half),
        ],
        flops=kid_flops,
        moved=20_000_000,
    )(child_parent, child_index, own_border_rows, own_factor, *diagonal_parts, *inverse_parts, *kid_parts)

    total = call(
        functools.partial(image_kernel, pieces),
        shape_of((1, size + 2 * kid_size)),
        [VMEM] * (pieces + 10),
        [
            pltpu.VMEM((border_size, size), half),
            pltpu.VMEM((border_size, size), half),
            pltpu.VMEM((own_border, size), half),
            pltpu.VMEM((own_border, size), half),
        ],
        flops=6 * own_border * size * (border_size + size + 2 * kid_size),
        moved=15_000_000,
    )(*factor_parts, own_border_rows, *state)

    total = total + over_core(total)
    bit = 2
    while bit < pieces:
        total = total + over_front(total, bit)
        bit *= 2
    other = over_front(total, 1)
    return call(
        finish_kernel,
        (shape_of((1, size)), shape_of((2, kid_size))),
        [SMEM, VMEM, VMEM],
    )(child_parent, total, other)


def solution(mesh):
    whole = P("leaf", "front", None)
    return jax.shard_map(
        shards,
        mesh=mesh,
        in_specs=(whole,) * 5 + (P(), P()),
        out_specs=(P("leaf", None), P("leaf", None)),
        check_vma=False,
    )
```

```python
import functools

import jax
import jax.numpy as jnp
from jax import lax
from jax.experimental import pallas as pl
from jax.experimental.pallas import tpu as pltpu
from jax.sharding import PartitionSpec as P

MIB = 1024 * 1024
COLS = 256
LANES = 128
ROWS = 8


def shape_of(shape, dtype=jnp.float32):
    return jax.ShapeDtypeStruct(shape, dtype)


def exchange(value, leaf_mask, front_mask):
    fronts = lax.axis_size("front")
    pairs = [
        (leaf * fronts + front, (leaf ^ leaf_mask) * fronts + (front ^ front_mask))
        for leaf in range(lax.axis_size("leaf"))
        for front in range(fronts)
    ]
    return lax.ppermute(value, ("leaf", "front"), pairs)


def cross(value):
    fronts = lax.axis_size("front")
    pairs = []
    for leaf in range(lax.axis_size("leaf")):
        for front in range(fronts):
            flip = (leaf ^ front) & 1
            pairs.append((leaf * fronts + front, (leaf ^ flip) * fronts + (front ^ flip)))
    return lax.ppermute(value, ("leaf", "front"), pairs)


def after(value, *others):
    return lax.optimization_barrier((value, *others))[0]


def kids_of(parent_ref, owner):
    partner = owner ^ 1
    pool = [2 * owner, 2 * owner + 1, 2 * partner, 2 * partner + 1]
    member = [parent_ref[kid] == owner for kid in pool]
    first = jnp.where(member[0], 0, jnp.where(member[1], 1, 2))
    second = jnp.where(member[3], 3, jnp.where(member[2], 2, 1))
    ids = [2 * jnp.where(slot < 2, owner, partner) + (slot & 1) for slot in (first, second)]
    return (first, second), ids


def place_of():
    front, leaf = lax.axis_index("front"), lax.axis_index("leaf")
    owner = (leaf & -2) | (front & 1)
    block = (front & -2) | (leaf & 1)
    return owner, block


def rounded(value):
    return value.astype(jnp.bfloat16)


def halves(value):
    high = rounded(value)
    return high, rounded(value - high.astype(jnp.float32))


def dot(left, right):
    return jnp.dot(left, right, preferred_element_type=jnp.float32)


def product(left, right):
    (left_high, left_low), (right_high, right_low) = left, right
    return dot(left_high, right_high) + (dot(left_high, right_low) + dot(left_low, right_high))


def column_sum(value):
    return jnp.sum(value, axis=0, keepdims=True)


def spans(width):
    return [slice(start, start + COLS) for start in range(0, width, COLS)]


def select_kernel(parent_ref, *refs):
    slots, _ = kids_of(parent_ref, lax.axis_index("leaf"))
    half = len(refs) // 3
    for own, other, out in zip(refs[:half], refs[half : 2 * half], refs[2 * half :]):
        for place, slot in enumerate(slots):
            for source in range(4):

                @pl.when(slot == source)
                def _(own=own, other=other, out=out, place=place, source=source):
                    out[place] = (own if source < 2 else other)[source % 2]


def tiles_of(ref, start, rows, column, lanes):
    return jnp.concatenate([ref[pl.ds(start + (row * lanes + column) * ROWS, ROWS), :] for row in range(rows)], axis=0)


def kid_kernel(pieces, parent_ref, index_ref, factor, *refs):
    diagonal, kid_inverse, kid_rows = refs[:pieces], refs[pieces : 2 * pieces], refs[2 * pieces : 3 * pieces]
    reduced, lower_high, weights, lift_high, diag_high, diag_low, parent_sum, kid_sum = refs[
        3 * pieces : 3 * pieces + 8
    ]
    placed, kid_tiles, inv_high, inv_low, up_high, up_low, lifted = refs[3 * pieces + 8 :]
    owner, block = place_of()
    _, ids = kids_of(parent_ref, owner)
    size, border_size = diag_high.shape[0], lower_high.shape[1]
    own_rows, own_border = diagonal[0].shape[0], factor.shape[0]
    kid_size = kid_inverse[0].shape[2]
    kid_block, inv_block = kid_rows[0].shape[1], kid_inverse[0].shape[1]
    lanes = kid_size // LANES
    batch = 8 * ROWS

    parent_sum[...] = column_sum(diagonal[0][...] * diagonal[0][...])
    for mask in range(pieces):
        start = pl.multiple_of((block ^ mask) * own_rows, 16)
        high, low = halves(diagonal[mask][...])
        diag_high[pl.ds(start, own_rows), :] = high
        diag_low[pl.ds(start, own_rows), :] = low
    factor_halves = halves(factor[...])
    for span in spans(size):
        weights[:, span] = product(factor_halves, (diag_high[:, span], diag_low[:, span]))

    for kid in range(2):
        own_sum = column_sum(kid_inverse[0][kid] * kid_inverse[0][kid])
        for mask in range(pieces):
            start = pl.multiple_of((block ^ mask) * inv_block, 16)
            high, low = halves(kid_inverse[mask][kid])
            inv_high[pl.ds(start, inv_block), :] = high
            inv_low[pl.ds(start, inv_block), :] = low

        def clear(step, carry):
            placed[pl.ds(pl.multiple_of(step * 512, 512), 512), :] = jnp.zeros((512, LANES), jnp.float32)
            return carry

        lax.fori_loop(0, placed.shape[0] // 512, clear, 0)
        for mask in range(pieces):
            kid_weight = product(halves(kid_rows[mask][kid]), (inv_high[...], inv_low[...]))
            for row in range(kid_block // ROWS):
                for column in range(lanes):
                    kid_tiles[pl.ds((row * lanes + column) * ROWS, ROWS), :] = kid_weight[
                        row * ROWS : (row + 1) * ROWS, column * LANES : (column + 1) * LANES
                    ]
            start = (block ^ mask) * kid_block

            def put(step, carry, kid=kid, start=start):
                for row in range(ROWS):
                    target = index_ref[ids[kid], start + step * ROWS + row]
                    place = (target >> 3) * (lanes * ROWS) + (target & 7)
                    placed[pl.ds(place, lanes, stride=ROWS), :] = kid_tiles[
                        pl.ds(step * (lanes * ROWS) + row, lanes, stride=ROWS), :
                    ]
                return carry

            lax.fori_loop(0, kid_block // ROWS, put, 0, unroll=2)

        def upper(step, carry):
            start = pl.multiple_of(step * (batch * lanes), batch * lanes)
            for column in range(lanes):
                high, low = halves(tiles_of(placed, start, 8, column, lanes))
                target = pl.ds(pl.multiple_of(step * batch, batch), batch)
                up_high[target, column * LANES : (column + 1) * LANES] = high
                up_low[target, column * LANES : (column + 1) * LANES] = low
            return carry

        lax.fori_loop(0, size // batch, upper, 0)

        def lower(step, carry, kid=kid):
            start = pl.multiple_of(step * (batch * lanes) + size * lanes, batch * lanes)
            for column in range(lanes):
                target = pl.ds(pl.multiple_of(step * batch, batch), batch)
                lower_high[kid, target, column * LANES : (column + 1) * LANES] = rounded(
                    tiles_of(placed, start, 8, column, lanes)
                )
            return carry

        lax.fori_loop(0, border_size // batch, lower, 0)

        own_start = pl.multiple_of((size + block * own_border) * lanes, ROWS)
        for span in spans(kid_size):
            lifted[...] = product((diag_high[...], diag_low[...]), (up_high[:, span], up_low[:, span]))
            lift_high[kid, :, span] = rounded(lifted[...])
            own = lifted[pl.ds(pl.multiple_of(block * own_rows, 16), own_rows), :]
            kid_sum[kid : kid + 1, span] = own_sum[:, span] + column_sum(own * own)
            image = dot(factor_halves[0], lift_high[kid, :, span])
            for half in range(COLS // LANES):
                column = span.start // LANES + half
                own_lower = tiles_of(placed, own_start, own_border // ROWS, column, lanes)
                reduced[kid, :, column * LANES : (column + 1) * LANES] = (
                    own_lower - image[:, half * LANES : (half + 1) * LANES]
                )


def border_kernel(border, lower_high, border_high, border_lower):
    border_high[...] = rounded(border[...])
    for kid in range(2):
        for span in spans(lower_high.shape[2]):
            border_lower[kid, :, span] = dot(border_high[...], lower_high[kid, :, span])


def image_kernel(pieces, *refs):
    factor = refs[:pieces]
    border_high, border_lower, reduced, weights, lift_high, diag_high, diag_low, parent_sum, kid_sum, out = refs[
        pieces : pieces + 10
    ]
    factor_high, fold_high, fold_low = refs[pieces + 10 :]
    _, block = place_of()
    own_border, size = factor[0].shape
    kid_size = reduced.shape[2]
    for mask in range(pieces):
        start = pl.multiple_of((block ^ mask) * own_border, 16)
        factor_high[pl.ds(start, own_border), :] = rounded(factor[mask][...])
    for span in spans(size):
        fold_high[:, span], fold_low[:, span] = halves(dot(border_high[...], factor_high[:, span]))
    fold = fold_high[...], fold_low[...]
    for span in spans(size):
        image = product(fold, (diag_high[:, span], diag_low[:, span]))
        out[:, span] = parent_sum[:, span] + column_sum(weights[:, span] * image)
    for kid in range(2):
        for span in spans(kid_size):
            image = border_lower[kid, :, span] - dot(fold[0], lift_high[kid, :, span])
            target = size + kid * kid_size + span.start
            out[:, target : target + COLS] = kid_sum[kid : kid + 1, span] + column_sum(reduced[kid, :, span] * image)


def finish_kernel(count, parent_ref, *refs):
    partials, (parent_out, kid_out) = refs[:count], refs[count:]
    leaf = lax.axis_index("leaf")
    size, kid_size = parent_out.shape[1], kid_out.shape[1]
    sums = []
    for group in (partials[: count // 2], partials[count // 2 :]):
        terms = [group[at][...] + group[at + 1][...] for at in range(0, len(group), 2)]
        sums.append(functools.reduce(jnp.add, terms))
    owner, _ = place_of()
    parent_out[...] = jnp.where(owner == leaf, sums[0][:, :size], sums[1][:, :size])
    for parent, total in ((owner, sums[0]), (owner ^ 1, sums[1])):
        _, ids = kids_of(parent_ref, parent)
        for place in range(2):
            for kid in range(2):

                @pl.when(ids[place] == 2 * leaf + kid)
                def _(total=total, place=place, kid=kid):
                    start = size + place * kid_size
                    kid_out[kid : kid + 1] = total[:, start : start + kid_size]


def call(kernel, out_shape, scalars, limit, scratch=(), flops=0, moved=0):
    def run(*args):
        specs = [pl.BlockSpec(memory_space=pltpu.SMEM if at < scalars else pltpu.VMEM) for at in range(len(args))]
        args = [
            value if at < scalars else pltpu.with_memory_space_constraint(value, pltpu.VMEM)
            for at, value in enumerate(args)
        ]
        return pl.pallas_call(
            kernel,
            out_shape=jax.tree.map(lambda leaf: pltpu.VMEM(leaf.shape, leaf.dtype), out_shape),
            in_specs=specs,
            out_specs=jax.tree.map(lambda _: pl.BlockSpec(memory_space=pltpu.VMEM), out_shape),
            scratch_shapes=scratch,
            compiler_params=pltpu.CompilerParams(vmem_limit_bytes=limit * MIB),
            cost_estimate=pl.CostEstimate(flops=flops, bytes_accessed=moved, transcendentals=0),
        )(*args)

    return run


def shards(border, factor, diagonal, kid_rows, kid_inverse, child_index, child_parent):
    border, factor, diagonal = border[0], factor[0], diagonal[0]
    pieces = lax.axis_size("front")
    size, kid_size, border_size = diagonal.shape[1], kid_rows.shape[2], border.shape[1]
    own_border = border.shape[0]
    lanes = kid_size // LANES
    half = jnp.bfloat16

    def over_fronts(value):
        parts = {0: value}
        bit = 2
        while bit < pieces:
            for mask in list(parts):
                parts[mask | bit] = exchange(parts[mask], 0, bit)
            bit *= 2
        return parts

    def over_cores(parts, *others):
        return {mask | 1: exchange(after(part, *others), 1, 0) for mask, part in parts.items()}

    def spread(parts, gate_own, gate_rest):
        own = {0: parts[0]}
        rest = {mask: part for mask, part in parts.items() if mask}
        return parts | over_cores(own, gate_own) | over_cores(rest, gate_rest)

    def listed(parts):
        return [parts[mask] for mask in range(pieces)]

    last = pieces - 2
    crossed_diagonal = cross(diagonal)
    kid_bytes = kid_rows.size * 4 + kid_inverse.size * 4
    own_inverse, own_kids = call(
        select_kernel, (shape_of(kid_inverse.shape), shape_of(kid_rows.shape)), 1, 4, moved=3 * kid_bytes
    )(child_parent, kid_inverse, kid_rows, exchange(kid_inverse, 1, 0), exchange(kid_rows, 1, 0))
    own_inverse = cross(after(own_inverse, crossed_diagonal))
    own_kids = cross(after(own_kids, crossed_diagonal))
    own_factor = cross(after(factor, own_kids))
    own_border_rows = cross(after(border, own_factor))

    diagonal_parts = over_fronts(crossed_diagonal)
    inverse_parts = over_fronts(after(own_inverse, diagonal_parts[last]))
    kid_parts = over_fronts(after(own_kids, inverse_parts[0]))
    arrived = kid_parts[last]
    diagonal_parts = spread(diagonal_parts, own_kids, arrived)
    inverse_parts = spread(inverse_parts, own_kids, arrived)
    kid_parts = spread(kid_parts, own_kids, arrived)
    factor_parts = over_fronts(after(own_factor, inverse_parts[last | 1]))
    factor_parts[0] = own_factor

    reduced, lower_high, *state = call(
        functools.partial(kid_kernel, pieces),
        (
            shape_of((2, own_border, kid_size)),
            shape_of((2, border_size, kid_size), half),
            shape_of((own_border, size)),
            shape_of((2, size, kid_size), half),
            shape_of((size, size), half),
            shape_of((size, size), half),
            shape_of((1, size)),
            shape_of((2, kid_size)),
        ),
        2,
        22,
        [
            pltpu.VMEM(((size + border_size) * lanes, LANES), jnp.float32),
            pltpu.VMEM((kid_rows.shape[1] * lanes, LANES), jnp.float32),
            pltpu.VMEM((kid_size, kid_size), half),
            pltpu.VMEM((kid_size, kid_size), half),
            pltpu.VMEM((size, kid_size), half),
            pltpu.VMEM((size, kid_size), half),
            pltpu.VMEM((size, COLS), jnp.float32),
        ],
        flops=10_000_000_000,
        moved=10_000_000,
    )(child_parent, child_index, own_factor, *listed(diagonal_parts), *listed(inverse_parts), *listed(kid_parts))

    factor_parts = spread(factor_parts, arrived, state[0])

    border_high, border_lower = call(
        border_kernel,
        (shape_of(border.shape, half), shape_of((2, own_border, kid_size))),
        0,
        8,
        flops=1_200_000_000,
        moved=1_000_000,
    )(own_border_rows, lower_high)

    total = call(
        functools.partial(image_kernel, pieces),
        shape_of((1, size + 2 * kid_size)),
        0,
        16,
        [
            pltpu.VMEM((border_size, size), half),
            pltpu.VMEM((own_border, size), half),
            pltpu.VMEM((own_border, size), half),
        ],
        flops=3_000_000_000,
        moved=1_000_000,
    )(*listed(factor_parts), border_high, border_lower, reduced, *state)

    bit = 4
    while bit < pieces:
        total = total + exchange(total, 0, bit)
        bit *= 2
    low = range(min(pieces, 4))
    order = [(core, mask) for parity in (0, 1) for mask in low if mask % 2 == parity for core in (0, 1)]
    partials = [exchange(total, core, mask) if core or mask else total for core, mask in order]
    return call(
        functools.partial(finish_kernel, len(partials)), (shape_of((1, size)), shape_of((2, kid_size))), 1, 4
    )(child_parent, *partials)


def solution(mesh):
    whole = P("leaf", "front", None)
    return jax.shard_map(
        shards,
        mesh=mesh,
        in_specs=(whole,) * 5 + (P(), P()),
        out_specs=(P("leaf", None), P("leaf", None)),
        check_vma=False,
    )
```

```python
import functools

import jax
import jax.numpy as jnp
from jax import lax
from jax.experimental import pallas as pl
from jax.experimental.pallas import tpu as pltpu
from jax.sharding import PartitionSpec as P

MIB = 1024 * 1024
COLS = 256


def shape_of(shape, dtype=jnp.float32):
    return jax.ShapeDtypeStruct(shape, dtype)


def exchange(value, leaf_mask, front_mask):
    fronts = lax.axis_size("front")
    pairs = [
        (leaf * fronts + front, (leaf ^ leaf_mask) * fronts + (front ^ front_mask))
        for leaf in range(lax.axis_size("leaf"))
        for front in range(fronts)
    ]
    return lax.ppermute(value, ("leaf", "front"), pairs)


def cross(value):
    fronts = lax.axis_size("front")
    pairs = []
    for leaf in range(lax.axis_size("leaf")):
        for front in range(fronts):
            flip = (leaf ^ front) & 1
            pairs.append((leaf * fronts + front, (leaf ^ flip) * fronts + (front ^ flip)))
    return lax.ppermute(value, ("leaf", "front"), pairs)


def after(value, *others):
    return lax.optimization_barrier((value, *others))[0]


def kids_of(parent_ref, owner):
    partner = owner ^ 1
    pool = [2 * owner, 2 * owner + 1, 2 * partner, 2 * partner + 1]
    member = [parent_ref[kid] == owner for kid in pool]
    first = jnp.where(member[0], 0, jnp.where(member[1], 1, 2))
    second = jnp.where(member[3], 3, jnp.where(member[2], 2, 1))
    ids = [2 * jnp.where(slot < 2, owner, partner) + (slot & 1) for slot in (first, second)]
    return (first, second), ids


def place_of():
    front, leaf = lax.axis_index("front"), lax.axis_index("leaf")
    owner = (leaf & -2) | (front & 1)
    block = (front & -2) | (leaf & 1)
    return owner, block


def rounded(value):
    return value.astype(jnp.bfloat16)


def halves(value):
    high = rounded(value)
    return high, rounded(value - high.astype(jnp.float32))


def dot(left, right):
    return jnp.dot(left, right, preferred_element_type=jnp.float32)


def product(left, right):
    (left_high, left_low), (right_high, right_low) = left, right
    return dot(left_high, right_high) + (dot(left_high, right_low) + dot(left_low, right_high))


def column_sum(value):
    return jnp.sum(value, axis=0, keepdims=True)


def spans(width):
    return [slice(start, start + COLS) for start in range(0, width, COLS)]


def select_kernel(parent_ref, index_ref, own_rows, own_inverse, other_rows, other_inverse, kid_out, index_out):
    leaf = lax.axis_index("leaf")
    slots, _ = kids_of(parent_ref, leaf)
    split = own_rows.shape[1]
    for place, slot in enumerate(slots):
        for source in range(4):
            rows, inverse = (own_rows, own_inverse) if source < 2 else (other_rows, other_inverse)

            @pl.when(slot == source)
            def _(rows=rows, inverse=inverse, place=place, source=source):
                kid_out[place, :split] = rows[source % 2]
                kid_out[place, split:] = inverse[source % 2]

    owner, block = place_of()
    _, ids = kids_of(parent_ref, owner)
    for place, kid in enumerate(ids):
        for mask in range(index_out.shape[1]):
            index_out[place, mask : mask + 1, :] = index_ref[kid, pl.ds(block ^ mask, 1), :]


def picks(index, first, rows):
    position = lax.broadcasted_iota(jnp.int32, (rows, index.shape[1]), 0) + first
    return rounded(jnp.where(position == index, 1.0, 0.0))


def diagonal_kernel(pieces, index, *refs):
    diagonal = refs[:pieces]
    diag_high, diag_low, pick_high, pick_low, parent_sum = refs[pieces:]
    _, block = place_of()
    own_rows, size = diagonal[0].shape
    parent_sum[...] = column_sum(diagonal[0][...] * diagonal[0][...])
    for mask in range(pieces):
        start = pl.multiple_of((block ^ mask) * own_rows, 16)
        high, low = halves(diagonal[mask][...])
        diag_high[pl.ds(start, own_rows), :] = high
        diag_low[pl.ds(start, own_rows), :] = low
    for kid in range(2):
        for mask in range(pieces):
            pick = picks(index[kid, mask : mask + 1, :], 0, size)
            pick_high[kid, mask] = rounded(dot(diag_high[...], pick))
            pick_low[kid, mask] = rounded(dot(diag_low[...], pick))


def kid_kernel(pieces, index, pick_high, pick_low, head, tail, *refs):
    kids = refs[:pieces]
    reduced, lift_high, kid_high, kid_sum, inv_high, inv_low, lifted = refs[pieces:]
    _, block = place_of()
    size, own_border = lifted.shape[0], head.shape[0] + tail.shape[0]
    kid_block = kid_high.shape[2]
    inv_block, own_rows = kids[0].shape[1] - kid_block, size // pieces
    factor_high = jnp.concatenate([rounded(head[...]), rounded(tail[...])], axis=0)
    for kid in range(2):
        own_inverse = kids[0][kid, kid_block:]
        for mask in range(pieces):
            start = pl.multiple_of((block ^ mask) * inv_block, 16)
            high, low = halves(kids[mask][kid, kid_block:])
            inv_high[pl.ds(start, inv_block), :] = high
            inv_low[pl.ds(start, inv_block), :] = low
        inverse = inv_high[...], inv_low[...]
        for mask in range(pieces):
            weight = halves(product(halves(kids[mask][kid, :kid_block]), inverse))
            kid_high[kid, mask] = weight[0]
            lifted_part = product((pick_high[kid, mask], pick_low[kid, mask]), weight)
            pick = picks(index[kid, mask : mask + 1, :], size + block * own_border, own_border)
            lower_part = dot(pick, weight[0]) + dot(pick, weight[1])
            lifted[...] = lifted_part if mask == 0 else lifted[...] + lifted_part
            reduced[kid] = lower_part if mask == 0 else reduced[kid] + lower_part
        own = lifted[pl.ds(pl.multiple_of(block * own_rows, 16), own_rows), :]
        kid_sum[kid : kid + 1] = column_sum(own_inverse * own_inverse) + column_sum(own * own)
        lift_high[kid] = rounded(lifted[...])
        reduced[kid] = reduced[kid] - dot(factor_high, lift_high[kid])


def border_kernel(index, border, head, tail, diag_high, diag_low, kid_high, border_high, border_lower, weights):
    border_high[...] = rounded(border[...])
    size, border_size = head.shape[1], border.shape[1]
    for kid in range(2):
        for mask in range(kid_high.shape[1]):
            pick = picks(index[kid, mask : mask + 1, :], size, border_size)
            rows = rounded(dot(border_high[...], pick))
            part = dot(rows, kid_high[kid, mask])
            border_lower[kid] = part if mask == 0 else border_lower[kid] + part
    for part, start in ((head, 0), (tail, head.shape[0])):
        part_halves = halves(part[...])
        rows = slice(start, start + part.shape[0])
        for span in spans(size):
            weights[rows, span] = product(part_halves, (diag_high[:, span], diag_low[:, span]))


def image_kernel(pieces, *refs):
    heads, tails = refs[:pieces], refs[pieces : 2 * pieces]
    border_high, border_lower, weights, reduced, lift_high, diag_high, diag_low, parent_sum, kid_sum, out = refs[
        2 * pieces : 2 * pieces + 10
    ]
    factor_high, fold_high, fold_low = refs[2 * pieces + 10 :]
    _, block = place_of()
    head, size = heads[0].shape
    tail = tails[0].shape[0]
    kid_size = reduced.shape[2]
    for mask in range(pieces):
        start = pl.multiple_of((block ^ mask) * (head + tail), 16)
        factor_high[pl.ds(start, head), :] = rounded(heads[mask][...])
        factor_high[pl.ds(pl.multiple_of(start + head, 16), tail), :] = rounded(tails[mask][...])
    for span in spans(size):
        fold_high[:, span], fold_low[:, span] = halves(dot(border_high[...], factor_high[:, span]))
    fold = fold_high[...], fold_low[...]
    for span in spans(size):
        image = product(fold, (diag_high[:, span], diag_low[:, span]))
        out[:, span] = parent_sum[:, span] + column_sum(weights[:, span] * image)
    for kid in range(2):
        for span in spans(kid_size):
            image = border_lower[kid, :, span] - dot(fold[0], lift_high[kid, :, span])
            target = size + kid * kid_size + span.start
            out[:, target : target + COLS] = kid_sum[kid : kid + 1, span] + column_sum(reduced[kid, :, span] * image)


def finish_kernel(parent_ref, *refs):
    partials, (parent_out, kid_out) = refs[:-2], refs[-2:]
    leaf = lax.axis_index("leaf")
    size, kid_size = parent_out.shape[1], kid_out.shape[1]
    half = len(partials) // 2
    sums = [functools.reduce(jnp.add, [ref[...] for ref in group]) for group in (partials[:half], partials[half:])]
    owner, _ = place_of()
    parent_out[...] = jnp.where(owner == leaf, sums[0][:, :size], sums[1][:, :size])
    for parent, total in ((owner, sums[0]), (owner ^ 1, sums[1])):
        _, ids = kids_of(parent_ref, parent)
        for place in range(2):
            for kid in range(2):

                @pl.when(ids[place] == 2 * leaf + kid)
                def _(total=total, place=place, kid=kid):
                    start = size + place * kid_size
                    kid_out[kid : kid + 1] = total[:, start : start + kid_size]


def call(kernel, out_shape, limit, scalars=0, loose=0, keep=True, scratch=(), moved=1_000):
    def run(*args):
        specs = [pl.BlockSpec(memory_space=pltpu.SMEM if at < scalars else pltpu.VMEM) for at in range(len(args))]
        args = [
            pltpu.with_memory_space_constraint(value, pltpu.HBM if at < loose else pltpu.VMEM)
            for at, value in enumerate(args)
        ]
        results = out_shape
        if keep:
            results = jax.tree.map(lambda leaf: pltpu.VMEM(leaf.shape, leaf.dtype), results)
        return pl.pallas_call(
            kernel,
            out_shape=results,
            in_specs=specs,
            out_specs=jax.tree.map(lambda _: pl.BlockSpec(memory_space=pltpu.VMEM), out_shape),
            scratch_shapes=scratch,
            compiler_params=pltpu.CompilerParams(vmem_limit_bytes=limit * MIB),
            cost_estimate=pl.CostEstimate(flops=0, bytes_accessed=moved, transcendentals=0),
        )(*args)

    return run


def shards(border, factor, diagonal, kid_rows, kid_inverse, child_index, child_parent):
    border, factor, diagonal = border[0], factor[0], diagonal[0]
    pieces = lax.axis_size("front")
    size, kid_size, border_size = diagonal.shape[1], kid_rows.shape[2], border.shape[1]
    own_border = border.shape[0]
    kid_block = kid_rows.shape[1]
    half = jnp.bfloat16

    def over_fronts(value):
        parts = {0: value}
        bit = 2
        while bit < pieces:
            for mask in list(parts):
                parts[mask | bit] = exchange(parts[mask], 0, bit)
            bit *= 2
        return parts

    def spread(parts, gate_own, gate_rest):
        shared = {1: exchange(after(parts[0], *gate_own), 1, 0)}
        for mask in list(parts)[1:]:
            shared[mask | 1] = exchange(after(parts[mask], *gate_rest), 1, 0)
        parts = parts | shared
        return [parts[mask] for mask in range(pieces)]

    last = pieces - 2
    head = -(-own_border // 64) * 16
    factor_head, factor_tail = factor[:head], factor[head:]
    raw_heads = over_fronts(factor_head)
    own_diagonal = cross(diagonal)
    index = child_index.reshape(child_index.shape[0], pieces, kid_block)
    kid_shape = (2, kid_block + kid_inverse.shape[1], kid_size)
    own_kids, index = call(
        select_kernel,
        (shape_of(kid_shape), shape_of((2, pieces, kid_block), jnp.int32)),
        6,
        scalars=1,
        loose=4,
    )(child_parent, index, kid_rows, kid_inverse, exchange(kid_rows, 1, 0), exchange(kid_inverse, 1, 0))
    own_kids = cross(after(own_kids, own_diagonal, raw_heads[last]))
    own_tail = cross(after(factor_tail, own_kids))
    heads = {mask: cross(after(value, own_kids)) for mask, value in raw_heads.items()}
    own_border_rows = cross(after(border, own_kids))

    diagonal_parts = over_fronts(own_diagonal)
    kid_parts = over_fronts(after(own_kids, diagonal_parts[last]))
    diagonal_parts = spread(diagonal_parts, [own_kids], [own_kids])
    diag_high, diag_low, pick_high, pick_low, parent_sum = call(
        functools.partial(diagonal_kernel, pieces),
        (
            shape_of((size, size), half),
            shape_of((size, size), half),
            shape_of((2, pieces, size, kid_block), half),
            shape_of((2, pieces, size, kid_block), half),
            shape_of((1, size)),
        ),
        10,
    )(after(index, own_tail, *heads.values()), *diagonal_parts)
    kids_here = after(kid_parts[last], pick_high)
    tails = over_fronts(after(own_tail, kids_here))
    tails[0] = own_tail
    kid_parts = spread(kid_parts, [], [pick_high])
    own_head = heads[0]
    heads = spread(heads, [kids_here], [kids_here])

    reduced, lift_high, kid_high, kid_sum = call(
        functools.partial(kid_kernel, pieces),
        (
            shape_of((2, own_border, kid_size)),
            shape_of((2, size, kid_size), half),
            shape_of((2, pieces, kid_block, kid_size), half),
            shape_of((2, kid_size)),
        ),
        12,
        scratch=[
            pltpu.VMEM((kid_size, kid_size), half),
            pltpu.VMEM((kid_size, kid_size), half),
            pltpu.VMEM((size, kid_size), jnp.float32),
        ],
    )(index, pick_high, pick_low, own_head, after(own_tail, *heads), *kid_parts)

    border_high, border_lower, weights = call(
        border_kernel,
        (shape_of(border.shape, half), shape_of((2, own_border, kid_size)), shape_of((own_border, size))),
        12,
    )(index, own_border_rows, own_head, own_tail, diag_high, diag_low, kid_high)

    tails = spread(tails, [kids_here], [border_lower])
    total = call(
        functools.partial(image_kernel, pieces),
        shape_of((1, size + 2 * kid_size)),
        12,
        scratch=[
            pltpu.VMEM((border_size, size), half),
            pltpu.VMEM((own_border, size), half),
            pltpu.VMEM((own_border, size), half),
        ],
    )(
        *heads,
        *tails,
        border_high,
        border_lower,
        weights,
        reduced,
        lift_high,
        diag_high,
        diag_low,
        parent_sum,
        kid_sum,
    )

    total = total + exchange(total, 1, 0)
    bit = 4
    while bit < pieces:
        total = total + exchange(total, 0, bit)
        bit *= 2
    near = range(min(pieces, 4))
    order = [mask for parity in (0, 1) for mask in near if mask % 2 == parity]
    partials = [exchange(total, 0, mask) if mask else total for mask in order]
    return call(finish_kernel, (shape_of((1, size)), shape_of((2, kid_size))), 2, scalars=1, loose=1, keep=False)(
        child_parent, *partials
    )


def solution(mesh):
    whole = P("leaf", "front", None)
    return jax.shard_map(
        shards,
        mesh=mesh,
        in_specs=(whole,) * 5 + (P(), P()),
        out_specs=(P("leaf", None), P("leaf", None)),
        check_vma=False,
    )
```

```python
import functools

import jax
import jax.numpy as jnp
from jax import lax
from jax.experimental import pallas as pl
from jax.experimental.pallas import tpu as pltpu
from jax.sharding import PartitionSpec as P

MIB = 1024 * 1024
COLS = 256


def shape_of(shape, dtype=jnp.float32):
    return jax.ShapeDtypeStruct(shape, dtype)


def exchange(value, leaf_mask, front_mask):
    fronts = lax.axis_size("front")
    pairs = [
        (leaf * fronts + front, (leaf ^ leaf_mask) * fronts + (front ^ front_mask))
        for leaf in range(lax.axis_size("leaf"))
        for front in range(fronts)
    ]
    return lax.ppermute(value, ("leaf", "front"), pairs)


def cross(value):
    fronts = lax.axis_size("front")
    pairs = []
    for leaf in range(lax.axis_size("leaf")):
        for front in range(fronts):
            flip = (leaf ^ front) & 1
            pairs.append((leaf * fronts + front, (leaf ^ flip) * fronts + (front ^ flip)))
    return lax.ppermute(value, ("leaf", "front"), pairs)


def after(value, *others):
    return lax.optimization_barrier((value, *others))[0]


def kids_of(parent_ref, owner):
    partner = owner ^ 1
    pool = [2 * owner, 2 * owner + 1, 2 * partner, 2 * partner + 1]
    member = [parent_ref[kid] == owner for kid in pool]
    first = jnp.where(member[0], 0, jnp.where(member[1], 1, 2))
    second = jnp.where(member[3], 3, jnp.where(member[2], 2, 1))
    ids = [2 * jnp.where(slot < 2, owner, partner) + (slot & 1) for slot in (first, second)]
    return (first, second), ids


def place_of():
    front, leaf = lax.axis_index("front"), lax.axis_index("leaf")
    owner = (leaf & -2) | (front & 1)
    block = (front & -2) | (leaf & 1)
    return owner, block


def rounded(value):
    return value.astype(jnp.bfloat16)


def halves(value):
    high = rounded(value)
    return high, rounded(value - high.astype(jnp.float32))


def dot(left, right):
    return jnp.dot(left, right, preferred_element_type=jnp.float32)


def product(left, right):
    (left_high, left_low), (right_high, right_low) = left, right
    return dot(left_high, right_high) + (dot(left_high, right_low) + dot(left_low, right_high))


def column_sum(value):
    return jnp.sum(value, axis=0, keepdims=True)


def spans(width):
    return [slice(start, start + COLS) for start in range(0, width, COLS)]


def select_kernel(parent_ref, index_ref, own_rows, own_inverse, other_rows, other_inverse, kid_out, index_out):
    leaf = lax.axis_index("leaf")
    slots, _ = kids_of(parent_ref, leaf)
    split = own_rows.shape[1]
    for place, slot in enumerate(slots):
        for source in range(4):
            rows, inverse = (own_rows, own_inverse) if source < 2 else (other_rows, other_inverse)

            @pl.when(slot == source)
            def _(rows=rows, inverse=inverse, place=place, source=source):
                kid_out[place, :split] = rows[source % 2]
                kid_out[place, split:] = inverse[source % 2]

    owner, block = place_of()
    _, ids = kids_of(parent_ref, owner)
    pieces, width = index_out.shape[1:]
    for place, kid in enumerate(ids):
        row = index_ref[pl.ds(kid, 1), :]
        parts = [row[:, start : start + width] for start in range(0, pieces * width, width)]
        for mask in range(pieces):
            part = parts[0]
            for at in range(1, pieces):
                part = jnp.where((block ^ mask) == at, parts[at], part)
            index_out[place, mask : mask + 1, :] = part


def picks(index, first, rows):
    position = lax.broadcasted_iota(jnp.int32, (rows, index.shape[1]), 0) + first
    return rounded(jnp.where(position == index, 1.0, 0.0))


def diagonal_kernel(pieces, index, *refs):
    diagonal = refs[:pieces]
    diag_high, diag_low, pick_high, pick_low, parent_sum = refs[pieces:]
    _, block = place_of()
    own_rows, size = diagonal[0].shape
    parent_sum[...] = column_sum(diagonal[0][...] * diagonal[0][...])
    for mask in range(pieces):
        start = pl.multiple_of((block ^ mask) * own_rows, 16)
        high, low = halves(diagonal[mask][...])
        diag_high[pl.ds(start, own_rows), :] = high
        diag_low[pl.ds(start, own_rows), :] = low
    for kid in range(2):
        for mask in range(pieces):
            pick = picks(index[kid, mask : mask + 1, :], 0, size)
            pick_high[kid, mask] = rounded(dot(diag_high[...], pick))
            pick_low[kid, mask] = rounded(dot(diag_low[...], pick))


def kid_kernel(pieces, index, pick_high, pick_low, factor, diag_high, diag_low, *refs):
    kids = refs[:pieces]
    reduced, lift_high, lower_high, weights, kid_sum, inv_high, inv_low, lifted, lower = refs[pieces:]
    _, block = place_of()
    size, own_border, border_size = lifted.shape[0], factor.shape[0], lower.shape[0]
    kid_block = index.shape[2]
    inv_block, own_rows = kids[0].shape[1] - kid_block, size // pieces
    factor_halves = halves(factor[...])
    for span in spans(size):
        weights[:, span] = product(factor_halves, (diag_high[:, span], diag_low[:, span]))
    for kid in range(2):
        own_inverse = kids[0][kid, kid_block:]
        for mask in range(pieces):
            start = pl.multiple_of((block ^ mask) * inv_block, 16)
            high, low = halves(kids[mask][kid, kid_block:])
            inv_high[pl.ds(start, inv_block), :] = high
            inv_low[pl.ds(start, inv_block), :] = low
        inverse = inv_high[...], inv_low[...]
        for mask in range(pieces):
            weight = halves(product(halves(kids[mask][kid, :kid_block]), inverse))
            lifted_part = product((pick_high[kid, mask], pick_low[kid, mask]), weight)
            pick = picks(index[kid, mask : mask + 1, :], size + block * own_border, own_border)
            lower_part = dot(pick, weight[0]) + dot(pick, weight[1])
            lifted[...] = lifted_part if mask == 0 else lifted[...] + lifted_part
            reduced[kid] = lower_part if mask == 0 else reduced[kid] + lower_part
            part = dot(picks(index[kid, mask : mask + 1, :], size, border_size), weight[0])
            lower[...] = part if mask == 0 else lower[...] + part
        own = lifted[pl.ds(pl.multiple_of(block * own_rows, 16), own_rows), :]
        kid_sum[kid : kid + 1] = column_sum(own_inverse * own_inverse) + column_sum(own * own)
        lift_high[kid] = rounded(lifted[...])
        lower_high[kid] = rounded(lower[...])
        reduced[kid] = reduced[kid] - dot(factor_halves[0], lift_high[kid])


def border_kernel(border, lower_high, border_high, border_lower):
    border_high[...] = rounded(border[...])
    for kid in range(2):
        for span in spans(lower_high.shape[2]):
            border_lower[kid, :, span] = dot(border_high[...], lower_high[kid, :, span])


def image_kernel(pieces, *refs):
    factor = refs[:pieces]
    border_high, border_lower, weights, reduced, lift_high, diag_high, diag_low, parent_sum, kid_sum, out = refs[
        pieces : pieces + 10
    ]
    factor_high, fold_high, fold_low = refs[pieces + 10 :]
    _, block = place_of()
    own_border, size = factor[0].shape
    kid_size = reduced.shape[2]
    for mask in range(pieces):
        start = pl.multiple_of((block ^ mask) * own_border, 16)
        factor_high[pl.ds(start, own_border), :] = rounded(factor[mask][...])
    for span in spans(size):
        fold_high[:, span], fold_low[:, span] = halves(dot(border_high[...], factor_high[:, span]))
    fold = fold_high[...], fold_low[...]
    for span in spans(size):
        image = product(fold, (diag_high[:, span], diag_low[:, span]))
        out[:, span] = parent_sum[:, span] + column_sum(weights[:, span] * image)
    for kid in range(2):
        for span in spans(kid_size):
            image = border_lower[kid, :, span] - dot(fold[0], lift_high[kid, :, span])
            target = size + kid * kid_size + span.start
            out[:, target : target + COLS] = kid_sum[kid : kid + 1, span] + column_sum(reduced[kid, :, span] * image)


def finish_kernel(parent_ref, *refs):
    partials, (parent_out, kid_out) = refs[:-2], refs[-2:]
    leaf = lax.axis_index("leaf")
    size, kid_size = parent_out.shape[1], kid_out.shape[1]
    half = len(partials) // 2
    sums = [functools.reduce(jnp.add, [ref[...] for ref in group]) for group in (partials[:half], partials[half:])]
    owner, _ = place_of()
    parent_out[...] = jnp.where(owner == leaf, sums[0][:, :size], sums[1][:, :size])
    for parent, total in ((owner, sums[0]), (owner ^ 1, sums[1])):
        _, ids = kids_of(parent_ref, parent)
        for place in range(2):
            for kid in range(2):

                @pl.when(ids[place] == 2 * leaf + kid)
                def _(total=total, place=place, kid=kid):
                    start = size + place * kid_size
                    kid_out[kid : kid + 1] = total[:, start : start + kid_size]


def call(kernel, out_shape, limit, scalars=0, loose=0, keep=True, scratch=(), moved=1_000):
    def run(*args):
        specs = [pl.BlockSpec(memory_space=pltpu.SMEM if at < scalars else pltpu.VMEM) for at in range(len(args))]
        args = [
            pltpu.with_memory_space_constraint(value, pltpu.HBM if at < loose else pltpu.VMEM)
            for at, value in enumerate(args)
        ]
        results = out_shape
        if keep:
            results = jax.tree.map(lambda leaf: pltpu.VMEM(leaf.shape, leaf.dtype), results)
        return pl.pallas_call(
            kernel,
            out_shape=results,
            in_specs=specs,
            out_specs=jax.tree.map(lambda _: pl.BlockSpec(memory_space=pltpu.VMEM), out_shape),
            scratch_shapes=scratch,
            compiler_params=pltpu.CompilerParams(vmem_limit_bytes=limit * MIB),
            cost_estimate=pl.CostEstimate(flops=0, bytes_accessed=moved, transcendentals=0),
        )(*args)

    return run


def shards(border, factor, diagonal, kid_rows, kid_inverse, child_index, child_parent):
    border, factor, diagonal = border[0], factor[0], diagonal[0]
    pieces = lax.axis_size("front")
    size, kid_size, border_size = diagonal.shape[1], kid_rows.shape[2], border.shape[1]
    own_border = border.shape[0]
    kid_block = kid_rows.shape[1]
    half = jnp.bfloat16

    def over_fronts(value):
        parts = {0: value}
        bit = 2
        while bit < pieces:
            for mask in list(parts):
                parts[mask | bit] = exchange(parts[mask], 0, bit)
            bit *= 2
        return parts

    def spread(parts, gate_own, gate_rest):
        shared = {1: exchange(after(parts[0], *gate_own), 1, 0)}
        for mask in list(parts)[1:]:
            shared[mask | 1] = exchange(after(parts[mask], *gate_rest), 1, 0)
        parts = parts | shared
        return [parts[mask] for mask in range(pieces)]

    last = pieces - 2
    raw_diagonal = over_fronts(diagonal)
    own_diagonal = cross(diagonal)
    kid_shape = (2, kid_block + kid_inverse.shape[1], kid_size)
    own_kids, index = call(
        select_kernel, (shape_of(kid_shape), shape_of((2, pieces, kid_block), jnp.int32)), 6, scalars=1, loose=4
    )(child_parent, child_index, kid_rows, kid_inverse, exchange(kid_rows, 1, 0), exchange(kid_inverse, 1, 0))
    own_kids = cross(after(own_kids, own_diagonal, raw_diagonal[last]))

    diagonal_parts = {mask: cross(after(value, own_kids)) for mask, value in raw_diagonal.items() if mask}
    crossed = diagonal_parts[last]
    diagonal_parts = spread({0: own_diagonal} | diagonal_parts, [own_kids], [own_kids])
    own_factor = cross(after(factor, own_kids))
    own_border_rows = cross(after(border, crossed))
    kid_parts = over_fronts(own_kids)

    diag_high, diag_low, pick_high, pick_low, parent_sum = call(
        functools.partial(diagonal_kernel, pieces),
        (
            shape_of((size, size), half),
            shape_of((size, size), half),
            shape_of((2, pieces, size, kid_block), half),
            shape_of((2, pieces, size, kid_block), half),
            shape_of((1, size)),
        ),
        10,
    )(index, *diagonal_parts)
    kids_here = after(kid_parts[last], pick_high)
    factor_parts = over_fronts(after(own_factor, kids_here))
    factor_parts[0] = own_factor
    kid_parts = spread(kid_parts, [], [pick_high])

    reduced, lift_high, lower_high, weights, kid_sum = call(
        functools.partial(kid_kernel, pieces),
        (
            shape_of((2, own_border, kid_size)),
            shape_of((2, size, kid_size), half),
            shape_of((2, border_size, kid_size), half),
            shape_of((own_border, size)),
            shape_of((2, kid_size)),
        ),
        20,
        scratch=[
            pltpu.VMEM((kid_size, kid_size), half),
            pltpu.VMEM((kid_size, kid_size), half),
            pltpu.VMEM((size, kid_size), jnp.float32),
            pltpu.VMEM((border_size, kid_size), jnp.float32),
        ],
    )(index, pick_high, pick_low, own_factor, diag_high, diag_low, *kid_parts)

    border_high, border_lower = call(
        border_kernel, (shape_of(border.shape, half), shape_of((2, own_border, kid_size))), 8
    )(own_border_rows, lower_high)

    factor_parts = spread(factor_parts, [kids_here], [border_lower])
    total = call(
        functools.partial(image_kernel, pieces),
        shape_of((1, size + 2 * kid_size)),
        12,
        scratch=[
            pltpu.VMEM((border_size, size), half),
            pltpu.VMEM((own_border, size), half),
            pltpu.VMEM((own_border, size), half),
        ],
    )(
        *factor_parts,
        border_high,
        border_lower,
        weights,
        reduced,
        lift_high,
        diag_high,
        diag_low,
        parent_sum,
        kid_sum,
    )

    total = total + exchange(total, 1, 0)
    bit = 4
    while bit < pieces:
        total = total + exchange(total, 0, bit)
        bit *= 2
    near = range(min(pieces, 4))
    order = [mask for parity in (0, 1) for mask in near if mask % 2 == parity]
    partials = [exchange(total, 0, mask) if mask else total for mask in order]
    return call(finish_kernel, (shape_of((1, size)), shape_of((2, kid_size))), 2, scalars=1, loose=1, keep=False)(
        child_parent, *partials
    )


def solution(mesh):
    whole = P("leaf", "front", None)
    return jax.shard_map(
        shards,
        mesh=mesh,
        in_specs=(whole,) * 5 + (P(), P()),
        out_specs=(P("leaf", None), P("leaf", None)),
        check_vma=False,
    )
```

```python
import functools

import jax
import jax.numpy as jnp
from jax import lax
from jax.experimental import pallas as pl
from jax.experimental.pallas import tpu as pltpu
from jax.sharding import PartitionSpec as P

MIB = 1024 * 1024
COLS = 256


def shape_of(shape, dtype=jnp.float32):
    return jax.ShapeDtypeStruct(shape, dtype)


def exchange(value, leaf_mask, front_mask, parity=None):
    fronts = lax.axis_size("front")
    pairs = [
        (leaf * fronts + front, (leaf ^ leaf_mask) * fronts + (front ^ front_mask))
        for leaf in range(lax.axis_size("leaf"))
        for front in range(fronts)
        if parity is None or (leaf ^ front) & 1 == parity
    ]
    return lax.ppermute(value, ("leaf", "front"), pairs)


def cross(value):
    fronts = lax.axis_size("front")
    pairs = []
    for leaf in range(lax.axis_size("leaf")):
        for front in range(fronts):
            flip = (leaf ^ front) & 1
            pairs.append((leaf * fronts + front, (leaf ^ flip) * fronts + (front ^ flip)))
    return lax.ppermute(value, ("leaf", "front"), pairs)


def after(value, *others):
    return lax.optimization_barrier((value, *others))[0]


def kids_of(parent_ref, owner):
    partner = owner ^ 1
    pool = [2 * owner, 2 * owner + 1, 2 * partner, 2 * partner + 1]
    member = [parent_ref[kid] == owner for kid in pool]
    first = jnp.where(member[0], 0, jnp.where(member[1], 1, 2))
    second = jnp.where(member[3], 3, jnp.where(member[2], 2, 1))
    ids = [2 * jnp.where(slot < 2, owner, partner) + (slot & 1) for slot in (first, second)]
    return (first, second), ids


def place_of():
    front, leaf = lax.axis_index("front"), lax.axis_index("leaf")
    owner = (leaf & -2) | (front & 1)
    block = (front & -2) | (leaf & 1)
    return owner, block


def keeps():
    return ((lax.axis_index("leaf") ^ lax.axis_index("front")) & 1) == 0


def store(pair, action):
    for ref, chosen in zip(pair, (keeps(), jnp.logical_not(keeps()))):
        pl.when(chosen)(functools.partial(action, ref))


def rounded(value):
    return value.astype(jnp.bfloat16)


def halves(value):
    high = rounded(value)
    return high, rounded(value - high.astype(jnp.float32))


def dot(left, right):
    return jnp.dot(left, right, preferred_element_type=jnp.float32)


def product(left, right):
    (left_high, left_low), (right_high, right_low) = left, right
    return dot(left_high, right_high) + (dot(left_high, right_low) + dot(left_low, right_high))


def column_sum(value):
    return jnp.sum(value, axis=0, keepdims=True)


def spans(width):
    return [slice(start, start + COLS) for start in range(0, width, COLS)]


def select_kernel(parent_ref, index_ref, own_rows, own_inverse, other_rows, other_inverse, first_out, second_out, index_out):
    leaf = lax.axis_index("leaf")
    slots, _ = kids_of(parent_ref, leaf)
    split = own_rows.shape[1]
    for place, slot in enumerate(slots):
        for source in range(4):
            rows, inverse = (own_rows, own_inverse) if source < 2 else (other_rows, other_inverse)

            @pl.when(slot == source)
            def _(rows=rows, inverse=inverse, place=place, source=source):
                kid_out = (first_out, second_out)[place]
                kid_out[:split] = rows[source % 2]
                kid_out[split:] = inverse[source % 2]

    owner, block = place_of()
    _, ids = kids_of(parent_ref, owner)
    pieces, width = index_out.shape[1:]
    for place, kid in enumerate(ids):
        row = index_ref[pl.ds(kid, 1), :]
        parts = [row[:, start : start + width] for start in range(0, pieces * width, width)]
        for mask in range(pieces):
            part = parts[0]
            for at in range(1, pieces):
                part = jnp.where((block ^ mask) == at, parts[at], part)
            index_out[place, mask : mask + 1, :] = part


def picks(index, first, rows):
    position = lax.broadcasted_iota(jnp.int32, (rows, index.shape[1]), 0) + first
    return rounded(jnp.where(position == index, 1.0, 0.0))


def unpacked(pieces, refs):
    pairs = [(refs[0], refs[0]), (refs[1], refs[1])]
    for at in range(2, 2 * pieces - 2, 4):
        near_keep, near_swap, far_keep, far_swap = refs[at : at + 4]
        pairs += [(near_keep, near_swap), (far_keep, far_swap)]
    return pairs


def diagonal_kernel(pieces, index, *refs):
    diagonal = unpacked(pieces, refs)
    diag_high, diag_low, pick_high, pick_low, parent_sum = refs[2 * pieces - 2 :]
    _, block = place_of()
    own_rows, size = refs[0].shape
    parent_sum[...] = column_sum(refs[0][...] * refs[0][...])
    for mask, pair in enumerate(diagonal):
        start = pl.multiple_of((block ^ mask) * own_rows, 16)

        def put(ref, start=start):
            diag_high[pl.ds(start, own_rows), :], diag_low[pl.ds(start, own_rows), :] = halves(ref[...])

        if mask < 2:
            put(pair[0])
        else:
            store(pair, put)
    for kid in range(2):
        for mask in range(pieces):
            pick = picks(index[kid, mask : mask + 1, :], 0, size)
            pick_high[kid, mask] = rounded(dot(diag_high[...], pick))
            pick_low[kid, mask] = rounded(dot(diag_low[...], pick))


def kid_kernel(pieces, kid, index, pick_high, pick_low, factor, diag_high, diag_low, *refs):
    kids = refs[:pieces]
    reduced, lift_high, lower_high, kid_sum, *weights = refs[pieces:-4]
    inv_high, inv_low, lifted, lower = refs[-4:]
    _, block = place_of()
    size, own_border, border_size = lifted.shape[0], factor.shape[0], lower.shape[0]
    kid_block = index.shape[2]
    inv_block, own_rows = kids[0].shape[0] - kid_block, size // pieces
    factor_halves = halves(factor[...])
    for out in weights:
        for span in spans(size):
            out[:, span] = product(factor_halves, (diag_high[:, span], diag_low[:, span]))
    own_inverse = kids[0][kid_block:]
    for mask in range(pieces):
        start = pl.multiple_of((block ^ mask) * inv_block, 16)
        high, low = halves(kids[mask][kid_block:])
        inv_high[pl.ds(start, inv_block), :] = high
        inv_low[pl.ds(start, inv_block), :] = low
    inverse = inv_high[...], inv_low[...]
    for mask in range(pieces):
        weight = halves(product(halves(kids[mask][:kid_block]), inverse))
        lifted_part = product((pick_high[kid, mask], pick_low[kid, mask]), weight)
        pick = picks(index[kid, mask : mask + 1, :], size + block * own_border, own_border)
        own_part = dot(pick, weight[0]) + dot(pick, weight[1])
        part = dot(picks(index[kid, mask : mask + 1, :], size, border_size), weight[0])
        lifted[...] = lifted_part if mask == 0 else lifted[...] + lifted_part
        reduced[...] = own_part if mask == 0 else reduced[...] + own_part
        lower[...] = part if mask == 0 else lower[...] + part
    own = lifted[pl.ds(pl.multiple_of(block * own_rows, 16), own_rows), :]
    kid_sum[...] = column_sum(own_inverse * own_inverse) + column_sum(own * own)
    lift_high[...] = rounded(lifted[...])
    lower_high[...] = rounded(lower[...])
    reduced[...] = reduced[...] - dot(factor_halves[0], lift_high[...])


def border_kernel(border, first, second, border_high, border_lower):
    border_high[...] = rounded(border[...])
    for kid, lower_high in enumerate((first, second)):
        for span in spans(lower_high.shape[1]):
            border_lower[kid, :, span] = dot(border_high[...], lower_high[:, span])


def image_kernel(pieces, *refs):
    factor = unpacked(pieces, refs)
    border_high, border_lower, weights, diag_high, diag_low, parent_sum, *kids, out, factor_high, fold_high, fold_low = (
        refs[2 * pieces - 2 :]
    )
    _, block = place_of()
    own_border, size = refs[0].shape
    for mask, pair in enumerate(factor):
        start = pl.multiple_of((block ^ mask) * own_border, 16)

        def put(ref, start=start):
            factor_high[pl.ds(start, own_border), :] = rounded(ref[...])

        if mask < 2:
            put(pair[0])
        else:
            store(pair, put)
    for span in spans(size):
        fold_high[:, span], fold_low[:, span] = halves(dot(border_high[...], factor_high[:, span]))
    fold = fold_high[...], fold_low[...]
    for span in spans(size):
        image = product(fold, (diag_high[:, span], diag_low[:, span]))
        out[:, span] = parent_sum[:, span] + column_sum(weights[:, span] * image)
    for kid, (reduced, lift_high, kid_sum) in enumerate((kids[:3], kids[3:])):
        kid_size = reduced.shape[1]
        for span in spans(kid_size):
            image = border_lower[kid, :, span] - dot(fold[0], lift_high[:, span])
            target = size + kid * kid_size + span.start
            out[:, target : target + COLS] = kid_sum[:, span] + column_sum(reduced[:, span] * image)


def finish_kernel(parent_ref, *refs):
    partials, (parent_out, kid_out) = refs[:-2], refs[-2:]
    leaf = lax.axis_index("leaf")
    size, kid_size = parent_out.shape[1], kid_out.shape[1]
    half = len(partials) // 2
    sums = [functools.reduce(jnp.add, [ref[...] for ref in group]) for group in (partials[:half], partials[half:])]
    owner, _ = place_of()
    parent_out[...] = jnp.where(owner == leaf, sums[0][:, :size], sums[1][:, :size])
    for parent, total in ((owner, sums[0]), (owner ^ 1, sums[1])):
        _, ids = kids_of(parent_ref, parent)
        for place in range(2):
            for kid in range(2):

                @pl.when(ids[place] == 2 * leaf + kid)
                def _(total=total, place=place, kid=kid):
                    start = size + place * kid_size
                    kid_out[kid : kid + 1] = total[:, start : start + kid_size]


def call(kernel, out_shape, limit, scalars=0, loose=0, keep=True, scratch=(), moved=1_000):
    def run(*args):
        specs = [pl.BlockSpec(memory_space=pltpu.SMEM if at < scalars else pltpu.VMEM) for at in range(len(args))]
        args = [
            pltpu.with_memory_space_constraint(value, pltpu.HBM if at < loose else pltpu.VMEM)
            for at, value in enumerate(args)
        ]
        results = out_shape
        if keep:
            results = jax.tree.map(lambda leaf: pltpu.VMEM(leaf.shape, leaf.dtype), results)
        return pl.pallas_call(
            kernel,
            out_shape=results,
            in_specs=specs,
            out_specs=jax.tree.map(lambda _: pl.BlockSpec(memory_space=pltpu.VMEM), out_shape),
            scratch_shapes=scratch,
            compiler_params=pltpu.CompilerParams(vmem_limit_bytes=limit * MIB),
            cost_estimate=pl.CostEstimate(flops=0, bytes_accessed=moved, transcendentals=0),
        )(*args)

    return run


def shards(border, factor, diagonal, kid_rows, kid_inverse, child_index, child_parent):
    border, factor, diagonal = border[0], factor[0], diagonal[0]
    pieces = lax.axis_size("front")
    size, kid_size, border_size = diagonal.shape[1], kid_rows.shape[2], border.shape[1]
    own_border = border.shape[0]
    kid_block = kid_rows.shape[1]
    half = jnp.bfloat16

    def over_fronts(value, parity=None):
        parts = {0: value}
        bit = 2
        while bit < pieces:
            for mask in list(parts):
                parts[mask | bit] = exchange(parts[mask], 0, bit, parity)
            bit *= 2
        return parts

    def shared(parts, gate_own, gate_rest):
        others = {mask | 1: exchange(after(part, *(gate_rest if mask else gate_own)), 1, 0) for mask, part in parts.items()}
        parts = parts | others
        return [parts[mask] for mask in range(pieces)]

    def gathered(own, keep, swap, gate_own, gate_keep, gate_swap):
        result = [own, exchange(after(own, *gate_own), 1, 0)]
        for mask in list(keep)[1:]:
            far_swap = exchange(after(keep[mask], *gate_keep), 1, 0, 0)
            far_keep = exchange(after(swap[mask], *gate_swap), 1, 0, 1)
            result += [keep[mask], swap[mask], far_keep, far_swap]
        return result

    last = pieces - 2
    keep_diagonal = over_fronts(diagonal, 0)
    keep_factor = over_fronts(factor, 0)
    own_diagonal = cross(diagonal)
    kid_shape = (kid_block + kid_inverse.shape[1], kid_size)
    first, second, index = call(
        select_kernel,
        (shape_of(kid_shape), shape_of(kid_shape), shape_of((2, pieces, kid_block), jnp.int32)),
        6,
        scalars=1,
        loose=4,
    )(child_parent, child_index, kid_rows, kid_inverse, exchange(kid_rows, 1, 0), exchange(kid_inverse, 1, 0))
    first = cross(after(first, own_diagonal, keep_diagonal[last]))
    swap_diagonal = over_fronts(own_diagonal, 1)
    second = cross(after(second, first, swap_diagonal[last], keep_factor[last]))
    own_factor = cross(after(factor, second))

    first_parts = over_fronts(after(first, swap_diagonal[last]))
    diagonal_parts = gathered(own_diagonal, keep_diagonal, swap_diagonal, [first], [first], [])
    diag_high, diag_low, pick_high, pick_low, parent_sum = call(
        functools.partial(diagonal_kernel, pieces),
        (
            shape_of((size, size), half),
            shape_of((size, size), half),
            shape_of((2, pieces, size, kid_block), half),
            shape_of((2, pieces, size, kid_block), half),
            shape_of((1, size)),
        ),
        10,
    )(index, *diagonal_parts)
    own_border_rows = cross(after(border, own_factor, pick_high))
    second_parts = over_fronts(second)
    first_parts = shared(first_parts, [], [])

    kid_outs = (
        shape_of((own_border, kid_size)),
        shape_of((size, kid_size), half),
        shape_of((border_size, kid_size), half),
        shape_of((1, kid_size)),
    )
    kid_scratch = [
        pltpu.VMEM((kid_size, kid_size), half),
        pltpu.VMEM((kid_size, kid_size), half),
        pltpu.VMEM((size, kid_size), jnp.float32),
        pltpu.VMEM((border_size, kid_size), jnp.float32),
    ]
    common = (index, pick_high, pick_low, own_factor, diag_high, diag_low)
    first_reduced, first_lift, first_lower, first_sum, weights = call(
        functools.partial(kid_kernel, pieces, 0), kid_outs + (shape_of((own_border, size)),), 14, scratch=kid_scratch
    )(*common, *first_parts)
    swap_factor = over_fronts(after(own_factor, second_parts[last], first_lift), 1)
    second_parts = shared(second_parts, [first_lift], [first_lift])
    second_reduced, second_lift, second_lower, second_sum = call(
        functools.partial(kid_kernel, pieces, 1), kid_outs, 14, scratch=kid_scratch
    )(*common, *second_parts)

    border_high, border_lower = call(
        border_kernel, (shape_of(border.shape, half), shape_of((2, own_border, kid_size))), 8
    )(own_border_rows, first_lower, second_lower)

    factor_parts = gathered(own_factor, keep_factor, swap_factor, [pick_high], [second], [border_lower])
    total = call(
        functools.partial(image_kernel, pieces),
        shape_of((1, size + 2 * kid_size)),
        12,
        scratch=[
            pltpu.VMEM((border_size, size), half),
            pltpu.VMEM((own_border, size), half),
            pltpu.VMEM((own_border, size), half),
        ],
    )(
        *factor_parts,
        border_high,
        border_lower,
        weights,
        diag_high,
        diag_low,
        parent_sum,
        first_reduced,
        first_lift,
        first_sum,
        second_reduced,
        second_lift,
        second_sum,
    )

    total = total + exchange(total, 1, 0)
    bit = 4
    while bit < pieces:
        total = total + exchange(total, 0, bit)
        bit *= 2
    near = range(min(pieces, 4))
    order = [mask for parity in (0, 1) for mask in near if mask % 2 == parity]
    partials = [exchange(total, 0, mask) if mask else total for mask in order]
    return call(finish_kernel, (shape_of((1, size)), shape_of((2, kid_size))), 2, scalars=1, loose=1, keep=False)(
        child_parent, *partials
    )


def solution(mesh):
    whole = P("leaf", "front", None)
    return jax.shard_map(
        shards,
        mesh=mesh,
        in_specs=(whole,) * 5 + (P(), P()),
        out_specs=(P("leaf", None), P("leaf", None)),
        check_vma=False,
    )
```

```python
import functools

import jax
import jax.numpy as jnp
from jax import lax
from jax.experimental import pallas as pl
from jax.experimental.pallas import tpu as pltpu
from jax.sharding import PartitionSpec as P

MIB = 1024 * 1024
COLS = 256


def shape_of(shape, dtype=jnp.float32):
    return jax.ShapeDtypeStruct(shape, dtype)


def exchange(value, leaf_mask, front_mask, parity=None):
    fronts = lax.axis_size("front")
    pairs = [
        (leaf * fronts + front, (leaf ^ leaf_mask) * fronts + (front ^ front_mask))
        for leaf in range(lax.axis_size("leaf"))
        for front in range(fronts)
        if parity is None or (leaf ^ front) & 1 == parity
    ]
    return lax.ppermute(value, ("leaf", "front"), pairs)


def cross(value):
    fronts = lax.axis_size("front")
    pairs = []
    for leaf in range(lax.axis_size("leaf")):
        for front in range(fronts):
            flip = (leaf ^ front) & 1
            pairs.append((leaf * fronts + front, (leaf ^ flip) * fronts + (front ^ flip)))
    return lax.ppermute(value, ("leaf", "front"), pairs)


def after(value, *others):
    return lax.optimization_barrier((value, *others))[0]


def kids_of(parent_ref, owner):
    partner = owner ^ 1
    pool = [2 * owner, 2 * owner + 1, 2 * partner, 2 * partner + 1]
    member = [parent_ref[kid] == owner for kid in pool]
    first = jnp.where(member[0], 0, jnp.where(member[1], 1, 2))
    second = jnp.where(member[3], 3, jnp.where(member[2], 2, 1))
    ids = [2 * jnp.where(slot < 2, owner, partner) + (slot & 1) for slot in (first, second)]
    return (first, second), ids


def place_of():
    front, leaf = lax.axis_index("front"), lax.axis_index("leaf")
    owner = (leaf & -2) | (front & 1)
    block = (front & -2) | (leaf & 1)
    return owner, block


def keeps():
    return ((lax.axis_index("leaf") ^ lax.axis_index("front")) & 1) == 0


def store(pair, action):
    for ref, chosen in zip(pair, (keeps(), jnp.logical_not(keeps()))):
        pl.when(chosen)(functools.partial(action, ref))


def rounded(value):
    return value.astype(jnp.bfloat16)


def halves(value):
    high = rounded(value)
    return high, rounded(value - high.astype(jnp.float32))


def dot(left, right):
    return jnp.dot(left, right, preferred_element_type=jnp.float32)


def product(left, right):
    (left_high, left_low), (right_high, right_low) = left, right
    return dot(left_high, right_high) + (dot(left_high, right_low) + dot(left_low, right_high))


def column_sum(value):
    return jnp.sum(value, axis=0, keepdims=True)


def spans(width):
    return [slice(start, start + COLS) for start in range(0, width, COLS)]


def pack(out, diagonal, inverses):
    rows, size = diagonal.shape
    block, kid_size = inverses[0].shape
    left, half = size - kid_size, block // 2
    out[:rows] = diagonal[...]
    out[rows : rows + block, :kid_size] = inverses[0][...]
    out[rows : rows + block, kid_size:] = inverses[1][:, :left]
    out[rows + block :, : kid_size - left] = inverses[1][:half, left:]
    out[rows + block :, kid_size - left : 2 * (kid_size - left)] = inverses[1][half:, left:]


def select_kernel(parent_ref, index_ref, diagonal, own_rows, own_inverse, other_rows, other_inverse, *refs):
    packed, rows_out, index_out, first, second = refs
    leaf = lax.axis_index("leaf")
    slots, _ = kids_of(parent_ref, leaf)
    for place, slot in enumerate(slots):
        for source in range(4):
            rows, inverse = (own_rows, own_inverse) if source < 2 else (other_rows, other_inverse)

            @pl.when(slot == source)
            def _(rows=rows, inverse=inverse, place=place, source=source):
                rows_out[place] = rows[source % 2]
                (first, second)[place][...] = inverse[source % 2]

    packed[...] = jnp.zeros(packed.shape, jnp.float32)
    pack(packed, diagonal, (first, second))
    owner, block = place_of()
    _, ids = kids_of(parent_ref, owner)
    pieces, width = index_out.shape[1:]
    for place, kid in enumerate(ids):
        row = index_ref[pl.ds(kid, 1), :]
        parts = [row[:, start : start + width] for start in range(0, pieces * width, width)]
        for mask in range(pieces):
            part = parts[0]
            for at in range(1, pieces):
                part = jnp.where((block ^ mask) == at, parts[at], part)
            index_out[place, mask : mask + 1, :] = part


def picks(index, first, rows):
    position = lax.broadcasted_iota(jnp.int32, (rows, index.shape[1]), 0) + first
    return rounded(jnp.where(position == index, 1.0, 0.0))


def unpacked(pieces, refs):
    pairs = [(refs[0], refs[0]), (refs[1], refs[1])]
    for at in range(2, 2 * pieces - 2, 4):
        near_keep, near_swap, far_keep, far_swap = refs[at : at + 4]
        pairs += [(near_keep, near_swap), (far_keep, far_swap)]
    return pairs


def diagonal_kernel(pieces, index, factor, *refs):
    packed = refs[:pieces]
    diag_high, diag_low, pick_high, pick_low, inv_high, inv_low, weights, parent_sum, kid_sum = refs[pieces:]
    _, block = place_of()
    size, kid_size = diag_high.shape[0], inv_high.shape[1]
    rows, inv_block = size // pieces, kid_size // pieces
    left, half = size - kid_size, inv_block // 2
    for mask in range(pieces):
        piece = packed[mask]
        values = piece[:rows, :]
        first = piece[rows : rows + inv_block, :kid_size]
        second_left = piece[rows : rows + inv_block, kid_size:]
        second_top = piece[rows + inv_block :, : kid_size - left]
        second_bottom = piece[rows + inv_block :, kid_size - left : 2 * (kid_size - left)]
        if mask == 0:
            parent_sum[...] = column_sum(values * values)
            kid_sum[:1] = column_sum(first * first)
            kid_sum[1:, :left] = column_sum(second_left * second_left)
            kid_sum[1:, left:] = column_sum(second_top * second_top) + column_sum(second_bottom * second_bottom)
        start = pl.multiple_of((block ^ mask) * rows, 16)
        diag_high[pl.ds(start, rows), :], diag_low[pl.ds(start, rows), :] = halves(values)
        start = pl.multiple_of((block ^ mask) * inv_block, 16)
        below = pl.multiple_of(start + half, 16)
        for kid, first_row, lanes, value in (
            (0, start, slice(0, kid_size), first),
            (1, start, slice(0, left), second_left),
            (1, start, slice(left, kid_size), second_top),
            (1, below, slice(left, kid_size), second_bottom),
        ):
            span = pl.ds(first_row, value.shape[0])
            inv_high[kid, span, lanes], inv_low[kid, span, lanes] = halves(value)
    for kid in range(2):
        for mask in range(pieces):
            pick = picks(index[kid, mask : mask + 1, :], 0, size)
            pick_high[kid, mask] = rounded(dot(diag_high[...], pick))
            pick_low[kid, mask] = rounded(dot(diag_low[...], pick))
    factor_halves = halves(factor[...])
    for span in spans(size):
        weights[:, span] = product(factor_halves, (diag_high[:, span], diag_low[:, span]))


def fold(kid, mask, rows, inverse, index, pick_high, pick_low, own_border, border_size):
    _, block = place_of()
    size = pick_high.shape[2]
    weight = halves(product(halves(rows), inverse))
    lifted = product((pick_high[kid, mask], pick_low[kid, mask]), weight)
    places = index[kid, mask : mask + 1, :]
    pick = picks(places, size + block * own_border, own_border)
    own_lower = dot(pick, weight[0]) + dot(pick, weight[1])
    lower = dot(picks(places, size, border_size), weight[0])
    return lifted, own_lower, rounded(lower)


def early_kernel(index, pick_high, pick_low, inv_high, inv_low, own_rows, core_rows, lifted, own_lower, lower):
    for kid in range(2):
        inverse = inv_high[kid], inv_low[kid]
        for mask, rows in enumerate((own_rows, core_rows)):
            parts = fold(
                kid, mask, rows[kid], inverse, index, pick_high, pick_low, own_lower.shape[1], lower.shape[1]
            )
            for ref, part in zip((lifted, own_lower, lower), parts):
                ref[kid] = part if mask == 0 else ref[kid] + part


def late_kernel(pieces, index, pick_high, pick_low, inv_high, inv_low, factor, early_lifted, early_own, early_lower, *refs):
    kid_rows = refs[: 2 * pieces - 4]
    kid_in, reduced, lift_high, lower_high, kid_sum, rows, lifted = refs[2 * pieces - 4 :]
    _, block = place_of()
    size = lifted.shape[0]
    own_rows = size // pieces
    factor_high = rounded(factor[...])
    for mask, pair in enumerate(unpacked(pieces, (None, None) + kid_rows)):
        if mask < 2:
            continue

        def put(ref, mask=mask):
            rows[mask - 2] = ref[...]

        store(pair, put)
    for kid in range(2):
        inverse = inv_high[kid], inv_low[kid]
        for mask in range(2, pieces):
            parts = fold(
                kid, mask, rows[mask - 2, kid], inverse, index, pick_high, pick_low, reduced.shape[1], lower_high.shape[1]
            )
            first = mask == 2
            lifted[...] = (early_lifted[kid] if first else lifted[...]) + parts[0]
            reduced[kid] = (early_own[kid] if first else reduced[kid]) + parts[1]
            lower_high[kid] = (early_lower[kid] if first else lower_high[kid]) + parts[2]
        own = lifted[pl.ds(pl.multiple_of(block * own_rows, 16), own_rows), :]
        kid_sum[kid : kid + 1] = kid_in[kid : kid + 1] + column_sum(own * own)
        lift_high[kid] = rounded(lifted[...])
        reduced[kid] = reduced[kid] - dot(factor_high, lift_high[kid])


def border_kernel(border, lower_high, border_high, border_lower):
    border_high[...] = rounded(border[...])
    for kid in range(2):
        for span in spans(lower_high.shape[2]):
            border_lower[kid, :, span] = dot(border_high[...], lower_high[kid, :, span])


def image_kernel(pieces, *refs):
    factor = unpacked(pieces, refs)
    border_high, border_lower, weights, diag_high, diag_low, parent_sum, reduced, lift_high, kid_sum = refs[
        2 * pieces - 2 : 2 * pieces + 7
    ]
    out, factor_high, fold_high, fold_low = refs[2 * pieces + 7 :]
    _, block = place_of()
    own_border, size = refs[0].shape
    for mask, pair in enumerate(factor):
        start = pl.multiple_of((block ^ mask) * own_border, 16)

        def put(ref, start=start):
            factor_high[pl.ds(start, own_border), :] = rounded(ref[...])

        if mask < 2:
            put(pair[0])
        else:
            store(pair, put)
    for span in spans(size):
        fold_high[:, span], fold_low[:, span] = halves(dot(border_high[...], factor_high[:, span]))
    folded = fold_high[...], fold_low[...]
    for span in spans(size):
        image = product(folded, (diag_high[:, span], diag_low[:, span]))
        out[:, span] = parent_sum[:, span] + column_sum(weights[:, span] * image)
    kid_size = reduced.shape[2]
    for kid in range(2):
        for span in spans(kid_size):
            image = border_lower[kid, :, span] - dot(folded[0], lift_high[kid, :, span])
            target = size + kid * kid_size + span.start
            out[:, target : target + COLS] = kid_sum[kid : kid + 1, span] + column_sum(reduced[kid, :, span] * image)


def finish_kernel(parent_ref, *refs):
    partials, (parent_out, kid_out) = refs[:-2], refs[-2:]
    leaf = lax.axis_index("leaf")
    size, kid_size = parent_out.shape[1], kid_out.shape[1]
    half = len(partials) // 2
    sums = [functools.reduce(jnp.add, [ref[...] for ref in group]) for group in (partials[:half], partials[half:])]
    owner, _ = place_of()
    parent_out[...] = jnp.where(owner == leaf, sums[0][:, :size], sums[1][:, :size])
    for parent, total in ((owner, sums[0]), (owner ^ 1, sums[1])):
        _, ids = kids_of(parent_ref, parent)
        for place in range(2):
            for kid in range(2):

                @pl.when(ids[place] == 2 * leaf + kid)
                def _(total=total, place=place, kid=kid):
                    start = size + place * kid_size
                    kid_out[kid : kid + 1] = total[:, start : start + kid_size]


def call(kernel, out_shape, limit, scalars=0, loose=0, keep=True, scratch=(), moved=1_000):
    def run(*args):
        specs = [pl.BlockSpec(memory_space=pltpu.SMEM if at < scalars else pltpu.VMEM) for at in range(len(args))]
        args = [
            pltpu.with_memory_space_constraint(value, pltpu.HBM if at < loose else pltpu.VMEM)
            for at, value in enumerate(args)
        ]
        results = out_shape
        if keep:
            results = jax.tree.map(lambda leaf: pltpu.VMEM(leaf.shape, leaf.dtype), results)
        return pl.pallas_call(
            kernel,
            out_shape=results,
            in_specs=specs,
            out_specs=jax.tree.map(lambda _: pl.BlockSpec(memory_space=pltpu.VMEM), out_shape),
            scratch_shapes=scratch,
            compiler_params=pltpu.CompilerParams(vmem_limit_bytes=limit * MIB),
            cost_estimate=pl.CostEstimate(flops=0, bytes_accessed=moved, transcendentals=0),
        )(*args)

    return run


def shards(border, factor, diagonal, kid_rows, kid_inverse, child_index, child_parent):
    border, factor, diagonal = border[0], factor[0], diagonal[0]
    pieces = lax.axis_size("front")
    size, kid_size, border_size = diagonal.shape[1], kid_rows.shape[2], border.shape[1]
    own_border = border.shape[0]
    kid_block = kid_rows.shape[1]
    half = jnp.bfloat16

    def over_fronts(value, parity=None):
        parts = {0: value}
        bit = 2
        while bit < pieces:
            for mask in list(parts):
                parts[mask | bit] = exchange(parts[mask], 0, bit, parity)
            bit *= 2
        return parts

    def gathered(own, keep, swap, gate_own, gate_keep, gate_swap):
        result = [own, exchange(after(own, *gate_own), 1, 0)]
        for mask in list(keep)[1:]:
            far_swap = exchange(after(keep[mask], *gate_keep), 1, 0, 0)
            far_keep = exchange(after(swap[mask], *gate_swap), 1, 0, 1)
            result += [keep[mask], swap[mask], far_keep, far_swap]
        return result

    last = pieces - 2
    inv_block = kid_inverse.shape[1]
    keep_factor = over_fronts(factor, 0)
    own_factor = cross(factor)
    packed, kid_rows, index = call(
        select_kernel,
        (
            shape_of((diagonal.shape[0] + inv_block + inv_block // 2, size)),
            shape_of(kid_rows.shape),
            shape_of((2, pieces, kid_block), jnp.int32),
        ),
        10,
        scalars=1,
        loose=5,
        scratch=[pltpu.VMEM(kid_inverse.shape[1:], jnp.float32)] * 2,
    )(child_parent, child_index, diagonal, kid_rows, kid_inverse, exchange(kid_rows, 1, 0), exchange(kid_inverse, 1, 0))
    packed = cross(after(packed, keep_factor[last]))
    own_kids = cross(after(kid_rows, own_factor))
    packed_parts = over_fronts(packed)
    keep_kids = over_fronts(own_kids, 0)
    swap_kids = over_fronts(own_kids, 1)
    own_border_rows = cross(after(border, own_kids, packed_parts[last], keep_kids[last]))
    near, far = list(packed_parts.items())[0], list(packed_parts.items())[1:]
    packed_parts[1] = exchange(after(near[1], own_kids), 1, 0)
    for mask, part in far:
        packed_parts[mask | 1] = exchange(part, 1, 0)
    kids_core = exchange(after(own_kids, packed_parts[last]), 1, 0)

    diag_high, diag_low, pick_high, pick_low, inv_high, inv_low, weights, parent_sum, inv_sum = call(
        functools.partial(diagonal_kernel, pieces),
        (
            shape_of((size, size), half),
            shape_of((size, size), half),
            shape_of((2, pieces, size, kid_block), half),
            shape_of((2, pieces, size, kid_block), half),
            shape_of((2, kid_size, kid_size), half),
            shape_of((2, kid_size, kid_size), half),
            shape_of((own_border, size)),
            shape_of((1, size)),
            shape_of((2, kid_size)),
        ),
        10,
    )(index, own_factor, *[packed_parts[mask] for mask in range(pieces)])
    common = (index, pick_high, pick_low, inv_high, inv_low)
    early = call(
        early_kernel,
        (
            shape_of((2, size, kid_size)),
            shape_of((2, own_border, kid_size)),
            shape_of((2, border_size, kid_size), half),
        ),
        14,
    )(*common, own_kids, kids_core)

    kid_parts = []
    for mask in list(keep_kids)[1:]:
        far_swap = exchange(after(keep_kids[mask], early[0]), 1, 0, 0)
        far_keep = exchange(after(swap_kids[mask], early[0]), 1, 0, 1)
        kid_parts += [keep_kids[mask], swap_kids[mask], far_keep, far_swap]
    swap_factor = over_fronts(after(own_factor, swap_kids[last], early[0]), 1)
    reduced, lift_high, lower_high, kid_sum = call(
        functools.partial(late_kernel, pieces),
        (
            shape_of((2, own_border, kid_size)),
            shape_of((2, size, kid_size), half),
            shape_of((2, border_size, kid_size), half),
            shape_of((2, kid_size)),
        ),
        14,
        scratch=[
            pltpu.VMEM((pieces - 2, *kid_rows.shape), jnp.float32),
            pltpu.VMEM((size, kid_size), jnp.float32),
        ],
    )(*common, own_factor, *early, *kid_parts, inv_sum)

    border_high, border_lower = call(
        border_kernel, (shape_of(border.shape, half), shape_of((2, own_border, kid_size))), 8
    )(own_border_rows, lower_high)

    factor_parts = gathered(own_factor, keep_factor, swap_factor, [own_kids], [own_kids], [border_lower])
    total = call(
        functools.partial(image_kernel, pieces),
        shape_of((1, size + 2 * kid_size)),
        12,
        scratch=[
            pltpu.VMEM((border_size, size), half),
            pltpu.VMEM((own_border, size), half),
            pltpu.VMEM((own_border, size), half),
        ],
    )(*factor_parts, border_high, border_lower, weights, diag_high, diag_low, parent_sum, reduced, lift_high, kid_sum)

    total = total + exchange(total, 1, 0)
    bit = 4
    while bit < pieces:
        total = total + exchange(total, 0, bit)
        bit *= 2
    near = range(min(pieces, 4))
    order = [mask for parity in (0, 1) for mask in near if mask % 2 == parity]
    partials = [exchange(total, 0, mask) if mask else total for mask in order]
    return call(finish_kernel, (shape_of((1, size)), shape_of((2, kid_size))), 2, scalars=1, loose=1, keep=False)(
        child_parent, *partials
    )


def solution(mesh):
    whole = P("leaf", "front", None)
    return jax.shard_map(
        shards,
        mesh=mesh,
        in_specs=(whole,) * 5 + (P(), P()),
        out_specs=(P("leaf", None), P("leaf", None)),
        check_vma=False,
    )
```

```python
import functools

import jax
import jax.numpy as jnp
from jax import lax
from jax.experimental import pallas as pl
from jax.experimental.pallas import tpu as pltpu
from jax.sharding import PartitionSpec as P

MIB = 1024 * 1024
COLS = 256


def shape_of(shape, dtype=jnp.float32):
    return jax.ShapeDtypeStruct(shape, dtype)


def exchange(value, leaf_mask, front_mask, parity=None):
    fronts = lax.axis_size("front")
    pairs = [
        (leaf * fronts + front, (leaf ^ leaf_mask) * fronts + (front ^ front_mask))
        for leaf in range(lax.axis_size("leaf"))
        for front in range(fronts)
        if parity is None or (leaf ^ front) & 1 == parity
    ]
    return lax.ppermute(value, ("leaf", "front"), pairs)


def cross(value):
    fronts = lax.axis_size("front")
    pairs = []
    for leaf in range(lax.axis_size("leaf")):
        for front in range(fronts):
            flip = (leaf ^ front) & 1
            pairs.append((leaf * fronts + front, (leaf ^ flip) * fronts + (front ^ flip)))
    return lax.ppermute(value, ("leaf", "front"), pairs)


def after(value, *others):
    return lax.optimization_barrier((value, *others))[0]


def kids_of(parent_ref, owner):
    partner = owner ^ 1
    pool = [2 * owner, 2 * owner + 1, 2 * partner, 2 * partner + 1]
    member = [parent_ref[kid] == owner for kid in pool]
    first = jnp.where(member[0], 0, jnp.where(member[1], 1, 2))
    second = jnp.where(member[3], 3, jnp.where(member[2], 2, 1))
    ids = [2 * jnp.where(slot < 2, owner, partner) + (slot & 1) for slot in (first, second)]
    return (first, second), ids


def place_of():
    front, leaf = lax.axis_index("front"), lax.axis_index("leaf")
    owner = (leaf & -2) | (front & 1)
    block = (front & -2) | (leaf & 1)
    return owner, block


def keeps():
    return ((lax.axis_index("leaf") ^ lax.axis_index("front")) & 1) == 0


def store(pair, action):
    for ref, chosen in zip(pair, (keeps(), jnp.logical_not(keeps()))):
        pl.when(chosen)(functools.partial(action, ref))


def rounded(value):
    return value.astype(jnp.bfloat16)


def halves(value):
    high = rounded(value)
    return high, rounded(value - high.astype(jnp.float32))


def dot(left, right):
    return jnp.dot(left, right, preferred_element_type=jnp.float32)


def product(left, right):
    (left_high, left_low), (right_high, right_low) = left, right
    return dot(left_high, right_high) + (dot(left_high, right_low) + dot(left_low, right_high))


def column_sum(value):
    return jnp.sum(value, axis=0, keepdims=True)


def spans(width):
    return [slice(start, start + COLS) for start in range(0, width, COLS)]


def select_kernel(parent_ref, index_ref, own_rows, own_inverse, other_rows, other_inverse, kid_out, index_out):
    leaf = lax.axis_index("leaf")
    slots, _ = kids_of(parent_ref, leaf)
    split = own_rows.shape[1]
    for place, slot in enumerate(slots):
        for source in range(4):
            rows, inverse = (own_rows, own_inverse) if source < 2 else (other_rows, other_inverse)

            @pl.when(slot == source)
            def _(rows=rows, inverse=inverse, place=place, source=source):
                kid_out[place, :split] = rows[source % 2]
                kid_out[place, split:] = inverse[source % 2]

    owner, block = place_of()
    _, ids = kids_of(parent_ref, owner)
    pieces, width = index_out.shape[1:]
    for place, kid in enumerate(ids):
        row = index_ref[pl.ds(kid, 1), :]
        parts = [row[:, start : start + width] for start in range(0, pieces * width, width)]
        for mask in range(pieces):
            part = parts[0]
            for at in range(1, pieces):
                part = jnp.where((block ^ mask) == at, parts[at], part)
            index_out[place, mask : mask + 1, :] = part


def picks(index, first, rows):
    position = lax.broadcasted_iota(jnp.int32, (rows, index.shape[1]), 0) + first
    return rounded(jnp.where(position == index, 1.0, 0.0))


def unpacked(pieces, refs):
    pairs = [(refs[0], refs[0]), (refs[1], refs[1])]
    for at in range(2, 2 * pieces - 2, 4):
        near_keep, near_swap, far_keep, far_swap = refs[at : at + 4]
        pairs += [(near_keep, near_swap), (far_keep, far_swap)]
    return pairs


def diagonal_kernel(pieces, index, *refs):
    diagonal = unpacked(pieces, refs)
    diag_high, diag_low, pick_high, pick_low, parent_sum = refs[2 * pieces - 2 :]
    _, block = place_of()
    own_rows, size = refs[0].shape
    parent_sum[...] = column_sum(refs[0][...] * refs[0][...])
    for mask, pair in enumerate(diagonal):
        start = pl.multiple_of((block ^ mask) * own_rows, 16)

        def put(ref, start=start):
            diag_high[pl.ds(start, own_rows), :], diag_low[pl.ds(start, own_rows), :] = halves(ref[...])

        if mask < 2:
            put(pair[0])
        else:
            store(pair, put)
    for kid in range(2):
        for mask in range(pieces):
            pick = picks(index[kid, mask : mask + 1, :], 0, size)
            pick_high[kid, mask] = rounded(dot(diag_high[...], pick))
            pick_low[kid, mask] = rounded(dot(diag_low[...], pick))


def kid_kernel(pieces, index, pick_high, pick_low, factor, diag_high, diag_low, *refs):
    kids = refs[:pieces]
    reduced, lift_high, lower_high, weights, kid_sum, inv_high, inv_low, lifted, lower = refs[pieces:]
    _, block = place_of()
    size, own_border, border_size = lifted.shape[0], factor.shape[0], lower.shape[0]
    kid_block = index.shape[2]
    inv_block, own_rows = kids[0].shape[1] - kid_block, size // pieces
    factor_halves = halves(factor[...])
    for span in spans(size):
        weights[:, span] = product(factor_halves, (diag_high[:, span], diag_low[:, span]))
    for kid in range(2):
        own_inverse = kids[0][kid, kid_block:]
        for mask in range(pieces):
            start = pl.multiple_of((block ^ mask) * inv_block, 16)
            high, low = halves(kids[mask][kid, kid_block:])
            inv_high[pl.ds(start, inv_block), :] = high
            inv_low[pl.ds(start, inv_block), :] = low
        inverse = inv_high[...], inv_low[...]
        for mask in range(pieces):
            weight = halves(product(halves(kids[mask][kid, :kid_block]), inverse))
            lifted_part = product((pick_high[kid, mask], pick_low[kid, mask]), weight)
            pick = picks(index[kid, mask : mask + 1, :], size + block * own_border, own_border)
            lower_part = dot(pick, weight[0]) + dot(pick, weight[1])
            lifted[...] = lifted_part if mask == 0 else lifted[...] + lifted_part
            reduced[kid] = lower_part if mask == 0 else reduced[kid] + lower_part
            part = dot(picks(index[kid, mask : mask + 1, :], size, border_size), weight[0])
            lower[...] = part if mask == 0 else lower[...] + part
        own = lifted[pl.ds(pl.multiple_of(block * own_rows, 16), own_rows), :]
        kid_sum[kid : kid + 1] = column_sum(own_inverse * own_inverse) + column_sum(own * own)
        lift_high[kid] = rounded(lifted[...])
        lower_high[kid] = rounded(lower[...])
        reduced[kid] = reduced[kid] - dot(factor_halves[0], lift_high[kid])


def border_kernel(border, lower_high, border_high, border_lower):
    border_high[...] = rounded(border[...])
    for kid in range(2):
        for span in spans(lower_high.shape[2]):
            border_lower[kid, :, span] = dot(border_high[...], lower_high[kid, :, span])


def image_kernel(pieces, *refs):
    factor = refs[:pieces]
    border_high, border_lower, weights, reduced, lift_high, diag_high, diag_low, parent_sum, kid_sum, out = refs[
        pieces : pieces + 10
    ]
    factor_high, fold_high, fold_low = refs[pieces + 10 :]
    _, block = place_of()
    own_border, size = factor[0].shape
    kid_size = reduced.shape[2]
    for mask in range(pieces):
        start = pl.multiple_of((block ^ mask) * own_border, 16)
        factor_high[pl.ds(start, own_border), :] = rounded(factor[mask][...])
    for span in spans(size):
        fold_high[:, span], fold_low[:, span] = halves(dot(border_high[...], factor_high[:, span]))
    fold = fold_high[...], fold_low[...]
    for span in spans(size):
        image = product(fold, (diag_high[:, span], diag_low[:, span]))
        out[:, span] = parent_sum[:, span] + column_sum(weights[:, span] * image)
    for kid in range(2):
        for span in spans(kid_size):
            image = border_lower[kid, :, span] - dot(fold[0], lift_high[kid, :, span])
            target = size + kid * kid_size + span.start
            out[:, target : target + COLS] = kid_sum[kid : kid + 1, span] + column_sum(reduced[kid, :, span] * image)


def finish_kernel(parent_ref, *refs):
    partials, (parent_out, kid_out) = refs[:-2], refs[-2:]
    leaf = lax.axis_index("leaf")
    size, kid_size = parent_out.shape[1], kid_out.shape[1]
    half = len(partials) // 2
    sums = [functools.reduce(jnp.add, [ref[...] for ref in group]) for group in (partials[:half], partials[half:])]
    owner, _ = place_of()
    parent_out[...] = jnp.where(owner == leaf, sums[0][:, :size], sums[1][:, :size])
    for parent, total in ((owner, sums[0]), (owner ^ 1, sums[1])):
        _, ids = kids_of(parent_ref, parent)
        for place in range(2):
            for kid in range(2):

                @pl.when(ids[place] == 2 * leaf + kid)
                def _(total=total, place=place, kid=kid):
                    start = size + place * kid_size
                    kid_out[kid : kid + 1] = total[:, start : start + kid_size]


def call(kernel, out_shape, limit, scalars=0, loose=0, keep=True, scratch=(), moved=1_000):
    def run(*args):
        specs = [pl.BlockSpec(memory_space=pltpu.SMEM if at < scalars else pltpu.VMEM) for at in range(len(args))]
        args = [
            pltpu.with_memory_space_constraint(value, pltpu.HBM if at < loose else pltpu.VMEM)
            for at, value in enumerate(args)
        ]
        results = out_shape
        if keep:
            results = jax.tree.map(lambda leaf: pltpu.VMEM(leaf.shape, leaf.dtype), results)
        return pl.pallas_call(
            kernel,
            out_shape=results,
            in_specs=specs,
            out_specs=jax.tree.map(lambda _: pl.BlockSpec(memory_space=pltpu.VMEM), out_shape),
            scratch_shapes=scratch,
            compiler_params=pltpu.CompilerParams(vmem_limit_bytes=limit * MIB),
            cost_estimate=pl.CostEstimate(flops=0, bytes_accessed=moved, transcendentals=0),
        )(*args)

    return run


def shards(border, factor, diagonal, kid_rows, kid_inverse, child_index, child_parent):
    border, factor, diagonal = border[0], factor[0], diagonal[0]
    pieces = lax.axis_size("front")
    size, kid_size, border_size = diagonal.shape[1], kid_rows.shape[2], border.shape[1]
    own_border = border.shape[0]
    kid_block = kid_rows.shape[1]
    half = jnp.bfloat16

    def over_fronts(value, parity=None):
        parts = {0: value}
        bit = 2
        while bit < pieces:
            for mask in list(parts):
                parts[mask | bit] = exchange(parts[mask], 0, bit, parity)
            bit *= 2
        return parts

    def spread(parts, gate_own, gate_rest):
        others = {mask | 1: exchange(after(part, *(gate_rest if mask else gate_own)), 1, 0) for mask, part in parts.items()}
        parts = parts | others
        return [parts[mask] for mask in range(pieces)]

    last = pieces - 2
    keep_diagonal = over_fronts(diagonal, 0)
    own_diagonal = cross(diagonal)
    kid_shape = (2, kid_block + kid_inverse.shape[1], kid_size)
    own_kids, index = call(
        select_kernel, (shape_of(kid_shape), shape_of((2, pieces, kid_block), jnp.int32)), 6, scalars=1, loose=4
    )(child_parent, child_index, kid_rows, kid_inverse, exchange(kid_rows, 1, 0), exchange(kid_inverse, 1, 0))
    own_kids = cross(after(own_kids, own_diagonal, keep_diagonal[last]))
    swap_diagonal = over_fronts(own_diagonal, 1)
    own_factor = cross(after(factor, own_kids))
    kid_parts = over_fronts(after(own_kids, swap_diagonal[last]))

    diagonal_parts = [own_diagonal, exchange(after(own_diagonal, own_kids), 1, 0)]
    for mask in list(keep_diagonal)[1:]:
        far_swap = exchange(after(keep_diagonal[mask], own_kids), 1, 0, 0)
        far_keep = exchange(after(swap_diagonal[mask], own_kids), 1, 0, 1)
        diagonal_parts += [keep_diagonal[mask], swap_diagonal[mask], far_keep, far_swap]

    diag_high, diag_low, pick_high, pick_low, parent_sum = call(
        functools.partial(diagonal_kernel, pieces),
        (
            shape_of((size, size), half),
            shape_of((size, size), half),
            shape_of((2, pieces, size, kid_block), half),
            shape_of((2, pieces, size, kid_block), half),
            shape_of((1, size)),
        ),
        10,
    )(index, *diagonal_parts)
    own_border_rows = cross(after(border, own_factor, pick_high))
    kids_here = kid_parts[last]
    factor_parts = over_fronts(after(own_factor, kids_here))
    factor_parts[0] = own_factor
    kid_parts = spread(kid_parts, [own_kids], [pick_high])

    reduced, lift_high, lower_high, weights, kid_sum = call(
        functools.partial(kid_kernel, pieces),
        (
            shape_of((2, own_border, kid_size)),
            shape_of((2, size, kid_size), half),
            shape_of((2, border_size, kid_size), half),
            shape_of((own_border, size)),
            shape_of((2, kid_size)),
        ),
        20,
        scratch=[
            pltpu.VMEM((kid_size, kid_size), half),
            pltpu.VMEM((kid_size, kid_size), half),
            pltpu.VMEM((size, kid_size), jnp.float32),
            pltpu.VMEM((border_size, kid_size), jnp.float32),
        ],
    )(index, pick_high, pick_low, own_factor, diag_high, diag_low, *kid_parts)

    border_high, border_lower = call(
        border_kernel, (shape_of(border.shape, half), shape_of((2, own_border, kid_size))), 8
    )(own_border_rows, lower_high)

    factor_parts = spread(factor_parts, [kids_here], [border_lower])
    total = call(
        functools.partial(image_kernel, pieces),
        shape_of((1, size + 2 * kid_size)),
        12,
        scratch=[
            pltpu.VMEM((border_size, size), half),
            pltpu.VMEM((own_border, size), half),
            pltpu.VMEM((own_border, size), half),
        ],
    )(
        *factor_parts,
        border_high,
        border_lower,
        weights,
        reduced,
        lift_high,
        diag_high,
        diag_low,
        parent_sum,
        kid_sum,
    )

    total = total + exchange(total, 1, 0)
    bit = 4
    while bit < pieces:
        total = total + exchange(total, 0, bit)
        bit *= 2
    near = range(min(pieces, 4))
    order = [mask for parity in (0, 1) for mask in near if mask % 2 == parity]
    partials = [exchange(total, 0, mask) if mask else total for mask in order]
    return call(finish_kernel, (shape_of((1, size)), shape_of((2, kid_size))), 2, scalars=1, loose=1, keep=False)(
        child_parent, *partials
    )


def solution(mesh):
    whole = P("leaf", "front", None)
    return jax.shard_map(
        shards,
        mesh=mesh,
        in_specs=(whole,) * 5 + (P(), P()),
        out_specs=(P("leaf", None), P("leaf", None)),
        check_vma=False,
    )
```

```python
import functools

import jax
import jax.numpy as jnp
from jax import lax
from jax.experimental import pallas as pl
from jax.experimental.pallas import tpu as pltpu
from jax.sharding import PartitionSpec as P

MIB = 1024 * 1024
COLS = 256


def shape_of(shape, dtype=jnp.float32):
    return jax.ShapeDtypeStruct(shape, dtype)


def exchange(value, leaf_mask, front_mask):
    fronts = lax.axis_size("front")
    pairs = [
        (leaf * fronts + front, (leaf ^ leaf_mask) * fronts + (front ^ front_mask))
        for leaf in range(lax.axis_size("leaf"))
        for front in range(fronts)
    ]
    return lax.ppermute(value, ("leaf", "front"), pairs)


def cross(value):
    fronts = lax.axis_size("front")
    pairs = []
    for leaf in range(lax.axis_size("leaf")):
        for front in range(fronts):
            flip = (leaf ^ front) & 1
            pairs.append((leaf * fronts + front, (leaf ^ flip) * fronts + (front ^ flip)))
    return lax.ppermute(value, ("leaf", "front"), pairs)


def after(value, *others):
    return lax.optimization_barrier((value, *others))[0]


def kids_of(parent_ref, owner):
    partner = owner ^ 1
    pool = [2 * owner, 2 * owner + 1, 2 * partner, 2 * partner + 1]
    member = [parent_ref[kid] == owner for kid in pool]
    first = jnp.where(member[0], 0, jnp.where(member[1], 1, 2))
    second = jnp.where(member[3], 3, jnp.where(member[2], 2, 1))
    ids = [2 * jnp.where(slot < 2, owner, partner) + (slot & 1) for slot in (first, second)]
    return (first, second), ids


def place_of():
    front, leaf = lax.axis_index("front"), lax.axis_index("leaf")
    owner = (leaf & -2) | (front & 1)
    block = (front & -2) | (leaf & 1)
    return owner, block


def rounded(value):
    return value.astype(jnp.bfloat16)


def halves(value):
    high = rounded(value)
    return high, rounded(value - high.astype(jnp.float32))


def dot(left, right):
    return jnp.dot(left, right, preferred_element_type=jnp.float32)


def product(left, right):
    (left_high, left_low), (right_high, right_low) = left, right
    return dot(left_high, right_high) + (dot(left_high, right_low) + dot(left_low, right_high))


def column_sum(value):
    return jnp.sum(value, axis=0, keepdims=True)


def spans(width):
    return [slice(start, start + COLS) for start in range(0, width, COLS)]


def select_kernel(parent_ref, index_ref, own_rows, own_inverse, other_rows, other_inverse, kid_out, index_out):
    leaf = lax.axis_index("leaf")
    slots, _ = kids_of(parent_ref, leaf)
    split = own_rows.shape[1]
    for place, slot in enumerate(slots):
        for source in range(4):
            rows, inverse = (own_rows, own_inverse) if source < 2 else (other_rows, other_inverse)

            @pl.when(slot == source)
            def _(rows=rows, inverse=inverse, place=place, source=source):
                kid_out[place, :split] = rows[source % 2]
                kid_out[place, split:] = inverse[source % 2]

    owner, block = place_of()
    _, ids = kids_of(parent_ref, owner)
    pieces, width = index_out.shape[1:]
    for place, kid in enumerate(ids):
        row = index_ref[pl.ds(kid, 1), :]
        parts = [row[:, start : start + width] for start in range(0, pieces * width, width)]
        for mask in range(pieces):
            part = parts[0]
            for at in range(1, pieces):
                part = jnp.where((block ^ mask) == at, parts[at], part)
            index_out[place, mask : mask + 1, :] = part


def picks(index, first, rows):
    position = lax.broadcasted_iota(jnp.int32, (rows, index.shape[1]), 0) + first
    return rounded(jnp.where(position == index, 1.0, 0.0))


def diagonal_kernel(pieces, index, factor, *refs):
    diagonal = refs[:pieces]
    diag_high, diag_low, pick_high, pick_low, weights, parent_sum = refs[pieces:]
    _, block = place_of()
    own_rows, size = diagonal[0].shape
    parent_sum[...] = column_sum(diagonal[0][...] * diagonal[0][...])
    for mask in range(pieces):
        start = pl.multiple_of((block ^ mask) * own_rows, 16)
        high, low = halves(diagonal[mask][...])
        diag_high[pl.ds(start, own_rows), :] = high
        diag_low[pl.ds(start, own_rows), :] = low
    for kid in range(2):
        for mask in range(pieces):
            pick = picks(index[kid, mask : mask + 1, :], 0, size)
            pick_high[kid, mask] = rounded(dot(diag_high[...], pick))
            pick_low[kid, mask] = rounded(dot(diag_low[...], pick))
    factor_halves = halves(factor[...])
    for span in spans(size):
        weights[:, span] = product(factor_halves, (diag_high[:, span], diag_low[:, span]))


def kid_kernel(pieces, index, pick_high, pick_low, factor, *refs):
    kids = refs[:pieces]
    reduced, lift_high, lower_high, kid_sum, inv_high, inv_low, lifted, lower = refs[pieces:]
    _, block = place_of()
    size, own_border, border_size = lifted.shape[0], factor.shape[0], lower.shape[0]
    kid_block = index.shape[2]
    inv_block, own_rows = kids[0].shape[1] - kid_block, size // pieces
    factor_high = rounded(factor[...])
    for kid in range(2):
        own_inverse = kids[0][kid, kid_block:]
        for mask in range(pieces):
            start = pl.multiple_of((block ^ mask) * inv_block, 16)
            high, low = halves(kids[mask][kid, kid_block:])
            inv_high[pl.ds(start, inv_block), :] = high
            inv_low[pl.ds(start, inv_block), :] = low
        inverse = inv_high[...], inv_low[...]
        for mask in range(pieces):
            weight = halves(product(halves(kids[mask][kid, :kid_block]), inverse))
            lifted_part = product((pick_high[kid, mask], pick_low[kid, mask]), weight)
            pick = picks(index[kid, mask : mask + 1, :], size + block * own_border, own_border)
            lower_part = dot(pick, weight[0]) + dot(pick, weight[1])
            lifted[...] = lifted_part if mask == 0 else lifted[...] + lifted_part
            reduced[kid] = lower_part if mask == 0 else reduced[kid] + lower_part
            part = dot(picks(index[kid, mask : mask + 1, :], size, border_size), weight[0])
            lower[...] = part if mask == 0 else lower[...] + part
        own = lifted[pl.ds(pl.multiple_of(block * own_rows, 16), own_rows), :]
        kid_sum[kid : kid + 1] = column_sum(own_inverse * own_inverse) + column_sum(own * own)
        lift_high[kid] = rounded(lifted[...])
        lower_high[kid] = rounded(lower[...])
        reduced[kid] = reduced[kid] - dot(factor_high, lift_high[kid])


def border_kernel(border, lower_high, border_high, border_lower):
    border_high[...] = rounded(border[...])
    for kid in range(2):
        for span in spans(lower_high.shape[2]):
            border_lower[kid, :, span] = dot(border_high[...], lower_high[kid, :, span])


def image_kernel(pieces, *refs):
    factor = refs[:pieces]
    border_high, border_lower, weights, reduced, lift_high, diag_high, diag_low, parent_sum, kid_sum, out = refs[
        pieces : pieces + 10
    ]
    factor_high, fold_high, fold_low = refs[pieces + 10 :]
    _, block = place_of()
    own_border, size = factor[0].shape
    kid_size = reduced.shape[2]
    for mask in range(pieces):
        start = pl.multiple_of((block ^ mask) * own_border, 16)
        factor_high[pl.ds(start, own_border), :] = rounded(factor[mask][...])
    for span in spans(size):
        fold_high[:, span], fold_low[:, span] = halves(dot(border_high[...], factor_high[:, span]))
    fold = fold_high[...], fold_low[...]
    for span in spans(size):
        image = product(fold, (diag_high[:, span], diag_low[:, span]))
        out[:, span] = parent_sum[:, span] + column_sum(weights[:, span] * image)
    for kid in range(2):
        for span in spans(kid_size):
            image = border_lower[kid, :, span] - dot(fold[0], lift_high[kid, :, span])
            target = size + kid * kid_size + span.start
            out[:, target : target + COLS] = kid_sum[kid : kid + 1, span] + column_sum(reduced[kid, :, span] * image)


def finish_kernel(parent_ref, *refs):
    partials, (parent_out, kid_out) = refs[:-2], refs[-2:]
    leaf = lax.axis_index("leaf")
    size, kid_size = parent_out.shape[1], kid_out.shape[1]
    half = len(partials) // 2
    sums = [functools.reduce(jnp.add, [ref[...] for ref in group]) for group in (partials[:half], partials[half:])]
    owner, _ = place_of()
    parent_out[...] = jnp.where(owner == leaf, sums[0][:, :size], sums[1][:, :size])
    for parent, total in ((owner, sums[0]), (owner ^ 1, sums[1])):
        _, ids = kids_of(parent_ref, parent)
        for place in range(2):
            for kid in range(2):

                @pl.when(ids[place] == 2 * leaf + kid)
                def _(total=total, place=place, kid=kid):
                    start = size + place * kid_size
                    kid_out[kid : kid + 1] = total[:, start : start + kid_size]


def call(kernel, out_shape, limit, scalars=0, loose=0, keep=True, scratch=(), moved=1_000):
    def run(*args):
        specs = [pl.BlockSpec(memory_space=pltpu.SMEM if at < scalars else pltpu.VMEM) for at in range(len(args))]
        args = [
            pltpu.with_memory_space_constraint(value, pltpu.HBM if at < loose else pltpu.VMEM)
            for at, value in enumerate(args)
        ]
        results = out_shape
        if keep:
            results = jax.tree.map(lambda leaf: pltpu.VMEM(leaf.shape, leaf.dtype), results)
        return pl.pallas_call(
            kernel,
            out_shape=results,
            in_specs=specs,
            out_specs=jax.tree.map(lambda _: pl.BlockSpec(memory_space=pltpu.VMEM), out_shape),
            scratch_shapes=scratch,
            compiler_params=pltpu.CompilerParams(vmem_limit_bytes=limit * MIB),
            cost_estimate=pl.CostEstimate(flops=0, bytes_accessed=moved, transcendentals=0),
        )(*args)

    return run


def shards(border, factor, diagonal, kid_rows, kid_inverse, child_index, child_parent):
    border, factor, diagonal = border[0], factor[0], diagonal[0]
    pieces = lax.axis_size("front")
    size, kid_size, border_size = diagonal.shape[1], kid_rows.shape[2], border.shape[1]
    own_border = border.shape[0]
    kid_block = kid_rows.shape[1]
    half = jnp.bfloat16

    def over_fronts(value):
        parts = {0: value}
        bit = 2
        while bit < pieces:
            for mask in list(parts):
                parts[mask | bit] = exchange(parts[mask], 0, bit)
            bit *= 2
        return parts

    def spread(parts, gate_own, gate_rest):
        others = {mask | 1: exchange(after(part, *(gate_rest if mask else gate_own)), 1, 0) for mask, part in parts.items()}
        parts = parts | others
        return [parts[mask] for mask in range(pieces)]

    last = pieces - 2
    kid_shape = (2, kid_block + kid_inverse.shape[1], kid_size)
    own_kids, index = call(
        select_kernel, (shape_of(kid_shape), shape_of((2, pieces, kid_block), jnp.int32)), 6, scalars=1, loose=4
    )(child_parent, child_index, kid_rows, kid_inverse, exchange(kid_rows, 1, 0), exchange(kid_inverse, 1, 0))
    own_kids = cross(own_kids)
    kid_parts = over_fronts(own_kids)
    own_diagonal = cross(diagonal)
    own_factor = cross(after(factor, own_diagonal))
    diagonal_parts = over_fronts(own_diagonal)
    diagonal_here = diagonal_parts[last]
    diagonal_parts = spread(diagonal_parts, [own_factor], [])

    diag_high, diag_low, pick_high, pick_low, weights, parent_sum = call(
        functools.partial(diagonal_kernel, pieces),
        (
            shape_of((size, size), half),
            shape_of((size, size), half),
            shape_of((2, pieces, size, kid_block), half),
            shape_of((2, pieces, size, kid_block), half),
            shape_of((own_border, size)),
            shape_of((1, size)),
        ),
        10,
    )(index, own_factor, *diagonal_parts)
    own_border_rows = cross(after(border, own_factor, diagonal_here))
    kids_here = kid_parts[last]
    factor_parts = over_fronts(after(own_factor, kids_here))
    factor_parts[0] = own_factor
    kid_parts = spread(kid_parts, [own_factor], [pick_high])

    reduced, lift_high, lower_high, kid_sum = call(
        functools.partial(kid_kernel, pieces),
        (
            shape_of((2, own_border, kid_size)),
            shape_of((2, size, kid_size), half),
            shape_of((2, border_size, kid_size), half),
            shape_of((2, kid_size)),
        ),
        20,
        scratch=[
            pltpu.VMEM((kid_size, kid_size), half),
            pltpu.VMEM((kid_size, kid_size), half),
            pltpu.VMEM((size, kid_size), jnp.float32),
            pltpu.VMEM((border_size, kid_size), jnp.float32),
        ],
    )(index, pick_high, pick_low, own_factor, *kid_parts)

    border_high, border_lower = call(
        border_kernel, (shape_of(border.shape, half), shape_of((2, own_border, kid_size))), 8
    )(own_border_rows, lower_high)

    factor_parts = spread(factor_parts, [kids_here], [border_lower])
    total = call(
        functools.partial(image_kernel, pieces),
        shape_of((1, size + 2 * kid_size)),
        12,
        scratch=[
            pltpu.VMEM((border_size, size), half),
            pltpu.VMEM((own_border, size), half),
            pltpu.VMEM((own_border, size), half),
        ],
    )(
        *factor_parts,
        border_high,
        border_lower,
        weights,
        reduced,
        lift_high,
        diag_high,
        diag_low,
        parent_sum,
        kid_sum,
    )

    total = total + exchange(total, 1, 0)
    bit = 4
    while bit < pieces:
        total = total + exchange(total, 0, bit)
        bit *= 2
    near = range(min(pieces, 4))
    order = [mask for parity in (0, 1) for mask in near if mask % 2 == parity]
    partials = [exchange(total, 0, mask) if mask else total for mask in order]
    return call(finish_kernel, (shape_of((1, size)), shape_of((2, kid_size))), 2, scalars=1, loose=1, keep=False)(
        child_parent, *partials
    )


def solution(mesh):
    whole = P("leaf", "front", None)
    return jax.shard_map(
        shards,
        mesh=mesh,
        in_specs=(whole,) * 5 + (P(), P()),
        out_specs=(P("leaf", None), P("leaf", None)),
        check_vma=False,
    )
```

```python
import functools

import jax
import jax.numpy as jnp
from jax import lax
from jax.experimental import pallas as pl
from jax.experimental.pallas import tpu as pltpu
from jax.sharding import PartitionSpec as P

MIB = 1024 * 1024
COLS = 256


def shape_of(shape, dtype=jnp.float32):
    return jax.ShapeDtypeStruct(shape, dtype)


def exchange(value, leaf_mask, front_mask, parity=None):
    fronts = lax.axis_size("front")
    pairs = [
        (leaf * fronts + front, (leaf ^ leaf_mask) * fronts + (front ^ front_mask))
        for leaf in range(lax.axis_size("leaf"))
        for front in range(fronts)
        if parity is None or (leaf ^ front) & 1 == parity
    ]
    return lax.ppermute(value, ("leaf", "front"), pairs)


def cross(value):
    fronts = lax.axis_size("front")
    pairs = []
    for leaf in range(lax.axis_size("leaf")):
        for front in range(fronts):
            flip = (leaf ^ front) & 1
            pairs.append((leaf * fronts + front, (leaf ^ flip) * fronts + (front ^ flip)))
    return lax.ppermute(value, ("leaf", "front"), pairs)


def after(value, *others):
    return lax.optimization_barrier((value, *others))[0]


def kids_of(parent_ref, owner):
    partner = owner ^ 1
    pool = [2 * owner, 2 * owner + 1, 2 * partner, 2 * partner + 1]
    member = [parent_ref[kid] == owner for kid in pool]
    first = jnp.where(member[0], 0, jnp.where(member[1], 1, 2))
    second = jnp.where(member[3], 3, jnp.where(member[2], 2, 1))
    ids = [2 * jnp.where(slot < 2, owner, partner) + (slot & 1) for slot in (first, second)]
    return (first, second), ids


def place_of():
    front, leaf = lax.axis_index("front"), lax.axis_index("leaf")
    owner = (leaf & -2) | (front & 1)
    block = (front & -2) | (leaf & 1)
    return owner, block


def keeps():
    return ((lax.axis_index("leaf") ^ lax.axis_index("front")) & 1) == 0


def store(pair, action):
    for ref, chosen in zip(pair, (keeps(), jnp.logical_not(keeps()))):
        pl.when(chosen)(functools.partial(action, ref))


def rounded(value):
    return value.astype(jnp.bfloat16)


def halves(value):
    high = rounded(value)
    return high, rounded(value - high.astype(jnp.float32))


def dot(left, right):
    return jnp.dot(left, right, preferred_element_type=jnp.float32)


def product(left, right):
    (left_high, left_low), (right_high, right_low) = left, right
    return dot(left_high, right_high) + (dot(left_high, right_low) + dot(left_low, right_high))


def column_sum(value):
    return jnp.sum(value, axis=0, keepdims=True)


def spans(width):
    return [slice(start, start + COLS) for start in range(0, width, COLS)]


def select_kernel(parent_ref, index_ref, own_rows, own_inverse, other_rows, other_inverse, kid_out, index_out):
    leaf = lax.axis_index("leaf")
    slots, _ = kids_of(parent_ref, leaf)
    split = own_rows.shape[1]
    for place, slot in enumerate(slots):
        for source in range(4):
            rows, inverse = (own_rows, own_inverse) if source < 2 else (other_rows, other_inverse)

            @pl.when(slot == source)
            def _(rows=rows, inverse=inverse, place=place, source=source):
                kid_out[place, :split] = rows[source % 2]
                kid_out[place, split:] = inverse[source % 2]

    owner, block = place_of()
    _, ids = kids_of(parent_ref, owner)
    pieces, width = index_out.shape[1:]
    for place, kid in enumerate(ids):
        row = index_ref[pl.ds(kid, 1), :]
        parts = [row[:, start : start + width] for start in range(0, pieces * width, width)]
        for mask in range(pieces):
            part = parts[0]
            for at in range(1, pieces):
                part = jnp.where((block ^ mask) == at, parts[at], part)
            index_out[place, mask : mask + 1, :] = part


def picks(index, first, rows):
    position = lax.broadcasted_iota(jnp.int32, (rows, index.shape[1]), 0) + first
    return rounded(jnp.where(position == index, 1.0, 0.0))


def unpacked(pieces, refs):
    pairs = [(refs[0], refs[0]), (refs[1], refs[1])]
    for at in range(2, 2 * pieces - 2, 4):
        near_keep, near_swap, far_keep, far_swap = refs[at : at + 4]
        pairs += [(near_keep, near_swap), (far_keep, far_swap)]
    return pairs


def diagonal_kernel(pieces, index, factor, *refs):
    diagonal = refs[:pieces]
    diag_high, diag_low, pick_high, pick_low, weights, parent_sum = refs[pieces:]
    _, block = place_of()
    own_rows, size = diagonal[0].shape
    parent_sum[...] = column_sum(diagonal[0][...] * diagonal[0][...])
    for mask in range(pieces):
        start = pl.multiple_of((block ^ mask) * own_rows, 16)
        high, low = halves(diagonal[mask][...])
        diag_high[pl.ds(start, own_rows), :] = high
        diag_low[pl.ds(start, own_rows), :] = low
    for kid in range(2):
        for mask in range(pieces):
            pick = picks(index[kid, mask : mask + 1, :], 0, size)
            pick_high[kid, mask] = rounded(dot(diag_high[...], pick))
            pick_low[kid, mask] = rounded(dot(diag_low[...], pick))
    factor_halves = halves(factor[...])
    for span in spans(size):
        weights[:, span] = product(factor_halves, (diag_high[:, span], diag_low[:, span]))


def kid_kernel(pieces, index, pick_high, pick_low, factor, *refs):
    kids = refs[:pieces]
    reduced, lift_high, lower_high, kid_sum, inv_high, inv_low, lifted, lower = refs[pieces:]
    _, block = place_of()
    size, own_border, border_size = lifted.shape[0], factor.shape[0], lower.shape[0]
    kid_block = index.shape[2]
    inv_block, own_rows = kids[0].shape[1] - kid_block, size // pieces
    factor_high = rounded(factor[...])
    for kid in range(2):
        own_inverse = kids[0][kid, kid_block:]
        for mask in range(pieces):
            start = pl.multiple_of((block ^ mask) * inv_block, 16)
            high, low = halves(kids[mask][kid, kid_block:])
            inv_high[pl.ds(start, inv_block), :] = high
            inv_low[pl.ds(start, inv_block), :] = low
        inverse = inv_high[...], inv_low[...]
        for mask in range(pieces):
            high, low = halves(product(halves(kids[mask][kid, :kid_block]), inverse))
            lifted_part = dot(pick_high[kid, mask], high) + dot(pick_low[kid, mask], high)
            places = index[kid, mask : mask + 1, :]
            low_part = dot(picks(places, size + block * own_border, own_border), low)
            part = dot(picks(places, size, border_size), high)
            lifted[...] = lifted_part if mask == 0 else lifted[...] + lifted_part
            reduced[kid] = low_part if mask == 0 else reduced[kid] + low_part
            lower[...] = part if mask == 0 else lower[...] + part
        own = lifted[pl.ds(pl.multiple_of(block * own_rows, 16), own_rows), :]
        kid_sum[kid : kid + 1] = column_sum(own_inverse * own_inverse) + column_sum(own * own)
        lift_high[kid] = rounded(lifted[...])
        lower_high[kid] = rounded(lower[...])
        own_lower = lower[pl.ds(pl.multiple_of(block * own_border, 8), own_border), :]
        reduced[kid] = own_lower + reduced[kid] - dot(factor_high, lift_high[kid])


def border_kernel(border, lower_high, border_high, border_lower):
    border_high[...] = rounded(border[...])
    for kid in range(2):
        for span in spans(lower_high.shape[2]):
            border_lower[kid, :, span] = dot(border_high[...], lower_high[kid, :, span])


def image_kernel(pieces, *refs):
    factor = unpacked(pieces, refs)
    border_high, border_lower, weights, reduced, lift_high, diag_high, diag_low, parent_sum, kid_sum, out = refs[
        2 * pieces - 2 : 2 * pieces + 8
    ]
    factor_high, fold_high, fold_low = refs[2 * pieces + 8 :]
    _, block = place_of()
    own_border, size = refs[0].shape
    kid_size = reduced.shape[2]
    for mask, pair in enumerate(factor):
        start = pl.multiple_of((block ^ mask) * own_border, 16)

        def put(ref, start=start):
            factor_high[pl.ds(start, own_border), :] = rounded(ref[...])

        if mask < 2:
            put(pair[0])
        else:
            store(pair, put)
    for span in spans(size):
        fold_high[:, span], fold_low[:, span] = halves(dot(border_high[...], factor_high[:, span]))
    fold = fold_high[...], fold_low[...]
    for span in spans(size):
        image = product(fold, (diag_high[:, span], diag_low[:, span]))
        out[:, span] = parent_sum[:, span] + column_sum(weights[:, span] * image)
    for kid in range(2):
        for span in spans(kid_size):
            image = border_lower[kid, :, span] - dot(fold[0], lift_high[kid, :, span])
            target = size + kid * kid_size + span.start
            out[:, target : target + COLS] = kid_sum[kid : kid + 1, span] + column_sum(reduced[kid, :, span] * image)


def finish_kernel(parent_ref, *refs):
    partials, (parent_out, kid_out) = refs[:-2], refs[-2:]
    leaf = lax.axis_index("leaf")
    size, kid_size = parent_out.shape[1], kid_out.shape[1]
    half = len(partials) // 2
    sums = [functools.reduce(jnp.add, [ref[...] for ref in group]) for group in (partials[:half], partials[half:])]
    owner, _ = place_of()
    parent_out[...] = jnp.where(owner == leaf, sums[0][:, :size], sums[1][:, :size])
    for parent, total in ((owner, sums[0]), (owner ^ 1, sums[1])):
        _, ids = kids_of(parent_ref, parent)
        for place in range(2):
            for kid in range(2):

                @pl.when(ids[place] == 2 * leaf + kid)
                def _(total=total, place=place, kid=kid):
                    start = size + place * kid_size
                    kid_out[kid : kid + 1] = total[:, start : start + kid_size]


def call(kernel, out_shape, limit, scalars=0, loose=0, keep=True, scratch=(), moved=1_000):
    def run(*args):
        specs = [pl.BlockSpec(memory_space=pltpu.SMEM if at < scalars else pltpu.VMEM) for at in range(len(args))]
        args = [
            pltpu.with_memory_space_constraint(value, pltpu.HBM if at < loose else pltpu.VMEM)
            for at, value in enumerate(args)
        ]
        results = out_shape
        if keep:
            results = jax.tree.map(lambda leaf: pltpu.VMEM(leaf.shape, leaf.dtype), results)
        return pl.pallas_call(
            kernel,
            out_shape=results,
            in_specs=specs,
            out_specs=jax.tree.map(lambda _: pl.BlockSpec(memory_space=pltpu.VMEM), out_shape),
            scratch_shapes=scratch,
            compiler_params=pltpu.CompilerParams(vmem_limit_bytes=limit * MIB),
            cost_estimate=pl.CostEstimate(flops=0, bytes_accessed=moved, transcendentals=0),
        )(*args)

    return run


def shards(border, factor, diagonal, kid_rows, kid_inverse, child_index, child_parent):
    border, factor, diagonal = border[0], factor[0], diagonal[0]
    pieces = lax.axis_size("front")
    size, kid_size, border_size = diagonal.shape[1], kid_rows.shape[2], border.shape[1]
    own_border = border.shape[0]
    kid_block = kid_rows.shape[1]
    half = jnp.bfloat16

    def over_fronts(value, parity=None):
        parts = {0: value}
        bit = 2
        while bit < pieces:
            for mask in list(parts):
                parts[mask | bit] = exchange(parts[mask], 0, bit, parity)
            bit *= 2
        return parts

    def spread(parts, gate_own, gate_rest):
        others = {mask | 1: exchange(after(part, *(gate_rest if mask else gate_own)), 1, 0) for mask, part in parts.items()}
        parts = parts | others
        return [parts[mask] for mask in range(pieces)]

    last = pieces - 2
    keep_factor = over_fronts(factor, 0)
    own_diagonal = cross(diagonal)
    kid_shape = (2, kid_block + kid_inverse.shape[1], kid_size)
    own_kids, index = call(
        select_kernel, (shape_of(kid_shape), shape_of((2, pieces, kid_block), jnp.int32)), 6, scalars=1, loose=4
    )(child_parent, child_index, kid_rows, kid_inverse, exchange(kid_rows, 1, 0), exchange(kid_inverse, 1, 0))
    own_kids = cross(after(own_kids, own_diagonal, keep_factor[last]))
    diagonal_parts = over_fronts(own_diagonal)
    kid_parts = over_fronts(after(own_kids, diagonal_parts[last]))
    own_factor = cross(after(factor, own_diagonal))
    diagonal_parts = spread(diagonal_parts, [own_kids], [own_kids])

    diag_high, diag_low, pick_high, pick_low, weights, parent_sum = call(
        functools.partial(diagonal_kernel, pieces),
        (
            shape_of((size, size), half),
            shape_of((size, size), half),
            shape_of((2, pieces, size, kid_block), half),
            shape_of((2, pieces, size, kid_block), half),
            shape_of((own_border, size)),
            shape_of((1, size)),
        ),
        10,
    )(index, own_factor, *diagonal_parts)
    own_border_rows = cross(after(border, own_kids))
    kids_here = kid_parts[last]
    swap_factor = over_fronts(after(own_factor, kids_here), 1)
    kid_parts = spread(kid_parts, [own_kids], [pick_high])

    reduced, lift_high, lower_high, kid_sum = call(
        functools.partial(kid_kernel, pieces),
        (
            shape_of((2, own_border, kid_size)),
            shape_of((2, size, kid_size), half),
            shape_of((2, border_size, kid_size), half),
            shape_of((2, kid_size)),
        ),
        20,
        scratch=[
            pltpu.VMEM((kid_size, kid_size), half),
            pltpu.VMEM((kid_size, kid_size), half),
            pltpu.VMEM((size, kid_size), jnp.float32),
            pltpu.VMEM((border_size, kid_size), jnp.float32),
        ],
    )(index, pick_high, pick_low, own_factor, *kid_parts)

    border_high, border_lower = call(
        border_kernel, (shape_of(border.shape, half), shape_of((2, own_border, kid_size))), 8
    )(own_border_rows, lower_high)

    factor_parts = [own_factor, exchange(after(own_factor, kids_here), 1, 0)]
    for mask in list(keep_factor)[1:]:
        far_swap = exchange(after(keep_factor[mask], kids_here), 1, 0, 0)
        far_keep = exchange(after(swap_factor[mask], border_lower), 1, 0, 1)
        factor_parts += [keep_factor[mask], swap_factor[mask], far_keep, far_swap]
    total = call(
        functools.partial(image_kernel, pieces),
        shape_of((1, size + 2 * kid_size)),
        12,
        scratch=[
            pltpu.VMEM((border_size, size), half),
            pltpu.VMEM((own_border, size), half),
            pltpu.VMEM((own_border, size), half),
        ],
    )(
        *factor_parts,
        border_high,
        border_lower,
        weights,
        reduced,
        lift_high,
        diag_high,
        diag_low,
        parent_sum,
        kid_sum,
    )

    total = total + exchange(total, 1, 0)
    bit = 4
    while bit < pieces:
        total = total + exchange(total, 0, bit)
        bit *= 2
    near = range(min(pieces, 4))
    order = [mask for parity in (0, 1) for mask in near if mask % 2 == parity]
    partials = [exchange(total, 0, mask) if mask else total for mask in order]
    return call(finish_kernel, (shape_of((1, size)), shape_of((2, kid_size))), 2, scalars=1, loose=1, keep=False)(
        child_parent, *partials
    )


def solution(mesh):
    whole = P("leaf", "front", None)
    return jax.shard_map(
        shards,
        mesh=mesh,
        in_specs=(whole,) * 5 + (P(), P()),
        out_specs=(P("leaf", None), P("leaf", None)),
        check_vma=False,
    )
```

```python
import functools

import jax
import jax.numpy as jnp
from jax import lax
from jax.experimental import pallas as pl
from jax.experimental.pallas import tpu as pltpu
from jax.sharding import PartitionSpec as P

MIB = 1024 * 1024
COLS = 256


def shape_of(shape, dtype=jnp.float32):
    return jax.ShapeDtypeStruct(shape, dtype)


def exchange(value, leaf_mask, front_mask, parity=None):
    fronts = lax.axis_size("front")
    pairs = [
        (leaf * fronts + front, (leaf ^ leaf_mask) * fronts + (front ^ front_mask))
        for leaf in range(lax.axis_size("leaf"))
        for front in range(fronts)
        if parity is None or (leaf ^ front) & 1 == parity
    ]
    return lax.ppermute(value, ("leaf", "front"), pairs)


def cross(value):
    fronts = lax.axis_size("front")
    pairs = []
    for leaf in range(lax.axis_size("leaf")):
        for front in range(fronts):
            flip = (leaf ^ front) & 1
            pairs.append((leaf * fronts + front, (leaf ^ flip) * fronts + (front ^ flip)))
    return lax.ppermute(value, ("leaf", "front"), pairs)


def after(value, *others):
    return lax.optimization_barrier((value, *others))[0]


def kids_of(parent_ref, owner):
    partner = owner ^ 1
    pool = [2 * owner, 2 * owner + 1, 2 * partner, 2 * partner + 1]
    member = [parent_ref[kid] == owner for kid in pool]
    first = jnp.where(member[0], 0, jnp.where(member[1], 1, 2))
    second = jnp.where(member[3], 3, jnp.where(member[2], 2, 1))
    ids = [2 * jnp.where(slot < 2, owner, partner) + (slot & 1) for slot in (first, second)]
    return (first, second), ids


def place_of():
    front, leaf = lax.axis_index("front"), lax.axis_index("leaf")
    owner = (leaf & -2) | (front & 1)
    block = (front & -2) | (leaf & 1)
    return owner, block


def keeps():
    return ((lax.axis_index("leaf") ^ lax.axis_index("front")) & 1) == 0


def store(pair, action):
    for ref, chosen in zip(pair, (keeps(), jnp.logical_not(keeps()))):
        pl.when(chosen)(functools.partial(action, ref))


def rounded(value):
    return value.astype(jnp.bfloat16)


def halves(value):
    high = rounded(value)
    return high, rounded(value - high.astype(jnp.float32))


def dot(left, right):
    return jnp.dot(left, right, preferred_element_type=jnp.float32)


def product(left, right):
    (left_high, left_low), (right_high, right_low) = left, right
    return dot(left_high, right_high) + (dot(left_high, right_low) + dot(left_low, right_high))


def column_sum(value):
    return jnp.sum(value, axis=0, keepdims=True)


def spans(width):
    return [slice(start, start + COLS) for start in range(0, width, COLS)]


def select_kernel(parent_ref, index_ref, own_rows, own_inverse, other_rows, other_inverse, kid_out, index_out):
    leaf = lax.axis_index("leaf")
    slots, _ = kids_of(parent_ref, leaf)
    split = own_rows.shape[1]
    for place, slot in enumerate(slots):
        for source in range(4):
            rows, inverse = (own_rows, own_inverse) if source < 2 else (other_rows, other_inverse)

            @pl.when(slot == source)
            def _(rows=rows, inverse=inverse, place=place, source=source):
                kid_out[place, :split] = rows[source % 2]
                kid_out[place, split:] = inverse[source % 2]

    owner, block = place_of()
    _, ids = kids_of(parent_ref, owner)
    pieces, width = index_out.shape[1:]
    for place, kid in enumerate(ids):
        row = index_ref[pl.ds(kid, 1), :]
        parts = [row[:, start : start + width] for start in range(0, pieces * width, width)]
        for mask in range(pieces):
            part = parts[0]
            for at in range(1, pieces):
                part = jnp.where((block ^ mask) == at, parts[at], part)
            index_out[place, mask : mask + 1, :] = part


def picks(index, first, rows):
    position = lax.broadcasted_iota(jnp.int32, (rows, index.shape[1]), 0) + first
    return rounded(jnp.where(position == index, 1.0, 0.0))


def unpacked(pieces, refs):
    pairs = [(refs[0], refs[0]), (refs[1], refs[1])]
    for at in range(2, 2 * pieces - 2, 4):
        near_keep, near_swap, far_keep, far_swap = refs[at : at + 4]
        pairs += [(near_keep, near_swap), (far_keep, far_swap)]
    return pairs


def kid_kernel(pieces, index, *refs):
    kids = refs[:pieces]
    up_high, lower_high, own_lower, inv_sum, inv_high, inv_low, upper, lower = refs[pieces:]
    _, block = place_of()
    size, border_size, own_border = upper.shape[0], lower.shape[0], own_lower.shape[1]
    kid_block = index.shape[2]
    inv_block = kids[0].shape[1] - kid_block
    for kid in range(2):
        own_inverse = kids[0][kid, kid_block:]
        inv_sum[kid : kid + 1] = column_sum(own_inverse * own_inverse)
        for mask in range(pieces):
            start = pl.multiple_of((block ^ mask) * inv_block, 16)
            high, low = halves(kids[mask][kid, kid_block:])
            inv_high[pl.ds(start, inv_block), :] = high
            inv_low[pl.ds(start, inv_block), :] = low
        inverse = inv_high[...], inv_low[...]
        for mask in range(pieces):
            high, low = halves(product(halves(kids[mask][kid, :kid_block]), inverse))
            places = index[kid, mask : mask + 1, :]
            up_part = dot(picks(places, 0, size), high)
            part = dot(picks(places, size, border_size), high)
            low_part = dot(picks(places, size + block * own_border, own_border), low)
            upper[...] = up_part if mask == 0 else upper[...] + up_part
            lower[...] = part if mask == 0 else lower[...] + part
            own_lower[kid] = low_part if mask == 0 else own_lower[kid] + low_part
        up_high[kid] = rounded(upper[...])
        lower_high[kid] = rounded(lower[...])
        own_lower[kid] = own_lower[kid] + lower[pl.ds(pl.multiple_of(block * own_border, 8), own_border), :]


def lift_kernel(pieces, factor, up_high, own_lower, inv_sum, *refs):
    reduced, lift_high, diag_high, diag_low, weights, parent_sum, kid_sum, lifted = refs[2 * pieces - 2 :]
    _, block = place_of()
    own_rows, size = refs[0].shape
    parent_sum[...] = column_sum(refs[0][...] * refs[0][...])
    for mask, pair in enumerate(unpacked(pieces, refs)):
        start = pl.multiple_of((block ^ mask) * own_rows, 16)

        def put(ref, start=start):
            diag_high[pl.ds(start, own_rows), :], diag_low[pl.ds(start, own_rows), :] = halves(ref[...])

        if mask < 2:
            put(pair[0])
        else:
            store(pair, put)
    factor_halves = halves(factor[...])
    for kid in range(2):
        lifted[...] = dot(diag_high[...], up_high[kid]) + dot(diag_low[...], up_high[kid])
        own = lifted[pl.ds(pl.multiple_of(block * own_rows, 16), own_rows), :]
        kid_sum[kid : kid + 1] = inv_sum[kid : kid + 1] + column_sum(own * own)
        lift_high[kid] = rounded(lifted[...])
        reduced[kid] = own_lower[kid] - dot(factor_halves[0], lift_high[kid])
    for span in spans(size):
        weights[:, span] = product(factor_halves, (diag_high[:, span], diag_low[:, span]))


def border_kernel(top, rest, lower_high, border_high, border_lower):
    start = 0
    for part in (top, rest):
        border_high[start : start + part.shape[0]] = rounded(part[...])
        start += part.shape[0]
    for kid in range(2):
        for span in spans(lower_high.shape[2]):
            border_lower[kid, :, span] = dot(border_high[...], lower_high[kid, :, span])


def image_kernel(pieces, *refs):
    factor = unpacked(pieces, refs)
    border_high, border_lower, weights, reduced, lift_high, diag_high, diag_low, parent_sum, kid_sum, out = refs[
        2 * pieces - 2 : 2 * pieces + 8
    ]
    factor_high, fold_high, fold_low = refs[2 * pieces + 8 :]
    _, block = place_of()
    own_border, size = refs[0].shape
    kid_size = reduced.shape[2]
    for mask, pair in enumerate(factor):
        start = pl.multiple_of((block ^ mask) * own_border, 16)

        def put(ref, start=start):
            factor_high[pl.ds(start, own_border), :] = rounded(ref[...])

        if mask < 2:
            put(pair[0])
        else:
            store(pair, put)
    for span in spans(size):
        fold_high[:, span], fold_low[:, span] = halves(dot(border_high[...], factor_high[:, span]))
    fold = fold_high[...], fold_low[...]
    for span in spans(size):
        image = product(fold, (diag_high[:, span], diag_low[:, span]))
        out[:, span] = parent_sum[:, span] + column_sum(weights[:, span] * image)
    for kid in range(2):
        for span in spans(kid_size):
            image = border_lower[kid, :, span] - dot(fold[0], lift_high[kid, :, span])
            target = size + kid * kid_size + span.start
            out[:, target : target + COLS] = kid_sum[kid : kid + 1, span] + column_sum(reduced[kid, :, span] * image)


def finish_kernel(parent_ref, *refs):
    partials, (parent_out, kid_out) = refs[:-2], refs[-2:]
    leaf = lax.axis_index("leaf")
    size, kid_size = parent_out.shape[1], kid_out.shape[1]
    half = len(partials) // 2
    sums = [functools.reduce(jnp.add, [ref[...] for ref in group]) for group in (partials[:half], partials[half:])]
    owner, _ = place_of()
    parent_out[...] = jnp.where(owner == leaf, sums[0][:, :size], sums[1][:, :size])
    for parent, total in ((owner, sums[0]), (owner ^ 1, sums[1])):
        _, ids = kids_of(parent_ref, parent)
        for place in range(2):
            for kid in range(2):

                @pl.when(ids[place] == 2 * leaf + kid)
                def _(total=total, place=place, kid=kid):
                    start = size + place * kid_size
                    kid_out[kid : kid + 1] = total[:, start : start + kid_size]


def call(kernel, out_shape, limit, scalars=0, loose=0, keep=True, scratch=(), moved=1_000):
    def run(*args):
        specs = [pl.BlockSpec(memory_space=pltpu.SMEM if at < scalars else pltpu.VMEM) for at in range(len(args))]
        args = [
            pltpu.with_memory_space_constraint(value, pltpu.HBM if at < loose else pltpu.VMEM)
            for at, value in enumerate(args)
        ]
        results = out_shape
        if keep:
            results = jax.tree.map(lambda leaf: pltpu.VMEM(leaf.shape, leaf.dtype), results)
        return pl.pallas_call(
            kernel,
            out_shape=results,
            in_specs=specs,
            out_specs=jax.tree.map(lambda _: pl.BlockSpec(memory_space=pltpu.VMEM), out_shape),
            scratch_shapes=scratch,
            compiler_params=pltpu.CompilerParams(vmem_limit_bytes=limit * MIB),
            cost_estimate=pl.CostEstimate(flops=0, bytes_accessed=moved, transcendentals=0),
        )(*args)

    return run


def shards(border, factor, diagonal, kid_rows, kid_inverse, child_index, child_parent):
    border, factor, diagonal = border[0], factor[0], diagonal[0]
    pieces = lax.axis_size("front")
    size, kid_size, border_size = diagonal.shape[1], kid_rows.shape[2], border.shape[1]
    own_border = border.shape[0]
    kid_block = kid_rows.shape[1]
    half = jnp.bfloat16

    def over_fronts(value, parity=None):
        parts = {0: value}
        bit = 2
        while bit < pieces:
            for mask in list(parts):
                parts[mask | bit] = exchange(parts[mask], 0, bit, parity)
            bit *= 2
        return parts

    def spread(parts, gate_own, gate_rest):
        others = {mask | 1: exchange(after(part, *(gate_rest if mask else gate_own)), 1, 0) for mask, part in parts.items()}
        parts = parts | others
        return [parts[mask] for mask in range(pieces)]

    def gathered(own, keep, swap, gate_own, gate_keep, gate_swap):
        result = [own, exchange(after(own, *gate_own), 1, 0)]
        for mask in list(keep)[1:]:
            far_swap = exchange(after(keep[mask], *gate_keep), 1, 0, 0)
            far_keep = exchange(after(swap[mask], *gate_swap), 1, 0, 1)
            result += [keep[mask], swap[mask], far_keep, far_swap]
        return result

    last = pieces - 2
    top = -(-own_border // 48) * 16
    border_top, border_rest = border[:top], border[top:]
    keep_factor = over_fronts(factor, 0)
    kid_shape = (2, kid_block + kid_inverse.shape[1], kid_size)
    own_kids, index = call(
        select_kernel, (shape_of(kid_shape), shape_of((2, pieces, kid_block), jnp.int32)), 6, scalars=1, loose=4
    )(child_parent, child_index, kid_rows, kid_inverse, exchange(kid_rows, 1, 0), exchange(kid_inverse, 1, 0))
    own_kids = cross(own_kids)
    kid_parts = over_fronts(own_kids)
    kids_here = kid_parts[last]
    own_top = cross(after(border_top, own_kids))
    own_diagonal = cross(after(diagonal, own_kids, keep_factor[last]))
    own_factor = cross(after(factor, own_kids))
    own_rest = cross(after(border_rest, own_top))
    keep_diagonal = over_fronts(own_diagonal, 0)
    swap_diagonal = over_fronts(own_diagonal, 1)
    swap_factor = over_fronts(after(own_factor, kids_here), 1)
    kid_parts = spread(kid_parts, [own_diagonal], [keep_diagonal[last], own_factor, own_top])

    up_high, lower_high, own_lower, inv_sum = call(
        functools.partial(kid_kernel, pieces),
        (
            shape_of((2, size, kid_size), half),
            shape_of((2, border_size, kid_size), half),
            shape_of((2, own_border, kid_size)),
            shape_of((2, kid_size)),
        ),
        20,
        scratch=[
            pltpu.VMEM((kid_size, kid_size), half),
            pltpu.VMEM((kid_size, kid_size), half),
            pltpu.VMEM((size, kid_size), jnp.float32),
            pltpu.VMEM((border_size, kid_size), jnp.float32),
        ],
    )(index, *kid_parts)
    diagonal_parts = gathered(own_diagonal, keep_diagonal, swap_diagonal, [up_high], [up_high], [up_high])

    reduced, lift_high, diag_high, diag_low, weights, parent_sum, kid_sum = call(
        functools.partial(lift_kernel, pieces),
        (
            shape_of((2, own_border, kid_size)),
            shape_of((2, size, kid_size), half),
            shape_of((size, size), half),
            shape_of((size, size), half),
            shape_of((own_border, size)),
            shape_of((1, size)),
            shape_of((2, kid_size)),
        ),
        12,
        scratch=[pltpu.VMEM((size, kid_size), jnp.float32)],
    )(own_factor, up_high, own_lower, inv_sum, *diagonal_parts)

    border_high, border_lower = call(
        border_kernel, (shape_of(border.shape, half), shape_of((2, own_border, kid_size))), 8
    )(own_top, own_rest, lower_high)

    factor_parts = gathered(own_factor, keep_factor, swap_factor, [kids_here], [kids_here], [lift_high, own_rest])
    total = call(
        functools.partial(image_kernel, pieces),
        shape_of((1, size + 2 * kid_size)),
        12,
        scratch=[
            pltpu.VMEM((border_size, size), half),
            pltpu.VMEM((own_border, size), half),
            pltpu.VMEM((own_border, size), half),
        ],
    )(
        *factor_parts,
        border_high,
        border_lower,
        weights,
        reduced,
        lift_high,
        diag_high,
        diag_low,
        parent_sum,
        kid_sum,
    )

    total = total + exchange(total, 1, 0)
    bit = 4
    while bit < pieces:
        total = total + exchange(total, 0, bit)
        bit *= 2
    near = range(min(pieces, 4))
    order = [mask for parity in (0, 1) for mask in near if mask % 2 == parity]
    partials = [exchange(total, 0, mask) if mask else total for mask in order]
    return call(finish_kernel, (shape_of((1, size)), shape_of((2, kid_size))), 2, scalars=1, loose=1, keep=False)(
        child_parent, *partials
    )


def solution(mesh):
    whole = P("leaf", "front", None)
    return jax.shard_map(
        shards,
        mesh=mesh,
        in_specs=(whole,) * 5 + (P(), P()),
        out_specs=(P("leaf", None), P("leaf", None)),
        check_vma=False,
    )
```

```python
import functools

import jax
import jax.numpy as jnp
from jax import lax
from jax.experimental import pallas as pl
from jax.experimental.pallas import tpu as pltpu
from jax.sharding import PartitionSpec as P

MIB = 1024 * 1024
COLS = 256


def shape_of(shape, dtype=jnp.float32):
    return jax.ShapeDtypeStruct(shape, dtype)


def exchange(value, leaf_mask, front_mask, parity=None):
    fronts = lax.axis_size("front")
    pairs = [
        (leaf * fronts + front, (leaf ^ leaf_mask) * fronts + (front ^ front_mask))
        for leaf in range(lax.axis_size("leaf"))
        for front in range(fronts)
        if parity is None or (leaf ^ front) & 1 == parity
    ]
    return lax.ppermute(value, ("leaf", "front"), pairs)


def cross(value):
    fronts = lax.axis_size("front")
    pairs = []
    for leaf in range(lax.axis_size("leaf")):
        for front in range(fronts):
            flip = (leaf ^ front) & 1
            pairs.append((leaf * fronts + front, (leaf ^ flip) * fronts + (front ^ flip)))
    return lax.ppermute(value, ("leaf", "front"), pairs)


def after(value, *others):
    return lax.optimization_barrier((value, *others))[0]


def kids_of(parent_ref, owner):
    partner = owner ^ 1
    pool = [2 * owner, 2 * owner + 1, 2 * partner, 2 * partner + 1]
    member = [parent_ref[kid] == owner for kid in pool]
    first = jnp.where(member[0], 0, jnp.where(member[1], 1, 2))
    second = jnp.where(member[3], 3, jnp.where(member[2], 2, 1))
    ids = [2 * jnp.where(slot < 2, owner, partner) + (slot & 1) for slot in (first, second)]
    return (first, second), ids


def place_of():
    front, leaf = lax.axis_index("front"), lax.axis_index("leaf")
    owner = (leaf & -2) | (front & 1)
    block = (front & -2) | (leaf & 1)
    return owner, block


def keeps():
    return ((lax.axis_index("leaf") ^ lax.axis_index("front")) & 1) == 0


def store(pair, action):
    for ref, chosen in zip(pair, (keeps(), jnp.logical_not(keeps()))):
        pl.when(chosen)(functools.partial(action, ref))


def rounded(value):
    return value.astype(jnp.bfloat16)


def halves(value):
    high = rounded(value)
    return high, rounded(value - high.astype(jnp.float32))


def dot(left, right):
    return jnp.dot(left, right, preferred_element_type=jnp.float32)


def product(left, right):
    (left_high, left_low), (right_high, right_low) = left, right
    return dot(left_high, right_high) + (dot(left_high, right_low) + dot(left_low, right_high))


def column_sum(value):
    return jnp.sum(value, axis=0, keepdims=True)


def spans(width):
    return [slice(start, start + COLS) for start in range(0, width, COLS)]


def select_kernel(parent_ref, index_ref, own_rows, own_inverse, other_rows, other_inverse, kid_out, index_out):
    leaf = lax.axis_index("leaf")
    slots, _ = kids_of(parent_ref, leaf)
    split = own_rows.shape[1]
    for place, slot in enumerate(slots):
        for source in range(4):
            rows, inverse = (own_rows, own_inverse) if source < 2 else (other_rows, other_inverse)

            @pl.when(slot == source)
            def _(rows=rows, inverse=inverse, place=place, source=source):
                kid_out[place, :split] = rows[source % 2]
                kid_out[place, split:] = inverse[source % 2]

    owner, block = place_of()
    _, ids = kids_of(parent_ref, owner)
    pieces, width = index_out.shape[1:]
    for place, kid in enumerate(ids):
        row = index_ref[pl.ds(kid, 1), :]
        parts = [row[:, start : start + width] for start in range(0, pieces * width, width)]
        for mask in range(pieces):
            part = parts[0]
            for at in range(1, pieces):
                part = jnp.where((block ^ mask) == at, parts[at], part)
            index_out[place, mask : mask + 1, :] = part


def picks(index, first, rows):
    position = lax.broadcasted_iota(jnp.int32, (rows, index.shape[1]), 0) + first
    return rounded(jnp.where(position == index, 1.0, 0.0))


def unpacked(pieces, refs):
    pairs = [(refs[0], refs[0]), (refs[1], refs[1])]
    for at in range(2, 2 * pieces - 2, 4):
        near_keep, near_swap, far_keep, far_swap = refs[at : at + 4]
        pairs += [(near_keep, near_swap), (far_keep, far_swap)]
    return pairs


def diagonal_kernel(pieces, index, factor, *refs):
    diag_high, diag_low, pick_high, pick_low, weights, parent_sum = refs[2 * pieces - 2 :]
    _, block = place_of()
    own_rows, size = refs[0].shape
    parent_sum[...] = column_sum(refs[0][...] * refs[0][...])
    for mask, pair in enumerate(unpacked(pieces, refs)):
        start = pl.multiple_of((block ^ mask) * own_rows, 16)

        def put(ref, start=start):
            diag_high[pl.ds(start, own_rows), :], diag_low[pl.ds(start, own_rows), :] = halves(ref[...])

        if mask < 2:
            put(pair[0])
        else:
            store(pair, put)
    for kid in range(2):
        for mask in range(pieces):
            pick = picks(index[kid, mask : mask + 1, :], 0, size)
            pick_high[kid, mask] = rounded(dot(diag_high[...], pick))
            pick_low[kid, mask] = rounded(dot(diag_low[...], pick))
    factor_halves = halves(factor[...])
    for span in spans(size):
        weights[:, span] = product(factor_halves, (diag_high[:, span], diag_low[:, span]))


def kid_kernel(pieces, index, pick_high, pick_low, factor, *refs):
    kids = refs[:pieces]
    reduced, lift_high, lower_high, kid_sum, inv_high, inv_low, lifted, lower = refs[pieces:]
    _, block = place_of()
    size, own_border, border_size = lifted.shape[0], factor.shape[0], lower.shape[0]
    kid_block = index.shape[2]
    inv_block, own_rows = kids[0].shape[1] - kid_block, size // pieces
    factor_high = rounded(factor[...])
    for kid in range(2):
        own_inverse = kids[0][kid, kid_block:]
        for mask in range(pieces):
            start = pl.multiple_of((block ^ mask) * inv_block, 16)
            high, low = halves(kids[mask][kid, kid_block:])
            inv_high[pl.ds(start, inv_block), :] = high
            inv_low[pl.ds(start, inv_block), :] = low
        inverse = inv_high[...], inv_low[...]
        for mask in range(pieces):
            high, low = halves(product(halves(kids[mask][kid, :kid_block]), inverse))
            lifted_part = dot(pick_high[kid, mask], high) + dot(pick_low[kid, mask], high)
            places = index[kid, mask : mask + 1, :]
            low_part = dot(picks(places, size + block * own_border, own_border), low)
            part = dot(picks(places, size, border_size), high)
            lifted[...] = lifted_part if mask == 0 else lifted[...] + lifted_part
            reduced[kid] = low_part if mask == 0 else reduced[kid] + low_part
            lower[...] = part if mask == 0 else lower[...] + part
        own = lifted[pl.ds(pl.multiple_of(block * own_rows, 16), own_rows), :]
        kid_sum[kid : kid + 1] = column_sum(own_inverse * own_inverse) + column_sum(own * own)
        lift_high[kid] = rounded(lifted[...])
        lower_high[kid] = rounded(lower[...])
        own_lower = lower[pl.ds(pl.multiple_of(block * own_border, 8), own_border), :]
        reduced[kid] = own_lower + reduced[kid] - dot(factor_high, lift_high[kid])


def border_kernel(border, lower_high, border_high, border_lower):
    border_high[...] = rounded(border[...])
    for kid in range(2):
        for span in spans(lower_high.shape[2]):
            border_lower[kid, :, span] = dot(border_high[...], lower_high[kid, :, span])


def image_kernel(pieces, *refs):
    factor = unpacked(pieces, refs)
    border_high, border_lower, weights, reduced, lift_high, diag_high, diag_low, parent_sum, kid_sum, out = refs[
        2 * pieces - 2 : 2 * pieces + 8
    ]
    factor_high, fold_high, fold_low = refs[2 * pieces + 8 :]
    _, block = place_of()
    own_border, size = refs[0].shape
    kid_size = reduced.shape[2]
    for mask, pair in enumerate(factor):
        start = pl.multiple_of((block ^ mask) * own_border, 16)

        def put(ref, start=start):
            factor_high[pl.ds(start, own_border), :] = rounded(ref[...])

        if mask < 2:
            put(pair[0])
        else:
            store(pair, put)
    for span in spans(size):
        fold_high[:, span], fold_low[:, span] = halves(dot(border_high[...], factor_high[:, span]))
    fold = fold_high[...], fold_low[...]
    for span in spans(size):
        image = product(fold, (diag_high[:, span], diag_low[:, span]))
        out[:, span] = parent_sum[:, span] + column_sum(weights[:, span] * image)
    for kid in range(2):
        for span in spans(kid_size):
            image = border_lower[kid, :, span] - dot(fold[0], lift_high[kid, :, span])
            target = size + kid * kid_size + span.start
            out[:, target : target + COLS] = kid_sum[kid : kid + 1, span] + column_sum(reduced[kid, :, span] * image)


def finish_kernel(parent_ref, *refs):
    partials, (parent_out, kid_out) = refs[:-2], refs[-2:]
    leaf = lax.axis_index("leaf")
    size, kid_size = parent_out.shape[1], kid_out.shape[1]
    half = len(partials) // 2
    sums = [functools.reduce(jnp.add, [ref[...] for ref in group]) for group in (partials[:half], partials[half:])]
    owner, _ = place_of()
    parent_out[...] = jnp.where(owner == leaf, sums[0][:, :size], sums[1][:, :size])
    for parent, total in ((owner, sums[0]), (owner ^ 1, sums[1])):
        _, ids = kids_of(parent_ref, parent)
        for place in range(2):
            for kid in range(2):

                @pl.when(ids[place] == 2 * leaf + kid)
                def _(total=total, place=place, kid=kid):
                    start = size + place * kid_size
                    kid_out[kid : kid + 1] = total[:, start : start + kid_size]


def call(kernel, out_shape, limit, scalars=0, loose=0, keep=True, scratch=(), moved=1_000):
    def run(*args):
        specs = [pl.BlockSpec(memory_space=pltpu.SMEM if at < scalars else pltpu.VMEM) for at in range(len(args))]
        args = [
            pltpu.with_memory_space_constraint(value, pltpu.HBM if at < loose else pltpu.VMEM)
            for at, value in enumerate(args)
        ]
        results = out_shape
        if keep:
            results = jax.tree.map(lambda leaf: pltpu.VMEM(leaf.shape, leaf.dtype), results)
        return pl.pallas_call(
            kernel,
            out_shape=results,
            in_specs=specs,
            out_specs=jax.tree.map(lambda _: pl.BlockSpec(memory_space=pltpu.VMEM), out_shape),
            scratch_shapes=scratch,
            compiler_params=pltpu.CompilerParams(vmem_limit_bytes=limit * MIB),
            cost_estimate=pl.CostEstimate(flops=0, bytes_accessed=moved, transcendentals=0),
        )(*args)

    return run


def shards(border, factor, diagonal, kid_rows, kid_inverse, child_index, child_parent):
    border, factor, diagonal = border[0], factor[0], diagonal[0]
    pieces = lax.axis_size("front")
    size, kid_size, border_size = diagonal.shape[1], kid_rows.shape[2], border.shape[1]
    own_border = border.shape[0]
    kid_block = kid_rows.shape[1]
    half = jnp.bfloat16

    def over_fronts(value, parity=None):
        parts = {0: value}
        bit = 2
        while bit < pieces:
            for mask in list(parts):
                parts[mask | bit] = exchange(parts[mask], 0, bit, parity)
            bit *= 2
        return parts

    def spread(parts, gate_own, gate_rest):
        others = {mask | 1: exchange(after(part, *(gate_rest if mask else gate_own)), 1, 0) for mask, part in parts.items()}
        parts = parts | others
        return [parts[mask] for mask in range(pieces)]

    def gathered(own, keep, swap, gate_own, gate_keep, gate_swap):
        result = [own, exchange(after(own, *gate_own), 1, 0)]
        for mask in list(keep)[1:]:
            far_swap = exchange(after(keep[mask], *gate_keep), 1, 0, 0)
            far_keep = exchange(after(swap[mask], *gate_swap), 1, 0, 1)
            result += [keep[mask], swap[mask], far_keep, far_swap]
        return result

    last = pieces - 2
    keep_diagonal = over_fronts(diagonal, 0)
    keep_factor = over_fronts(factor, 0)
    own_diagonal = cross(diagonal)
    kid_shape = (2, kid_block + kid_inverse.shape[1], kid_size)
    own_kids, index = call(
        select_kernel, (shape_of(kid_shape), shape_of((2, pieces, kid_block), jnp.int32)), 6, scalars=1, loose=4
    )(child_parent, child_index, kid_rows, kid_inverse, exchange(kid_rows, 1, 0), exchange(kid_inverse, 1, 0))
    own_kids = cross(after(own_kids, own_diagonal, keep_diagonal[last], keep_factor[last]))
    swap_diagonal = over_fronts(own_diagonal, 1)
    kid_parts = over_fronts(after(own_kids, swap_diagonal[last]))
    own_factor = cross(after(factor, own_kids))
    diagonal_parts = gathered(own_diagonal, keep_diagonal, swap_diagonal, [own_kids], [own_kids], [own_kids])

    diag_high, diag_low, pick_high, pick_low, weights, parent_sum = call(
        functools.partial(diagonal_kernel, pieces),
        (
            shape_of((size, size), half),
            shape_of((size, size), half),
            shape_of((2, pieces, size, kid_block), half),
            shape_of((2, pieces, size, kid_block), half),
            shape_of((own_border, size)),
            shape_of((1, size)),
        ),
        10,
    )(index, own_factor, *diagonal_parts)
    own_border_rows = cross(after(border, own_kids))
    kids_here = kid_parts[last]
    swap_factor = over_fronts(after(own_factor, kids_here), 1)
    kid_parts = spread(kid_parts, [own_kids], [pick_high])

    reduced, lift_high, lower_high, kid_sum = call(
        functools.partial(kid_kernel, pieces),
        (
            shape_of((2, own_border, kid_size)),
            shape_of((2, size, kid_size), half),
            shape_of((2, border_size, kid_size), half),
            shape_of((2, kid_size)),
        ),
        20,
        scratch=[
            pltpu.VMEM((kid_size, kid_size), half),
            pltpu.VMEM((kid_size, kid_size), half),
            pltpu.VMEM((size, kid_size), jnp.float32),
            pltpu.VMEM((border_size, kid_size), jnp.float32),
        ],
    )(index, pick_high, pick_low, own_factor, *kid_parts)

    border_high, border_lower = call(
        border_kernel, (shape_of(border.shape, half), shape_of((2, own_border, kid_size))), 8
    )(own_border_rows, lower_high)

    factor_parts = gathered(own_factor, keep_factor, swap_factor, [kids_here], [kids_here], [lift_high, own_border_rows])
    total = call(
        functools.partial(image_kernel, pieces),
        shape_of((1, size + 2 * kid_size)),
        12,
        scratch=[
            pltpu.VMEM((border_size, size), half),
            pltpu.VMEM((own_border, size), half),
            pltpu.VMEM((own_border, size), half),
        ],
    )(
        *factor_parts,
        border_high,
        border_lower,
        weights,
        reduced,
        lift_high,
        diag_high,
        diag_low,
        parent_sum,
        kid_sum,
    )

    total = total + exchange(total, 1, 0)
    bit = 4
    while bit < pieces:
        total = total + exchange(total, 0, bit)
        bit *= 2
    near = range(min(pieces, 4))
    order = [mask for parity in (0, 1) for mask in near if mask % 2 == parity]
    partials = [exchange(total, 0, mask) if mask else total for mask in order]
    return call(finish_kernel, (shape_of((1, size)), shape_of((2, kid_size))), 2, scalars=1, loose=1, keep=False)(
        child_parent, *partials
    )


def solution(mesh):
    whole = P("leaf", "front", None)
    return jax.shard_map(
        shards,
        mesh=mesh,
        in_specs=(whole,) * 5 + (P(), P()),
        out_specs=(P("leaf", None), P("leaf", None)),
        check_vma=False,
    )
```

```python
import functools

import jax
import jax.numpy as jnp
from jax import lax
from jax.experimental import pallas as pl
from jax.experimental.pallas import tpu as pltpu
from jax.sharding import PartitionSpec as P

MIB = 1024 * 1024
COLS = 256


def shape_of(shape, dtype=jnp.float32):
    return jax.ShapeDtypeStruct(shape, dtype)


def exchange(value, leaf_mask, front_mask, parity=None):
    fronts = lax.axis_size("front")
    pairs = [
        (leaf * fronts + front, (leaf ^ leaf_mask) * fronts + (front ^ front_mask))
        for leaf in range(lax.axis_size("leaf"))
        for front in range(fronts)
        if parity is None or (leaf ^ front) & 1 == parity
    ]
    return lax.ppermute(value, ("leaf", "front"), pairs)


def cross(value):
    fronts = lax.axis_size("front")
    pairs = []
    for leaf in range(lax.axis_size("leaf")):
        for front in range(fronts):
            flip = (leaf ^ front) & 1
            pairs.append((leaf * fronts + front, (leaf ^ flip) * fronts + (front ^ flip)))
    return lax.ppermute(value, ("leaf", "front"), pairs)


def after(value, *others):
    return lax.optimization_barrier((value, *others))[0]


def kids_of(parent_ref, owner):
    partner = owner ^ 1
    pool = [2 * owner, 2 * owner + 1, 2 * partner, 2 * partner + 1]
    member = [parent_ref[kid] == owner for kid in pool]
    first = jnp.where(member[0], 0, jnp.where(member[1], 1, 2))
    second = jnp.where(member[3], 3, jnp.where(member[2], 2, 1))
    ids = [2 * jnp.where(slot < 2, owner, partner) + (slot & 1) for slot in (first, second)]
    return (first, second), ids


def place_of():
    front, leaf = lax.axis_index("front"), lax.axis_index("leaf")
    owner = (leaf & -2) | (front & 1)
    block = (front & -2) | (leaf & 1)
    return owner, block


def keeps():
    return ((lax.axis_index("leaf") ^ lax.axis_index("front")) & 1) == 0


def store(pair, action):
    for ref, chosen in zip(pair, (keeps(), jnp.logical_not(keeps()))):
        pl.when(chosen)(functools.partial(action, ref))


def rounded(value):
    return value.astype(jnp.bfloat16)


def halves(value):
    high = rounded(value)
    return high, rounded(value - high.astype(jnp.float32))


def dot(left, right):
    return jnp.dot(left, right, preferred_element_type=jnp.float32)


def product(left, right):
    (left_high, left_low), (right_high, right_low) = left, right
    return dot(left_high, right_high) + (dot(left_high, right_low) + dot(left_low, right_high))


def column_sum(value):
    return jnp.sum(value, axis=0, keepdims=True)


def spans(width):
    return [slice(start, start + COLS) for start in range(0, width, COLS)]


def select_kernel(parent_ref, index_ref, own_rows, own_inverse, other_rows, other_inverse, kid_out, index_out):
    leaf = lax.axis_index("leaf")
    slots, _ = kids_of(parent_ref, leaf)
    split = own_rows.shape[1]
    for place, slot in enumerate(slots):
        for source in range(4):
            rows, inverse = (own_rows, own_inverse) if source < 2 else (other_rows, other_inverse)

            @pl.when(slot == source)
            def _(rows=rows, inverse=inverse, place=place, source=source):
                kid_out[place, :split] = rows[source % 2]
                kid_out[place, split:] = inverse[source % 2]

    owner, block = place_of()
    _, ids = kids_of(parent_ref, owner)
    pieces, width = index_out.shape[1:]
    for place, kid in enumerate(ids):
        row = index_ref[pl.ds(kid, 1), :]
        parts = [row[:, start : start + width] for start in range(0, pieces * width, width)]
        for mask in range(pieces):
            part = parts[0]
            for at in range(1, pieces):
                part = jnp.where((block ^ mask) == at, parts[at], part)
            index_out[place, mask : mask + 1, :] = part


def picks(index, first, rows):
    position = lax.broadcasted_iota(jnp.int32, (rows, index.shape[1]), 0) + first
    return rounded(jnp.where(position == index, 1.0, 0.0))


def unpacked(pieces, refs):
    pairs = [(refs[0], refs[0]), (refs[1], refs[1])]
    for at in range(2, 2 * pieces - 2, 4):
        near_keep, near_swap, far_keep, far_swap = refs[at : at + 4]
        pairs += [(near_keep, near_swap), (far_keep, far_swap)]
    return pairs


def diagonal_kernel(pieces, index, factor, *refs):
    diag_high, diag_low, pick_high, weights, parent_sum = refs[2 * pieces - 2 :]
    _, block = place_of()
    own_rows, size = refs[0].shape
    parent_sum[...] = column_sum(refs[0][...] * refs[0][...])
    for mask, pair in enumerate(unpacked(pieces, refs)):
        start = pl.multiple_of((block ^ mask) * own_rows, 16)

        def put(ref, start=start):
            diag_high[pl.ds(start, own_rows), :], diag_low[pl.ds(start, own_rows), :] = halves(ref[...])

        if mask < 2:
            put(pair[0])
        else:
            store(pair, put)
    kid_block = index.shape[2]
    for kid in range(2):
        for mask in range(pieces):

            @pl.when((block ^ mask) * kid_block < size)
            def _(kid=kid, mask=mask):
                pick_high[kid, mask] = rounded(dot(diag_high[...], picks(index[kid, mask : mask + 1, :], 0, size)))

    factor_halves = halves(factor[...])
    for span in spans(size):
        weights[:, span] = product(factor_halves, (diag_high[:, span], diag_low[:, span]))


def kid_kernel(pieces, index, pick_high, factor, *refs):
    kids = refs[:pieces]
    reduced, lift_high, lower_high, kid_sum, inv_high, inv_low, lifted, lower = refs[pieces:]
    _, block = place_of()
    size, own_border, border_size = lifted.shape[0], factor.shape[0], lower.shape[0]
    kid_block = index.shape[2]
    inv_block, own_rows = kids[0].shape[1] - kid_block, size // pieces
    factor_high = rounded(factor[...])
    middle, kid_size = border_size // 2, lifted.shape[1]
    for kid in range(2):
        own_inverse = kids[0][kid, kid_block:]
        for mask in range(pieces):
            start = pl.multiple_of((block ^ mask) * inv_block, 16)
            high, low = halves(kids[mask][kid, kid_block:])
            inv_high[pl.ds(start, inv_block), :] = high
            inv_low[pl.ds(start, inv_block), :] = low
        inverse = inv_high[...], inv_low[...]
        lifted[...] = jnp.zeros(lifted.shape, jnp.float32)
        lower[middle:] = jnp.zeros((border_size - middle, kid_size), jnp.float32)
        for mask in range(pieces):
            high, low = halves(product(halves(kids[mask][kid, :kid_block]), inverse))
            places = index[kid, mask : mask + 1, :]
            first_row = (block ^ mask) * kid_block

            @pl.when(first_row < size)
            def _(kid=kid, mask=mask, high=high):
                lifted[...] += dot(pick_high[kid, mask], high)

            low_part = dot(picks(places, size + block * own_border, own_border), low)
            reduced[kid] = low_part if mask == 0 else reduced[kid] + low_part
            part = dot(picks(places, size, middle), high)
            lower[:middle] = part if mask == 0 else lower[:middle] + part

            @pl.when(first_row + kid_block - 1 + border_size - pieces * kid_block >= middle)
            def _(places=places, high=high):
                lower[middle:] += dot(picks(places, size + middle, border_size - middle), high)

        own = lifted[pl.ds(pl.multiple_of(block * own_rows, 16), own_rows), :]
        kid_sum[kid : kid + 1] = column_sum(own_inverse * own_inverse) + column_sum(own * own)
        lift_high[kid] = rounded(lifted[...])
        lower_high[kid] = rounded(lower[...])
        own_lower = lower[pl.ds(pl.multiple_of(block * own_border, 8), own_border), :]
        reduced[kid] = own_lower + reduced[kid] - dot(factor_high, lift_high[kid])


def border_kernel(border, lower_high, border_high, border_lower):
    border_high[...] = rounded(border[...])
    for kid in range(2):
        for span in spans(lower_high.shape[2]):
            border_lower[kid, :, span] = dot(border_high[...], lower_high[kid, :, span])


def image_kernel(pieces, *refs):
    factor = unpacked(pieces, refs)
    border_high, border_lower, weights, reduced, lift_high, diag_high, diag_low, parent_sum, kid_sum, out = refs[
        2 * pieces - 2 : 2 * pieces + 8
    ]
    factor_high, fold_high, fold_low = refs[2 * pieces + 8 :]
    _, block = place_of()
    own_border, size = refs[0].shape
    kid_size = reduced.shape[2]
    for mask, pair in enumerate(factor):
        start = pl.multiple_of((block ^ mask) * own_border, 16)

        def put(ref, start=start):
            factor_high[pl.ds(start, own_border), :] = rounded(ref[...])

        if mask < 2:
            put(pair[0])
        else:
            store(pair, put)
    for span in spans(size):
        fold_high[:, span], fold_low[:, span] = halves(dot(border_high[...], factor_high[:, span]))
    fold = fold_high[...], fold_low[...]
    for span in spans(size):
        image = product(fold, (diag_high[:, span], diag_low[:, span]))
        out[:, span] = parent_sum[:, span] + column_sum(weights[:, span] * image)
    for kid in range(2):
        for span in spans(kid_size):
            image = border_lower[kid, :, span] - dot(fold[0], lift_high[kid, :, span])
            target = size + kid * kid_size + span.start
            out[:, target : target + COLS] = kid_sum[kid : kid + 1, span] + column_sum(reduced[kid, :, span] * image)


def finish_kernel(parent_ref, *refs):
    partials, (parent_out, kid_out) = refs[:-2], refs[-2:]
    leaf = lax.axis_index("leaf")
    size, kid_size = parent_out.shape[1], kid_out.shape[1]
    half = len(partials) // 2
    sums = [functools.reduce(jnp.add, [ref[...] for ref in group]) for group in (partials[:half], partials[half:])]
    owner, _ = place_of()
    parent_out[...] = jnp.where(owner == leaf, sums[0][:, :size], sums[1][:, :size])
    for parent, total in ((owner, sums[0]), (owner ^ 1, sums[1])):
        _, ids = kids_of(parent_ref, parent)
        for place in range(2):
            for kid in range(2):

                @pl.when(ids[place] == 2 * leaf + kid)
                def _(total=total, place=place, kid=kid):
                    start = size + place * kid_size
                    kid_out[kid : kid + 1] = total[:, start : start + kid_size]


def call(kernel, out_shape, limit, scalars=0, loose=0, keep=True, scratch=(), moved=1_000):
    def run(*args):
        specs = [pl.BlockSpec(memory_space=pltpu.SMEM if at < scalars else pltpu.VMEM) for at in range(len(args))]
        args = [
            pltpu.with_memory_space_constraint(value, pltpu.HBM if at < loose else pltpu.VMEM)
            for at, value in enumerate(args)
        ]
        results = out_shape
        if keep:
            results = jax.tree.map(lambda leaf: pltpu.VMEM(leaf.shape, leaf.dtype), results)
        return pl.pallas_call(
            kernel,
            out_shape=results,
            in_specs=specs,
            out_specs=jax.tree.map(lambda _: pl.BlockSpec(memory_space=pltpu.VMEM), out_shape),
            scratch_shapes=scratch,
            compiler_params=pltpu.CompilerParams(vmem_limit_bytes=limit * MIB),
            cost_estimate=pl.CostEstimate(flops=0, bytes_accessed=moved, transcendentals=0),
        )(*args)

    return run


def shards(border, factor, diagonal, kid_rows, kid_inverse, child_index, child_parent):
    border, factor, diagonal = border[0], factor[0], diagonal[0]
    pieces = lax.axis_size("front")
    size, kid_size, border_size = diagonal.shape[1], kid_rows.shape[2], border.shape[1]
    own_border = border.shape[0]
    kid_block = kid_rows.shape[1]
    half = jnp.bfloat16

    def over_fronts(value, parity=None):
        parts = {0: value}
        bit = 2
        while bit < pieces:
            for mask in list(parts):
                parts[mask | bit] = exchange(parts[mask], 0, bit, parity)
            bit *= 2
        return parts

    def spread(parts, gate_own, gate_rest):
        others = {mask | 1: exchange(after(part, *(gate_rest if mask else gate_own)), 1, 0) for mask, part in parts.items()}
        parts = parts | others
        return [parts[mask] for mask in range(pieces)]

    def gathered(own, keep, swap, gate_own, gate_keep, gate_swap):
        result = [own, exchange(after(own, *gate_own), 1, 0)]
        for mask in list(keep)[1:]:
            far_swap = exchange(after(keep[mask], *gate_keep), 1, 0, 0)
            far_keep = exchange(after(swap[mask], *gate_swap), 1, 0, 1)
            result += [keep[mask], swap[mask], far_keep, far_swap]
        return result

    last = pieces - 2
    raw_rows, raw_inverse = exchange(kid_rows, 1, 0), exchange(kid_inverse, 1, 0)
    keep_diagonal = over_fronts(after(diagonal, raw_rows, raw_inverse), 0)
    keep_factor = over_fronts(after(factor, raw_rows, raw_inverse), 0)
    own_diagonal = cross(after(diagonal, raw_rows, raw_inverse))
    kid_shape = (2, kid_block + kid_inverse.shape[1], kid_size)
    own_kids, index = call(
        select_kernel, (shape_of(kid_shape), shape_of((2, pieces, kid_block), jnp.int32)), 6, scalars=1, loose=4
    )(child_parent, child_index, kid_rows, kid_inverse, raw_rows, raw_inverse)
    own_kids = cross(after(own_kids, own_diagonal, keep_diagonal[last], keep_factor[last]))
    swap_diagonal = over_fronts(own_diagonal, 1)
    kid_parts = over_fronts(after(own_kids, swap_diagonal[last]))
    own_factor = cross(after(factor, own_kids))
    diagonal_parts = gathered(own_diagonal, keep_diagonal, swap_diagonal, [own_kids], [own_kids], [own_kids])

    diag_high, diag_low, pick_high, weights, parent_sum = call(
        functools.partial(diagonal_kernel, pieces),
        (
            shape_of((size, size), half),
            shape_of((size, size), half),
            shape_of((2, pieces, size, kid_block), half),
            shape_of((own_border, size)),
            shape_of((1, size)),
        ),
        10,
    )(index, own_factor, *diagonal_parts)
    own_border_rows = cross(after(border, own_kids))
    kids_here = kid_parts[last]
    swap_factor = over_fronts(after(own_factor, kids_here), 1)
    kid_parts = spread(kid_parts, [own_kids], [pick_high])

    reduced, lift_high, lower_high, kid_sum = call(
        functools.partial(kid_kernel, pieces),
        (
            shape_of((2, own_border, kid_size)),
            shape_of((2, size, kid_size), half),
            shape_of((2, border_size, kid_size), half),
            shape_of((2, kid_size)),
        ),
        20,
        scratch=[
            pltpu.VMEM((kid_size, kid_size), half),
            pltpu.VMEM((kid_size, kid_size), half),
            pltpu.VMEM((size, kid_size), jnp.float32),
            pltpu.VMEM((border_size, kid_size), jnp.float32),
        ],
    )(index, pick_high, own_factor, *kid_parts)

    border_high, border_lower = call(
        border_kernel, (shape_of(border.shape, half), shape_of((2, own_border, kid_size))), 8
    )(own_border_rows, lower_high)

    factor_parts = gathered(own_factor, keep_factor, swap_factor, [kids_here], [kids_here], [lift_high, own_border_rows])
    total = call(
        functools.partial(image_kernel, pieces),
        shape_of((1, size + 2 * kid_size)),
        12,
        scratch=[
            pltpu.VMEM((border_size, size), half),
            pltpu.VMEM((own_border, size), half),
            pltpu.VMEM((own_border, size), half),
        ],
    )(
        *factor_parts,
        border_high,
        border_lower,
        weights,
        reduced,
        lift_high,
        diag_high,
        diag_low,
        parent_sum,
        kid_sum,
    )

    total = total + exchange(total, 1, 0)
    bit = 4
    while bit < pieces:
        total = total + exchange(total, 0, bit)
        bit *= 2
    near = range(min(pieces, 4))
    order = [mask for parity in (0, 1) for mask in near if mask % 2 == parity]
    partials = [exchange(total, 0, mask) if mask else total for mask in order]
    return call(finish_kernel, (shape_of((1, size)), shape_of((2, kid_size))), 2, scalars=1, loose=1, keep=False)(
        child_parent, *partials
    )


def solution(mesh):
    whole = P("leaf", "front", None)
    return jax.shard_map(
        shards,
        mesh=mesh,
        in_specs=(whole,) * 5 + (P(), P()),
        out_specs=(P("leaf", None), P("leaf", None)),
        check_vma=False,
    )
```

```python
import functools

import jax
import jax.numpy as jnp
from jax import lax
from jax.experimental import pallas as pl
from jax.experimental.pallas import tpu as pltpu
from jax.sharding import PartitionSpec as P

MIB = 1024 * 1024
COLS = 256


def shape_of(shape, dtype=jnp.float32):
    return jax.ShapeDtypeStruct(shape, dtype)


def exchange(value, leaf_mask, front_mask, parity=None):
    fronts = lax.axis_size("front")
    pairs = [
        (leaf * fronts + front, (leaf ^ leaf_mask) * fronts + (front ^ front_mask))
        for leaf in range(lax.axis_size("leaf"))
        for front in range(fronts)
        if parity is None or (leaf ^ front) & 1 == parity
    ]
    return lax.ppermute(value, ("leaf", "front"), pairs)


def cross(value):
    fronts = lax.axis_size("front")
    pairs = []
    for leaf in range(lax.axis_size("leaf")):
        for front in range(fronts):
            flip = (leaf ^ front) & 1
            pairs.append((leaf * fronts + front, (leaf ^ flip) * fronts + (front ^ flip)))
    return lax.ppermute(value, ("leaf", "front"), pairs)


def after(value, *others):
    return lax.optimization_barrier((value, *others))[0]


def kids_of(parent_ref, owner):
    partner = owner ^ 1
    pool = [2 * owner, 2 * owner + 1, 2 * partner, 2 * partner + 1]
    member = [parent_ref[kid] == owner for kid in pool]
    first = jnp.where(member[0], 0, jnp.where(member[1], 1, 2))
    second = jnp.where(member[3], 3, jnp.where(member[2], 2, 1))
    ids = [2 * jnp.where(slot < 2, owner, partner) + (slot & 1) for slot in (first, second)]
    return (first, second), ids


def place_of():
    front, leaf = lax.axis_index("front"), lax.axis_index("leaf")
    owner = (leaf & -2) | (front & 1)
    block = (front & -2) | (leaf & 1)
    return owner, block


def keeps():
    return ((lax.axis_index("leaf") ^ lax.axis_index("front")) & 1) == 0


def store(pair, action):
    for ref, chosen in zip(pair, (keeps(), jnp.logical_not(keeps()))):
        pl.when(chosen)(functools.partial(action, ref))


def rounded(value):
    return value.astype(jnp.bfloat16)


def halves(value):
    high = rounded(value)
    return high, rounded(value - high.astype(jnp.float32))


def dot(left, right):
    return jnp.dot(left, right, preferred_element_type=jnp.float32)


def product(left, right):
    (left_high, left_low), (right_high, right_low) = left, right
    return dot(left_high, right_high) + (dot(left_high, right_low) + dot(left_low, right_high))


def column_sum(value):
    return jnp.sum(value, axis=0, keepdims=True)


def spans(width):
    return [slice(start, start + COLS) for start in range(0, width, COLS)]


def select_kernel(parent_ref, index_ref, own_rows, own_inverse, other_rows, other_inverse, kid_out, index_out):
    leaf = lax.axis_index("leaf")
    slots, _ = kids_of(parent_ref, leaf)
    split = own_rows.shape[1]
    for place, slot in enumerate(slots):
        for source in range(4):
            rows, inverse = (own_rows, own_inverse) if source < 2 else (other_rows, other_inverse)

            @pl.when(slot == source)
            def _(rows=rows, inverse=inverse, place=place, source=source):
                kid_out[place, :split] = rows[source % 2]
                kid_out[place, split:] = inverse[source % 2]

    owner, block = place_of()
    _, ids = kids_of(parent_ref, owner)
    pieces, width = index_out.shape[1:]
    for place, kid in enumerate(ids):
        row = index_ref[pl.ds(kid, 1), :]
        parts = [row[:, start : start + width] for start in range(0, pieces * width, width)]
        for mask in range(pieces):
            part = parts[0]
            for at in range(1, pieces):
                part = jnp.where((block ^ mask) == at, parts[at], part)
            index_out[place, mask : mask + 1, :] = part


def picks(index, first, rows):
    position = lax.broadcasted_iota(jnp.int32, (rows, index.shape[1]), 0) + first
    return rounded(jnp.where(position == index, 1.0, 0.0))


def unpacked(pieces, refs):
    pairs = [(refs[0], refs[0]), (refs[1], refs[1])]
    for at in range(2, 2 * pieces - 2, 4):
        near_keep, near_swap, far_keep, far_swap = refs[at : at + 4]
        pairs += [(near_keep, near_swap), (far_keep, far_swap)]
    return pairs


def diagonal_kernel(pieces, index, factor, *refs):
    diag_high, diag_low, pick_high, weights, parent_sum = refs[2 * pieces - 2 :]
    _, block = place_of()
    own_rows, size = refs[0].shape
    parent_sum[...] = column_sum(refs[0][...] * refs[0][...])
    for mask, pair in enumerate(unpacked(pieces, refs)):
        start = pl.multiple_of((block ^ mask) * own_rows, 16)

        def put(ref, start=start):
            diag_high[pl.ds(start, own_rows), :], diag_low[pl.ds(start, own_rows), :] = halves(ref[...])

        if mask < 2:
            put(pair[0])
        else:
            store(pair, put)
    for kid in range(2):
        for mask in range(pieces):
            pick = picks(index[kid, mask : mask + 1, :], 0, size)
            pick_high[kid, mask] = rounded(dot(diag_high[...], pick))
    factor_halves = halves(factor[...])
    for span in spans(size):
        weights[:, span] = product(factor_halves, (diag_high[:, span], diag_low[:, span]))


def kid_kernel(pieces, index, pick_high, factor, *refs):
    kids = refs[:pieces]
    reduced, lift_high, lower_high, kid_sum, inv_high, inv_low, lifted, lower = refs[pieces:]
    _, block = place_of()
    size, own_border, border_size = lifted.shape[0], factor.shape[0], lower.shape[0]
    kid_block = index.shape[2]
    inv_block, own_rows = kids[0].shape[1] - kid_block, size // pieces
    factor_high = rounded(factor[...])
    for kid in range(2):
        own_inverse = kids[0][kid, kid_block:]
        for mask in range(pieces):
            start = pl.multiple_of((block ^ mask) * inv_block, 16)
            high, low = halves(kids[mask][kid, kid_block:])
            inv_high[pl.ds(start, inv_block), :] = high
            inv_low[pl.ds(start, inv_block), :] = low
        inverse = inv_high[...], inv_low[...]
        for mask in range(pieces):
            high, low = halves(product(halves(kids[mask][kid, :kid_block]), inverse))
            lifted_part = dot(pick_high[kid, mask], high)
            places = index[kid, mask : mask + 1, :]
            low_part = dot(picks(places, size + block * own_border, own_border), low)
            part = dot(picks(places, size, border_size), high)
            lifted[...] = lifted_part if mask == 0 else lifted[...] + lifted_part
            reduced[kid] = low_part if mask == 0 else reduced[kid] + low_part
            lower[...] = part if mask == 0 else lower[...] + part
        own = lifted[pl.ds(pl.multiple_of(block * own_rows, 16), own_rows), :]
        kid_sum[kid : kid + 1] = column_sum(own_inverse * own_inverse) + column_sum(own * own)
        lift_high[kid] = rounded(lifted[...])
        lower_high[kid] = rounded(lower[...])
        own_lower = lower[pl.ds(pl.multiple_of(block * own_border, 8), own_border), :]
        reduced[kid] = own_lower + reduced[kid] - dot(factor_high, lift_high[kid])


def border_kernel(border, lower_high, border_high, border_lower):
    border_high[...] = rounded(border[...])
    for kid in range(2):
        for span in spans(lower_high.shape[2]):
            border_lower[kid, :, span] = dot(border_high[...], lower_high[kid, :, span])


def image_kernel(pieces, *refs):
    factor = unpacked(pieces, refs)
    border_high, border_lower, weights, reduced, lift_high, diag_high, diag_low, parent_sum, kid_sum, out = refs[
        2 * pieces - 2 : 2 * pieces + 8
    ]
    factor_high, fold_high, fold_low = refs[2 * pieces + 8 :]
    _, block = place_of()
    own_border, size = refs[0].shape
    kid_size = reduced.shape[2]
    for mask, pair in enumerate(factor):
        start = pl.multiple_of((block ^ mask) * own_border, 16)

        def put(ref, start=start):
            factor_high[pl.ds(start, own_border), :] = rounded(ref[...])

        if mask < 2:
            put(pair[0])
        else:
            store(pair, put)
    for span in spans(size):
        fold_high[:, span], fold_low[:, span] = halves(dot(border_high[...], factor_high[:, span]))
    fold = fold_high[...], fold_low[...]
    for span in spans(size):
        image = product(fold, (diag_high[:, span], diag_low[:, span]))
        out[:, span] = parent_sum[:, span] + column_sum(weights[:, span] * image)
    for kid in range(2):
        for span in spans(kid_size):
            image = border_lower[kid, :, span] - dot(fold[0], lift_high[kid, :, span])
            target = size + kid * kid_size + span.start
            out[:, target : target + COLS] = kid_sum[kid : kid + 1, span] + column_sum(reduced[kid, :, span] * image)


def finish_kernel(parent_ref, *refs):
    partials, (parent_out, kid_out) = refs[:-2], refs[-2:]
    leaf = lax.axis_index("leaf")
    size, kid_size = parent_out.shape[1], kid_out.shape[1]
    half = len(partials) // 2
    sums = [functools.reduce(jnp.add, [ref[...] for ref in group]) for group in (partials[:half], partials[half:])]
    owner, _ = place_of()
    parent_out[...] = jnp.where(owner == leaf, sums[0][:, :size], sums[1][:, :size])
    for parent, total in ((owner, sums[0]), (owner ^ 1, sums[1])):
        _, ids = kids_of(parent_ref, parent)
        for place in range(2):
            for kid in range(2):

                @pl.when(ids[place] == 2 * leaf + kid)
                def _(total=total, place=place, kid=kid):
                    start = size + place * kid_size
                    kid_out[kid : kid + 1] = total[:, start : start + kid_size]


def call(kernel, out_shape, limit, scalars=0, loose=0, keep=True, scratch=(), moved=1_000):
    def run(*args):
        specs = [pl.BlockSpec(memory_space=pltpu.SMEM if at < scalars else pltpu.VMEM) for at in range(len(args))]
        args = [
            pltpu.with_memory_space_constraint(value, pltpu.HBM if at < loose else pltpu.VMEM)
            for at, value in enumerate(args)
        ]
        results = out_shape
        if keep:
            results = jax.tree.map(lambda leaf: pltpu.VMEM(leaf.shape, leaf.dtype), results)
        return pl.pallas_call(
            kernel,
            out_shape=results,
            in_specs=specs,
            out_specs=jax.tree.map(lambda _: pl.BlockSpec(memory_space=pltpu.VMEM), out_shape),
            scratch_shapes=scratch,
            compiler_params=pltpu.CompilerParams(vmem_limit_bytes=limit * MIB),
            cost_estimate=pl.CostEstimate(flops=0, bytes_accessed=moved, transcendentals=0),
        )(*args)

    return run


def shards(border, factor, diagonal, kid_rows, kid_inverse, child_index, child_parent):
    border, factor, diagonal = border[0], factor[0], diagonal[0]
    pieces = lax.axis_size("front")
    size, kid_size, border_size = diagonal.shape[1], kid_rows.shape[2], border.shape[1]
    own_border = border.shape[0]
    kid_block = kid_rows.shape[1]
    half = jnp.bfloat16

    def over_fronts(value, parity=None):
        parts = {0: value}
        bit = 2
        while bit < pieces:
            for mask in list(parts):
                parts[mask | bit] = exchange(parts[mask], 0, bit, parity)
            bit *= 2
        return parts

    def spread(parts, gate_own, gate_rest):
        others = {mask | 1: exchange(after(part, *(gate_rest if mask else gate_own)), 1, 0) for mask, part in parts.items()}
        parts = parts | others
        return [parts[mask] for mask in range(pieces)]

    def gathered(own, keep, swap, gate_own, gate_keep, gate_swap):
        result = [own, exchange(after(own, *gate_own), 1, 0)]
        for mask in list(keep)[1:]:
            far_swap = exchange(after(keep[mask], *gate_keep), 1, 0, 0)
            far_keep = exchange(after(swap[mask], *gate_swap), 1, 0, 1)
            result += [keep[mask], swap[mask], far_keep, far_swap]
        return result

    last = pieces - 2
    keep_diagonal = over_fronts(diagonal, 0)
    keep_factor = over_fronts(factor, 0)
    own_diagonal = cross(diagonal)
    kid_shape = (2, kid_block + kid_inverse.shape[1], kid_size)
    own_kids, index = call(
        select_kernel, (shape_of(kid_shape), shape_of((2, pieces, kid_block), jnp.int32)), 6, scalars=1, loose=4
    )(child_parent, child_index, kid_rows, kid_inverse, exchange(kid_rows, 1, 0), exchange(kid_inverse, 1, 0))
    own_kids = cross(after(own_kids, own_diagonal, keep_diagonal[last], keep_factor[last]))
    swap_diagonal = over_fronts(own_diagonal, 1)
    kid_parts = over_fronts(after(own_kids, swap_diagonal[last]))
    own_factor = cross(after(factor, own_kids))
    diagonal_parts = gathered(own_diagonal, keep_diagonal, swap_diagonal, [own_kids], [own_kids], [own_kids])

    diag_high, diag_low, pick_high, weights, parent_sum = call(
        functools.partial(diagonal_kernel, pieces),
        (
            shape_of((size, size), half),
            shape_of((size, size), half),
            shape_of((2, pieces, size, kid_block), half),
            shape_of((own_border, size)),
            shape_of((1, size)),
        ),
        10,
    )(index, own_factor, *diagonal_parts)
    own_border_rows = cross(after(border, own_kids))
    kids_here = kid_parts[last]
    swap_factor = over_fronts(after(own_factor, kids_here), 1)
    kid_parts = spread(kid_parts, [own_kids], [pick_high])

    reduced, lift_high, lower_high, kid_sum = call(
        functools.partial(kid_kernel, pieces),
        (
            shape_of((2, own_border, kid_size)),
            shape_of((2, size, kid_size), half),
            shape_of((2, border_size, kid_size), half),
            shape_of((2, kid_size)),
        ),
        20,
        scratch=[
            pltpu.VMEM((kid_size, kid_size), half),
            pltpu.VMEM((kid_size, kid_size), half),
            pltpu.VMEM((size, kid_size), jnp.float32),
            pltpu.VMEM((border_size, kid_size), jnp.float32),
        ],
    )(index, pick_high, own_factor, *kid_parts)

    border_high, border_lower = call(
        border_kernel, (shape_of(border.shape, half), shape_of((2, own_border, kid_size))), 8
    )(own_border_rows, lower_high)

    factor_parts = gathered(own_factor, keep_factor, swap_factor, [kids_here], [kids_here], [lift_high, own_border_rows])
    total = call(
        functools.partial(image_kernel, pieces),
        shape_of((1, size + 2 * kid_size)),
        12,
        scratch=[
            pltpu.VMEM((border_size, size), half),
            pltpu.VMEM((own_border, size), half),
            pltpu.VMEM((own_border, size), half),
        ],
    )(
        *factor_parts,
        border_high,
        border_lower,
        weights,
        reduced,
        lift_high,
        diag_high,
        diag_low,
        parent_sum,
        kid_sum,
    )

    total = total + exchange(total, 1, 0)
    bit = 4
    while bit < pieces:
        total = total + exchange(total, 0, bit)
        bit *= 2
    near = range(min(pieces, 4))
    order = [mask for parity in (0, 1) for mask in near if mask % 2 == parity]
    partials = [exchange(total, 0, mask) if mask else total for mask in order]
    return call(finish_kernel, (shape_of((1, size)), shape_of((2, kid_size))), 2, scalars=1, loose=1, keep=False)(
        child_parent, *partials
    )


def solution(mesh):
    whole = P("leaf", "front", None)
    return jax.shard_map(
        shards,
        mesh=mesh,
        in_specs=(whole,) * 5 + (P(), P()),
        out_specs=(P("leaf", None), P("leaf", None)),
        check_vma=False,
    )
```

```python
import functools

import jax
import jax.numpy as jnp
from jax import lax
from jax.experimental import pallas as pl
from jax.experimental.pallas import tpu as pltpu
from jax.sharding import PartitionSpec as P

MIB = 1024 * 1024
COLS = 256


def shape_of(shape, dtype=jnp.float32):
    return jax.ShapeDtypeStruct(shape, dtype)


def exchange(value, leaf_mask, front_mask, parity=None):
    fronts = lax.axis_size("front")
    pairs = [
        (leaf * fronts + front, (leaf ^ leaf_mask) * fronts + (front ^ front_mask))
        for leaf in range(lax.axis_size("leaf"))
        for front in range(fronts)
        if parity is None or (leaf ^ front) & 1 == parity
    ]
    return lax.ppermute(value, ("leaf", "front"), pairs)


def cross(value):
    fronts = lax.axis_size("front")
    pairs = []
    for leaf in range(lax.axis_size("leaf")):
        for front in range(fronts):
            flip = (leaf ^ front) & 1
            pairs.append((leaf * fronts + front, (leaf ^ flip) * fronts + (front ^ flip)))
    return lax.ppermute(value, ("leaf", "front"), pairs)


def after(value, *others):
    return lax.optimization_barrier((value, *others))[0]


def kids_of(parent_ref, owner):
    partner = owner ^ 1
    pool = [2 * owner, 2 * owner + 1, 2 * partner, 2 * partner + 1]
    member = [parent_ref[kid] == owner for kid in pool]
    first = jnp.where(member[0], 0, jnp.where(member[1], 1, 2))
    second = jnp.where(member[3], 3, jnp.where(member[2], 2, 1))
    ids = [2 * jnp.where(slot < 2, owner, partner) + (slot & 1) for slot in (first, second)]
    return (first, second), ids


def place_of():
    front, leaf = lax.axis_index("front"), lax.axis_index("leaf")
    owner = (leaf & -2) | (front & 1)
    block = (front & -2) | (leaf & 1)
    return owner, block


def keeps():
    return ((lax.axis_index("leaf") ^ lax.axis_index("front")) & 1) == 0


def store(pair, action):
    for ref, chosen in zip(pair, (keeps(), jnp.logical_not(keeps()))):
        pl.when(chosen)(functools.partial(action, ref))


def rounded(value):
    return value.astype(jnp.bfloat16)


def halves(value):
    high = rounded(value)
    return high, rounded(value - high.astype(jnp.float32))


def dot(left, right):
    return jnp.dot(left, right, preferred_element_type=jnp.float32)


def product(left, right):
    (left_high, left_low), (right_high, right_low) = left, right
    return dot(left_high, right_high) + (dot(left_high, right_low) + dot(left_low, right_high))


def column_sum(value):
    return jnp.sum(value, axis=0, keepdims=True)


def spans(width):
    return [slice(start, start + COLS) for start in range(0, width, COLS)]


def select_kernel(parent_ref, index_ref, own_rows, own_inverse, other_rows, other_inverse, kid_out, index_out):
    leaf = lax.axis_index("leaf")
    slots, _ = kids_of(parent_ref, leaf)
    split = own_rows.shape[1]
    for place, slot in enumerate(slots):
        for source in range(4):
            rows, inverse = (own_rows, own_inverse) if source < 2 else (other_rows, other_inverse)

            @pl.when(slot == source)
            def _(rows=rows, inverse=inverse, place=place, source=source):
                kid_out[place, :split] = rows[source % 2]
                kid_out[place, split:] = inverse[source % 2]

    owner, block = place_of()
    _, ids = kids_of(parent_ref, owner)
    pieces, width = index_out.shape[1:]
    for place, kid in enumerate(ids):
        row = index_ref[pl.ds(kid, 1), :]
        parts = [row[:, start : start + width] for start in range(0, pieces * width, width)]
        for mask in range(pieces):
            part = parts[0]
            for at in range(1, pieces):
                part = jnp.where((block ^ mask) == at, parts[at], part)
            index_out[place, mask : mask + 1, :] = part


def picks(index, first, rows):
    position = lax.broadcasted_iota(jnp.int32, (rows, index.shape[1]), 0) + first
    return rounded(jnp.where(position == index, 1.0, 0.0))


def unpacked(pieces, refs):
    pairs = [(refs[0], refs[0]), (refs[1], refs[1])]
    for at in range(2, 2 * pieces - 2, 4):
        near_keep, near_swap, far_keep, far_swap = refs[at : at + 4]
        pairs += [(near_keep, near_swap), (far_keep, far_swap)]
    return pairs


def diagonal_kernel(pieces, index, factor, *refs):
    diag_high, diag_low, pick_high, weights, parent_sum = refs[2 * pieces - 2 :]
    _, block = place_of()
    own_rows, size = refs[0].shape
    parent_sum[...] = column_sum(refs[0][...] * refs[0][...])
    for mask, pair in enumerate(unpacked(pieces, refs)):
        start = pl.multiple_of((block ^ mask) * own_rows, 16)

        def put(ref, start=start):
            diag_high[pl.ds(start, own_rows), :], diag_low[pl.ds(start, own_rows), :] = halves(ref[...])

        if mask < 2:
            put(pair[0])
        else:
            store(pair, put)
    for kid in range(2):
        for mask in range(pieces):
            pick = picks(index[kid, mask : mask + 1, :], 0, size)
            pick_high[kid, mask] = rounded(dot(diag_high[...], pick))
    factor_halves = halves(factor[...])
    for span in spans(size):
        weights[:, span] = product(factor_halves, (diag_high[:, span], diag_low[:, span]))


def kid_kernel(pieces, index, pick_high, factor, *refs):
    kids = refs[:pieces]
    reduced, lift_high, lower_high, kid_sum, inv_high, inv_low, lifted, lower = refs[pieces:]
    _, block = place_of()
    size, own_border, border_size = lifted.shape[0], factor.shape[0], lower.shape[0]
    kid_block = index.shape[2]
    inv_block, own_rows = kids[0].shape[1] - kid_block, size // pieces
    factor_high = rounded(factor[...])
    for kid in range(2):
        own_inverse = kids[0][kid, kid_block:]
        for mask in range(pieces):
            start = pl.multiple_of((block ^ mask) * inv_block, 16)
            high, low = halves(kids[mask][kid, kid_block:])
            inv_high[pl.ds(start, inv_block), :] = high
            inv_low[pl.ds(start, inv_block), :] = low
        inverse = inv_high[...], inv_low[...]
        parts = [halves(product(halves(kids[mask][kid, :kid_block]), inverse)) for mask in range(pieces)]
        group = pieces if kid_block % 128 == 0 else 1
        for first in range(0, pieces, group):
            masks = range(first, first + group)
            high = jnp.concatenate([parts[mask][0] for mask in masks], axis=0)
            low = jnp.concatenate([parts[mask][1] for mask in masks], axis=0)
            pick = jnp.concatenate([pick_high[kid, mask] for mask in masks], axis=1)
            places = jnp.concatenate([index[kid, mask : mask + 1, :] for mask in masks], axis=1)
            lifted_part = dot(pick, high)
            low_part = dot(picks(places, size + block * own_border, own_border), low)
            lifted[...] = lifted_part if first == 0 else lifted[...] + lifted_part
            reduced[kid] = low_part if first == 0 else reduced[kid] + low_part
            for start in range(0, border_size, 384):
                part = dot(picks(places, size + start, 384), high)
                lower[start : start + 384] = part if first == 0 else lower[start : start + 384] + part
        own = lifted[pl.ds(pl.multiple_of(block * own_rows, 16), own_rows), :]
        kid_sum[kid : kid + 1] = column_sum(own_inverse * own_inverse) + column_sum(own * own)
        lift_high[kid] = rounded(lifted[...])
        lower_high[kid] = rounded(lower[...])
        own_lower = lower[pl.ds(pl.multiple_of(block * own_border, 8), own_border), :]
        reduced[kid] = own_lower + reduced[kid] - dot(factor_high, lift_high[kid])


def border_kernel(border, lower_high, border_high, border_lower):
    border_high[...] = rounded(border[...])
    for kid in range(2):
        for span in spans(lower_high.shape[2]):
            border_lower[kid, :, span] = dot(border_high[...], lower_high[kid, :, span])


def image_kernel(pieces, *refs):
    factor = unpacked(pieces, refs)
    border_high, border_lower, weights, reduced, lift_high, diag_high, diag_low, parent_sum, kid_sum, out = refs[
        2 * pieces - 2 : 2 * pieces + 8
    ]
    factor_high, fold_high, fold_low = refs[2 * pieces + 8 :]
    _, block = place_of()
    own_border, size = refs[0].shape
    kid_size = reduced.shape[2]
    for mask, pair in enumerate(factor):
        start = pl.multiple_of((block ^ mask) * own_border, 16)

        def put(ref, start=start):
            factor_high[pl.ds(start, own_border), :] = rounded(ref[...])

        if mask < 2:
            put(pair[0])
        else:
            store(pair, put)
    for span in spans(size):
        fold_high[:, span], fold_low[:, span] = halves(dot(border_high[...], factor_high[:, span]))
    fold = fold_high[...], fold_low[...]
    for span in spans(size):
        image = product(fold, (diag_high[:, span], diag_low[:, span]))
        out[:, span] = parent_sum[:, span] + column_sum(weights[:, span] * image)
    for kid in range(2):
        for span in spans(kid_size):
            image = border_lower[kid, :, span] - dot(fold[0], lift_high[kid, :, span])
            target = size + kid * kid_size + span.start
            out[:, target : target + COLS] = kid_sum[kid : kid + 1, span] + column_sum(reduced[kid, :, span] * image)


def finish_kernel(parent_ref, *refs):
    partials, (parent_out, kid_out) = refs[:-2], refs[-2:]
    leaf = lax.axis_index("leaf")
    size, kid_size = parent_out.shape[1], kid_out.shape[1]
    half = len(partials) // 2
    sums = [functools.reduce(jnp.add, [ref[...] for ref in group]) for group in (partials[:half], partials[half:])]
    owner, _ = place_of()
    parent_out[...] = jnp.where(owner == leaf, sums[0][:, :size], sums[1][:, :size])
    for parent, total in ((owner, sums[0]), (owner ^ 1, sums[1])):
        _, ids = kids_of(parent_ref, parent)
        for place in range(2):
            for kid in range(2):

                @pl.when(ids[place] == 2 * leaf + kid)
                def _(total=total, place=place, kid=kid):
                    start = size + place * kid_size
                    kid_out[kid : kid + 1] = total[:, start : start + kid_size]


def call(kernel, out_shape, limit, scalars=0, loose=0, keep=True, scratch=(), moved=1_000):
    def run(*args):
        specs = [pl.BlockSpec(memory_space=pltpu.SMEM if at < scalars else pltpu.VMEM) for at in range(len(args))]
        args = [
            pltpu.with_memory_space_constraint(value, pltpu.HBM if at < loose else pltpu.VMEM)
            for at, value in enumerate(args)
        ]
        results = out_shape
        if keep:
            results = jax.tree.map(lambda leaf: pltpu.VMEM(leaf.shape, leaf.dtype), results)
        return pl.pallas_call(
            kernel,
            out_shape=results,
            in_specs=specs,
            out_specs=jax.tree.map(lambda _: pl.BlockSpec(memory_space=pltpu.VMEM), out_shape),
            scratch_shapes=scratch,
            compiler_params=pltpu.CompilerParams(vmem_limit_bytes=limit * MIB),
            cost_estimate=pl.CostEstimate(flops=0, bytes_accessed=moved, transcendentals=0),
        )(*args)

    return run


def shards(border, factor, diagonal, kid_rows, kid_inverse, child_index, child_parent):
    border, factor, diagonal = border[0], factor[0], diagonal[0]
    pieces = lax.axis_size("front")
    size, kid_size, border_size = diagonal.shape[1], kid_rows.shape[2], border.shape[1]
    own_border = border.shape[0]
    kid_block = kid_rows.shape[1]
    half = jnp.bfloat16

    def over_fronts(value, parity=None):
        parts = {0: value}
        bit = 2
        while bit < pieces:
            for mask in list(parts):
                parts[mask | bit] = exchange(parts[mask], 0, bit, parity)
            bit *= 2
        return parts

    def spread(parts, gate_own, gate_rest):
        others = {mask | 1: exchange(after(part, *(gate_rest if mask else gate_own)), 1, 0) for mask, part in parts.items()}
        parts = parts | others
        return [parts[mask] for mask in range(pieces)]

    def gathered(own, keep, swap, gate_own, gate_keep, gate_swap):
        result = [own, exchange(after(own, *gate_own), 1, 0)]
        for mask in list(keep)[1:]:
            far_swap = exchange(after(keep[mask], *gate_keep), 1, 0, 0)
            far_keep = exchange(after(swap[mask], *gate_swap), 1, 0, 1)
            result += [keep[mask], swap[mask], far_keep, far_swap]
        return result

    last = pieces - 2
    keep_diagonal = over_fronts(diagonal, 0)
    keep_factor = over_fronts(factor, 0)
    own_diagonal = cross(diagonal)
    kid_shape = (2, kid_block + kid_inverse.shape[1], kid_size)
    own_kids, index = call(
        select_kernel, (shape_of(kid_shape), shape_of((2, pieces, kid_block), jnp.int32)), 6, scalars=1, loose=4
    )(child_parent, child_index, kid_rows, kid_inverse, exchange(kid_rows, 1, 0), exchange(kid_inverse, 1, 0))
    own_kids = cross(after(own_kids, own_diagonal, keep_diagonal[last], keep_factor[last]))
    swap_diagonal = over_fronts(own_diagonal, 1)
    kid_parts = over_fronts(after(own_kids, swap_diagonal[last]))
    own_factor = cross(after(factor, own_kids))
    diagonal_parts = gathered(own_diagonal, keep_diagonal, swap_diagonal, [own_kids], [own_kids], [own_kids])

    diag_high, diag_low, pick_high, weights, parent_sum = call(
        functools.partial(diagonal_kernel, pieces),
        (
            shape_of((size, size), half),
            shape_of((size, size), half),
            shape_of((2, pieces, size, kid_block), half),
            shape_of((own_border, size)),
            shape_of((1, size)),
        ),
        10,
    )(index, own_factor, *diagonal_parts)
    own_border_rows = cross(after(border, own_kids))
    kids_here = kid_parts[last]
    swap_factor = over_fronts(after(own_factor, kids_here), 1)
    kid_parts = spread(kid_parts, [own_kids], [pick_high])

    reduced, lift_high, lower_high, kid_sum = call(
        functools.partial(kid_kernel, pieces),
        (
            shape_of((2, own_border, kid_size)),
            shape_of((2, size, kid_size), half),
            shape_of((2, border_size, kid_size), half),
            shape_of((2, kid_size)),
        ),
        20,
        scratch=[
            pltpu.VMEM((kid_size, kid_size), half),
            pltpu.VMEM((kid_size, kid_size), half),
            pltpu.VMEM((size, kid_size), jnp.float32),
            pltpu.VMEM((border_size, kid_size), jnp.float32),
        ],
    )(index, pick_high, own_factor, *kid_parts)

    border_high, border_lower = call(
        border_kernel, (shape_of(border.shape, half), shape_of((2, own_border, kid_size))), 8
    )(own_border_rows, lower_high)

    factor_parts = gathered(own_factor, keep_factor, swap_factor, [kids_here], [kids_here], [lift_high, own_border_rows])
    total = call(
        functools.partial(image_kernel, pieces),
        shape_of((1, size + 2 * kid_size)),
        12,
        scratch=[
            pltpu.VMEM((border_size, size), half),
            pltpu.VMEM((own_border, size), half),
            pltpu.VMEM((own_border, size), half),
        ],
    )(
        *factor_parts,
        border_high,
        border_lower,
        weights,
        reduced,
        lift_high,
        diag_high,
        diag_low,
        parent_sum,
        kid_sum,
    )

    total = total + exchange(total, 1, 0)
    bit = 4
    while bit < pieces:
        total = total + exchange(total, 0, bit)
        bit *= 2
    near = range(min(pieces, 4))
    order = [mask for parity in (0, 1) for mask in near if mask % 2 == parity]
    partials = [exchange(total, 0, mask) if mask else total for mask in order]
    return call(finish_kernel, (shape_of((1, size)), shape_of((2, kid_size))), 2, scalars=1, loose=1, keep=False)(
        child_parent, *partials
    )


def solution(mesh):
    whole = P("leaf", "front", None)
    return jax.shard_map(
        shards,
        mesh=mesh,
        in_specs=(whole,) * 5 + (P(), P()),
        out_specs=(P("leaf", None), P("leaf", None)),
        check_vma=False,
    )
```
